128 devices in a mesh: tiles: 128 (over y, x, z, core).
Axes of the slice: x: 4, y: 4, z: 4, core: 2. Of those that a mesh axis runs over, the one named last changes fastest.
Arguments:
- tiles_in: float32 [1024, 250, 256], P('tiles'), may hold values from -6 to 6
- conv_weight: float32 [250, 49], replicated, may hold values from -0.875 to 0.875
- conv_bias: float32 [250], replicated, may hold values from -4 to 4
- norm_gain: float32 [250], replicated, may hold values from 0.5 to 1.5
- norm_bias: float32 [250], replicated, may hold values from -3 to 3
- weight_in: float32 [250, 1000], replicated, may hold values from -0.375 to 0.375
- bias_in: float32 [1000], replicated, may hold values from -3 to 3
- weight_out: float32 [1000, 250], replicated, may hold values from -0.1875 to 0.1875
- bias_out: float32 [250], replicated, may hold values from -3 to 3
- grad_out: float32 [1024, 250, 256], P('tiles'), may hold values from -6 to 6
- tile_counts: int32 [128], P('tiles'), may hold values from 4 to 8, as said below
- ocean_mask: int32 [1024, 256], P('tiles'), may hold values 0 or 1
- neighbours: int32 [1024, 8], P('tiles'), may hold values from -1 to 1023, as said below
- sample_ids: int32 [1024], P('tiles'), may hold values from 0 to 4, as said below
Outputs:
- output: float32 [1024, 250, 256], P('tiles')
- grad_tiles_in: float32 [1024, 250, 256], P('tiles')
- grad_conv_weight: float32 [250, 49], replicated
- grad_conv_bias: float32 [250], replicated
- grad_norm_gain: float32 [250], replicated
- grad_norm_bias: float32 [250], replicated
- grad_weight_in: float32 [250, 1000], replicated
- grad_bias_in: float32 [1000], replicated
- grad_weight_out: float32 [1000, 250], replicated
- grad_bias_out: float32 [250], replicated
The draws below stay inside these ranges and needn't reach their ends.
Inputs may be any that keep to these rules, and one draw needn't show every extreme that they name: `tile_counts`: one device holds 8 filled slots and another (4); filled slots come first on each device. `neighbours`: each entry is -1 or a filled slot on a device whose index differs from the tile's device by at most 2; slots that are not filled have only -1. `sample_ids`: never falling along the slots; each sample holds more than 8 slots.
All inputs are finite; a program needn't handle non-finite values. No bound on the sum of `ocean_mask` on one device may be relied on, other than what follows from the above.
Results may differ from the reference program's by a relative error of at most 0.0003.
Values sent between devices are 32-bit elements; how exact they have to be, the bound alone decides.
A program may use at most 384 MiB of HBM per device.

```python
import jax
import jax.numpy as jnp
from jax import lax

CHANNELS = 250
HIDDEN_SIZE = 1000
SIDE = 16
KSIZE = 7
REACH = 2
SAMPLES = 5
CAP = 8
SLOTS = 1024


def counts_helper(key):
    device_total = SLOTS // CAP
    first_key, third_key = jax.random.split(jax.random.fold_in(key, 101), 2)
    counts = jax.random.randint(first_key, (device_total,), (CAP + 1) // 2, CAP + 1)
    low_device = jax.random.randint(third_key, (), 0, device_total - 1)
    counts = counts.at[device_total - 1].set(CAP)
    counts = counts.at[low_device].set((CAP + 1) // 2)
    return counts.astype(jnp.int32)


def draw_tile_counts(key, part):
    return counts_helper(key)


def draw_neighbours(key, part):
    counts = counts_helper(key)
    key = jax.random.fold_in(key, 2)
    device_total = SLOTS // CAP
    first_key, second_key, third_key = jax.random.split(key, 3)
    slot_ids = jnp.arange(SLOTS, dtype=jnp.int32)
    home_device = slot_ids // CAP
    local_ids = slot_ids % CAP
    filled = local_ids < counts[home_device]
    step_dev = jax.random.randint(first_key, (SLOTS, 8), -REACH, REACH + 1)
    target = jnp.clip(home_device[:, None] + step_dev, 0, device_total - 1)
    chosen = jax.random.randint(second_key, (SLOTS, 8), 0, 1 << 20) % counts[target]
    coastal = jax.random.randint(third_key, (SLOTS, 8), 0, 5) == 0
    link_ids = target * CAP + chosen
    links = jnp.where(filled[:, None] & jnp.logical_not(coastal), link_ids, -1).astype(jnp.int32)
    return links.at[SLOTS - CAP, 4].set(SLOTS - 1).astype(jnp.int32)


def draw_sample_ids(key, part):
    key = jax.random.fold_in(key, 3)
    bounds = jnp.arange(1, SAMPLES, dtype=jnp.int32) * SLOTS // SAMPLES + jax.random.randint(key, (SAMPLES - 1,), -CAP, CAP + 1)
    slot_ids = jnp.arange(SLOTS, dtype=jnp.int32)
    return jnp.sum((slot_ids[:, None] >= bounds[None, :]).astype(jnp.int32), axis=1).astype(jnp.int32)


def set_ends(values, rng, low, high):
    shape = values.shape
    place = [jax.random.randint(jax.random.fold_in(rng, axis), (), 0, shape[axis]) for axis in range(len(shape))]
    values = values.at[tuple(place)].set(low)
    longest = shape.index(max(shape))
    place[longest] = (place[longest] + 1) % shape[longest]
    return values.at[tuple(place)].set(high)


def block_scale(stream_key, extent, cuts, least, top_value):
    factor_of, own = 1.0, jax.random.fold_in(stream_key, 6)
    for position, parts in cuts:
        heights = jnp.exp(jax.random.uniform(jax.random.fold_in(own, position), (parts,), jnp.float32, least / len(cuts), top_value / len(cuts)))
        factor_of = factor_of * jnp.repeat(heights, extent[position] // parts).reshape([-1 if axis == position else 1 for axis in range(len(extent))])
    return factor_of


def scatter_about(rng, dims, width, bound, shards=(), kind=jnp.bfloat16):
    drawn = width * jax.random.normal(rng, dims, jnp.float32)
    if shards:
        drawn = drawn * block_scale(rng, dims, shards, -0.22, 0.18)
    return jnp.clip(drawn, -bound, bound).astype(kind)


def setup_inputs(seed: int = 0) -> dict:
    splits = jax.random.split(jax.random.key(seed), 15)
    tiles_in = scatter_about(splits[0], (SLOTS, CHANNELS, SIDE * SIDE), 1.0, 6.0, ((0, 128),), jnp.float32)
    conv_weight = scatter_about(splits[1], (CHANNELS, KSIZE * KSIZE), (KSIZE * KSIZE) ** -0.5, 0.875, (), jnp.float32)
    conv_bias = scatter_about(splits[2], (CHANNELS,), 1.0, 4.0, (), jnp.float32)
    norm_gain = jnp.clip(1.0 + 0.1 * jax.random.normal(splits[3], (CHANNELS,), jnp.float32), 0.5, 1.5)
    norm_bias = scatter_about(splits[4], (CHANNELS,), 0.5, 3.0, (), jnp.float32)
    weight_in = scatter_about(splits[5], (CHANNELS, HIDDEN_SIZE), CHANNELS ** -0.5, 0.375, (), jnp.float32)
    bias_in = scatter_about(splits[6], (HIDDEN_SIZE,), 0.5, 3.0, (), jnp.float32)
    weight_out = scatter_about(splits[7], (HIDDEN_SIZE, CHANNELS), HIDDEN_SIZE ** -0.5, 0.1875, (), jnp.float32)
    bias_out = scatter_about(splits[8], (CHANNELS,), 0.5, 3.0, (), jnp.float32)
    grad_out = scatter_about(splits[9], (SLOTS, CHANNELS, SIDE * SIDE), 1.0, 6.0, ((0, 128),), jnp.float32)
    tile_counts = draw_tile_counts(jax.random.fold_in(splits[14], 71), 0)
    ocean_mask = set_ends((jax.random.randint(splits[11], (SLOTS, SIDE * SIDE), 0, 4) < 3).astype(jnp.int32), jax.random.fold_in(splits[11], 1), 0, 1)
    neighbours = draw_neighbours(jax.random.fold_in(splits[14], 71), 0)
    sample_ids = draw_sample_ids(jax.random.fold_in(splits[14], 71), 0)
    return {"tiles_in": tiles_in, "conv_weight": conv_weight, "conv_bias": conv_bias, "norm_gain": norm_gain, "norm_bias": norm_bias, "weight_in": weight_in, "bias_in": bias_in, "weight_out": weight_out, "bias_out": bias_out, "grad_out": grad_out, "tile_counts": tile_counts, "ocean_mask": ocean_mask, "neighbours": neighbours, "sample_ids": sample_ids}


NORM_EPSILON = 1e-05
HIGHEST_PRECISION = lax.Precision.HIGHEST

@jax.custom_vjp
def low(v):
    return lax.optimization_barrier(v.astype(jnp.bfloat16)).astype(jnp.float32)

@jax.custom_vjp
def low_back(v):
    return v

def low_keep(v):
    return (low(v), None)

def low_pass(kept, grad):
    return (grad,)

def back_keep(v):
    return (v, None)

def back_low(kept, grad):
    return (low(grad),)
low.defvjp(low_keep, low_pass)
low_back.defvjp(back_keep, back_low)

def assemble(own_tiles, near_tiles):
    tile_total = own_tiles.shape[0]
    channels = own_tiles.shape[1]
    rim_width = KSIZE // 2

    def as_square(values):
        return values.reshape(tile_total, channels, SIDE, SIDE)
    sides = [as_square(near_tiles[:, direction]) for direction in range(8)]
    upper_rows = jnp.concatenate([sides[0][:, :, SIDE - rim_width:, SIDE - rim_width:], sides[1][:, :, SIDE - rim_width:, :], sides[2][:, :, SIDE - rim_width:, :rim_width]], axis=3)
    middle_rows = jnp.concatenate([sides[3][:, :, :, SIDE - rim_width:], as_square(own_tiles), sides[4][:, :, :, :rim_width]], axis=3)
    lower_rows = jnp.concatenate([sides[5][:, :, :rim_width, SIDE - rim_width:], sides[6][:, :, :rim_width, :], sides[7][:, :, :rim_width, :rim_width]], axis=3)
    return jnp.concatenate([upper_rows, middle_rows, lower_rows], axis=2)

def depthwise(own_tiles, near_tiles, conv_weight, conv_bias):
    tile_total = own_tiles.shape[0]
    channels = own_tiles.shape[1]
    padded_side = SIDE + 2 * (KSIZE // 2)
    flat_tiles = assemble(own_tiles, near_tiles).reshape(tile_total, channels, padded_side * padded_side)
    flat_tiles = jnp.pad(flat_tiles, ((0, 0), (0, 0), (0, KSIZE - 1)))
    out_span = SIDE * padded_side
    running = jnp.zeros((tile_total, channels, out_span), jnp.float32)
    for row_step in range(KSIZE):
        for col_step in range(KSIZE):
            anchor = row_step * padded_side + col_step
            running = running + conv_weight[:, row_step * KSIZE + col_step][None, :, None] * flat_tiles[:, :, anchor:anchor + out_span]
    result = running.reshape(tile_total, channels, SIDE, padded_side)[:, :, :, :SIDE]
    return result.reshape(tile_total, channels, SIDE * SIDE) + conv_bias[None, :, None]

def dense_branch(oceanic, normed, tiles_in, norm_gain, norm_bias, weight_in, bias_in, weight_out, bias_out):
    scaled = normed * norm_gain[None, :, None] + norm_bias[None, :, None]
    hidden_pre = jnp.einsum('ch,tcp->thp', weight_in, scaled, precision=HIGHEST_PRECISION) + bias_in[None, :, None]
    hidden = jax.nn.gelu(hidden_pre, approximate=False)
    update = jnp.einsum('hc,thp->tcp', weight_out, hidden, precision=HIGHEST_PRECISION) + bias_out[None, :, None]
    return oceanic[:, None, :] * (tiles_in + update)

def reference(tiles_in, conv_weight, conv_bias, norm_gain, norm_bias, weight_in, bias_in, weight_out, bias_out, grad_out, tile_counts, ocean_mask, neighbours, sample_ids):
    slot_total = tiles_in.shape[0]
    channels = tiles_in.shape[1]
    block_total = slot_total // CAP
    slot_ids = jnp.arange(slot_total, dtype=jnp.int32)
    filled = (slot_ids % CAP < tile_counts[slot_ids // CAP]).astype(jnp.float32)
    oceanic = ocean_mask.astype(jnp.float32) * filled[:, None]
    member = (sample_ids[:, None] == jnp.arange(SAMPLES, dtype=jnp.int32)[None, :]).astype(jnp.float32)
    active = jnp.sum(oceanic)

    def forward(tiles_all, conv_weight, conv_bias, norm_gain, norm_bias, weight_in, bias_in, weight_out, bias_out):

        def conv_block(block_index):
            anchor = block_index * CAP
            own_tiles = lax.dynamic_slice_in_dim(tiles_all, anchor, CAP, 0)
            link_ids = lax.dynamic_slice_in_dim(neighbours, anchor, CAP, 0)
            is_valid = (link_ids >= 0).astype(jnp.float32)
            near_tiles = tiles_all[jnp.clip(link_ids, 0, slot_total - 1)] * is_valid[:, :, None, None]
            return depthwise(own_tiles, near_tiles, conv_weight, conv_bias)
        conv_out = lax.map(jax.checkpoint(conv_block), jnp.arange(block_total, dtype=jnp.int32)).reshape(tiles_all.shape)
        tile_sum = lax.optimization_barrier(jnp.sum(conv_out * oceanic[:, None, :], axis=(1, 2)))
        sample_cells = jnp.dot(lax.optimization_barrier(jnp.sum(oceanic, axis=1)), member, precision=HIGHEST_PRECISION)
        entries = channels * sample_cells
        sample_mean = jnp.dot(tile_sum, member, precision=HIGHEST_PRECISION) / entries
        centred = conv_out - jnp.dot(member, sample_mean, precision=HIGHEST_PRECISION)[:, None, None]
        tile_square = lax.optimization_barrier(jnp.sum(centred * centred * oceanic[:, None, :], axis=(1, 2)))
        variance = jnp.dot(tile_square, member, precision=HIGHEST_PRECISION) / entries
        inv_std = lax.rsqrt(variance + NORM_EPSILON)
        normed = centred * jnp.dot(member, inv_std, precision=HIGHEST_PRECISION)[:, None, None]
        cells_last = tiles_all.shape[2]

        def dense_block(items):
            return dense_branch(items[0], items[1], items[2], norm_gain, norm_bias, weight_in, bias_in, weight_out, bias_out)
        blocked = (oceanic.reshape(block_total, CAP, cells_last), normed.reshape(block_total, CAP, channels, cells_last), tiles_all.reshape(block_total, CAP, channels, cells_last))
        return lax.map(jax.checkpoint(dense_block), blocked).reshape(tiles_all.shape)
    output, pullback = jax.vjp(forward, tiles_in, conv_weight, conv_bias, norm_gain, norm_bias, weight_in, bias_in, weight_out, bias_out)
    grads = pullback(grad_out)
    scaled_grads = tuple((grad_part / active for grad_part in grads[1:]))
    return (output, grads[0]) + scaled_grads
```

```python
import functools

import jax
import jax.numpy as jnp
from jax import lax
from jax.experimental import pallas as pl
from jax.experimental.pallas import tpu as pltpu
from jax.sharding import PartitionSpec as P

SIDE = 16
KSIZE = 7
RIM = 3
REACH = 2
SAMPLES = 5
CAP = 8
CELLS = SIDE * SIDE
PAD = SIDE + 2 * RIM
LANES = 128
GROUPS = 2
ROWS = CELLS * CAP
RIM_CELLS = 156
RIM_ROWS = RIM_CELLS * CAP
HIDDEN_PAD = 1024
NORM_EPSILON = 1e-05
F32 = jnp.float32
BF16 = jnp.bfloat16
MIB = 1 << 20
MESH = pl.DeviceIdType.MESH
VMEM_SPEC = pl.BlockSpec(memory_space=pltpu.VMEM)
SMEM_SPEC = pl.BlockSpec(memory_space=pltpu.SMEM)
ANY_SPEC = pl.BlockSpec(memory_space=pl.ANY)


def params(mib=56, **more):
    return pltpu.CompilerParams(vmem_limit_bytes=mib * MIB, **more)


def rim_index(r, c):
    if r < RIM:
        return r * SIDE + c
    if r >= SIDE - RIM:
        return 48 + (r - (SIDE - RIM)) * SIDE + c
    if c < RIM:
        return 96 + (r - RIM) * RIM + c
    return 126 + (r - RIM) * RIM + c - (SIDE - RIM)


def region_runs():
    spans = {-1: (0, SIDE - RIM, RIM), 0: (RIM, 0, SIDE), 1: (RIM + SIDE, 0, RIM)}
    order = [(-1, -1), (-1, 0), (-1, 1), (0, -1), (0, 1), (1, -1), (1, 0), (1, 1)]
    runs = []
    for dr, dc in order:
        dst_r, src_r, rows = spans[dr]
        dst_c, src_c, cols = spans[dc]
        found = []

        def add(cells):
            start = 0
            while start < len(cells):
                stop = start + 1
                while (
                    stop < len(cells)
                    and stop - start < 8
                    and cells[stop][0] - cells[stop - 1][0] == cells[1][0] - cells[0][0]
                    and cells[stop][1] - cells[stop - 1][1] == cells[1][1] - cells[0][1]
                ):
                    stop += 1
                step = (cells[1][0] - cells[0][0], cells[1][1] - cells[0][1])
                found.append((cells[start][0], step[0], cells[start][1], step[1], stop - start))
                start = stop

        if dr == 0:
            for j in range(cols):
                cells = [
                    ((dst_r + i) * PAD + dst_c + j, rim_index(src_r + i, src_c + j))
                    for i in range(rows)
                ]
                add(cells[:RIM])
                add(cells[RIM : SIDE - RIM])
                add(cells[SIDE - RIM :])
        else:
            for i in range(rows):
                add(
                    [
                        ((dst_r + i) * PAD + dst_c + j, rim_index(src_r + i, src_c + j))
                        for j in range(cols)
                    ]
                )
        runs.append(found)
    return runs


RUNS = region_runs()


def to_rows_kernel(x_ref, o_ref):
    t = pl.program_id(0)
    for g in range(GROUPS):
        v = x_ref[0, g * LANES : (g + 1) * LANES, :]
        if g == 1:
            channel = lax.broadcasted_iota(jnp.int32, v.shape, 0)
            v = jnp.where(channel < 250 - LANES, v, 0.0)
        o_ref[g, pl.ds(t, CELLS, stride=CAP), :] = v.T


def to_rows_rim_kernel(x_ref, o_ref, rim_ref):
    to_rows_kernel(x_ref, o_ref)

    @pl.when(pl.program_id(0) == CAP - 1)
    def _():
        for g in range(GROUPS):
            for first, rim, cells in [(0, 0, 48), (13 * SIDE, 48, 48)]:
                rim_ref[g, pl.ds(rim * CAP, cells * CAP), :] = o_ref[
                    g, pl.ds(first * CAP, cells * CAP), :
                ]
            for r in range(RIM, SIDE - RIM):
                for c in (0, SIDE - RIM):
                    rim_ref[g, pl.ds(rim_index(r, c) * CAP, RIM * CAP), :] = o_ref[
                        g, pl.ds((r * SIDE + c) * CAP, RIM * CAP), :
                    ]


def to_rows(x, with_rim):
    block = pl.BlockSpec((GROUPS, ROWS, LANES), lambda t: (0, 0, 0))
    rows = jax.ShapeDtypeStruct((GROUPS, ROWS, LANES), F32)
    rim_block = pl.BlockSpec((GROUPS, RIM_ROWS, LANES), lambda t: (0, 0, 0))
    rim = jax.ShapeDtypeStruct((GROUPS, RIM_ROWS, LANES), F32)
    return pl.pallas_call(
        to_rows_rim_kernel if with_rim else to_rows_kernel,
        grid=(CAP,),
        in_specs=[pl.BlockSpec((1, 2 * LANES, CELLS), lambda t: (t, 0, 0))],
        out_specs=(block, rim_block) if with_rim else block,
        out_shape=(rows, rim) if with_rim else rows,
        compiler_params=params(),
        cost_estimate=pl.CostEstimate(flops=0, bytes_accessed=5 * MIB, transcendentals=0),
        name="to_rows",
    )(x)


def from_rows_kernel(x_ref, o_ref):
    t = pl.program_id(0)
    for g in range(GROUPS):
        o_ref[0, g * LANES : (g + 1) * LANES, :] = x_ref[g, pl.ds(t, CELLS, stride=CAP), :].T


def from_rows(x):
    return pl.pallas_call(
        from_rows_kernel,
        grid=(CAP,),
        in_specs=[pl.BlockSpec((GROUPS, ROWS, LANES), lambda t: (0, 0, 0))],
        out_specs=pl.BlockSpec((1, 2 * LANES, CELLS), lambda t: (t, 0, 0)),
        out_shape=jax.ShapeDtypeStruct((CAP, 250, CELLS), F32),
        compiler_params=params(),
        cost_estimate=pl.CostEstimate(flops=0, bytes_accessed=5 * MIB, transcendentals=0),
        name="from_rows",
    )(x)


def lane_mask(g):
    lane = lax.broadcasted_iota(jnp.int32, (CAP, LANES), 1)
    return (lane < 250 - g * LANES).astype(F32)


def conv_kernel(
    near_ref, own_ref, rim_ref, r0, r1, r2, r3, w_ref, b_ref, mask_ref, member_ref,
    padded_ref, conv_ref, stat_ref, pool, sems,
):
    sources = [r0, r1, rim_ref, r2, r3]
    copies = [
        pltpu.make_async_copy(
            src, pool.at[:, pl.ds(i * RIM_ROWS, RIM_ROWS), :], sems.at[i]
        )
        for i, src in enumerate(sources)
    ]
    for copy in copies:
        copy.start()
    for g in range(GROUPS):
        pool[g, pl.ds(5 * RIM_ROWS, RIM_ROWS), :] = jnp.zeros((RIM_ROWS, LANES), F32)
        for r in range(SIDE):
            padded_ref[g, pl.ds(((r + RIM) * PAD + RIM) * CAP, SIDE * CAP), :] = own_ref[
                g, pl.ds(r * SIDE * CAP, SIDE * CAP), :
            ]
    for copy in copies:
        copy.wait()

    def fill(t, carry):
        for k in range(8):
            q = near_ref[t, k]
            for dst, dst_step, src, src_step, length in RUNS[k]:
                for g in range(GROUPS):
                    padded_ref[
                        g, pl.ds(dst * CAP + t, length, stride=dst_step * CAP), :
                    ] = pool[g, pl.ds(q + src * CAP, length, stride=src_step * CAP), :]
        return carry

    lax.fori_loop(0, CAP, fill, 0)

    sums = jnp.zeros((CAP, LANES), F32)
    cells = jnp.zeros((CAP, LANES), F32)
    for g in range(GROUPS):

        def row(r, carry):
            total, count = carry
            acc = jnp.broadcast_to(b_ref[g][None], (SIDE, CAP, LANES))
            for a in range(KSIZE):
                x = padded_ref[g, pl.ds((r + a) * PAD * CAP, PAD * CAP), :].reshape(
                    PAD, CAP, LANES
                )
                for b in range(KSIZE):
                    acc = acc + w_ref[g, a * KSIZE + b][None] * x[b : b + SIDE]
            conv_ref[g, pl.ds(r * SIDE * CAP, SIDE * CAP), :] = acc.reshape(SIDE * CAP, LANES)
            m = mask_ref[pl.ds(r * SIDE, SIDE)]
            return total + jnp.sum(acc * m, axis=0), count + jnp.sum(m, axis=0)

        total, count = lax.fori_loop(
            0, SIDE, row, (jnp.zeros((CAP, LANES), F32), jnp.zeros((CAP, LANES), F32))
        )
        sums = sums + total
        cells = count
    entries = 250.0 * cells
    total = jnp.broadcast_to(jnp.sum(sums, axis=1, keepdims=True), (CAP, LANES))
    mean = total / jnp.maximum(entries, 1.0)

    squares = jnp.zeros((CAP, LANES), F32)
    for g in range(GROUPS):

        def square(r, acc):
            x = conv_ref[g, pl.ds(r * SIDE * CAP, SIDE * CAP), :].reshape(SIDE, CAP, LANES)
            diff = x - mean[None]
            return acc + jnp.sum(diff * diff * mask_ref[pl.ds(r * SIDE, SIDE)], axis=0)

        part = lax.fori_loop(0, SIDE, square, jnp.zeros((CAP, LANES), F32))
        squares = squares + part * lane_mask(g)
    spread = jnp.broadcast_to(jnp.sum(squares, axis=1, keepdims=True), (CAP, LANES))

    member = member_ref[...]
    n_tile = member * entries
    n = jnp.sum(n_tile, axis=0, keepdims=True)
    centre = jnp.sum(n_tile * mean, axis=0, keepdims=True) / jnp.maximum(n, 1.0)
    off = mean - centre
    m2 = jnp.sum(member * spread + n_tile * off * off, axis=0, keepdims=True)
    row_id = lax.broadcasted_iota(jnp.int32, (CAP, LANES), 0)
    stat_ref[...] = jnp.where(
        row_id == 0, n, jnp.where(row_id == 1, centre, jnp.where(row_id == 2, m2, 0.0))
    )


def conv_forward(near, own, rim, received, w, b, mask, member):
    return pl.pallas_call(
        conv_kernel,
        in_specs=[SMEM_SPEC, VMEM_SPEC] + [ANY_SPEC] * 5 + [VMEM_SPEC] * 4,
        out_specs=(VMEM_SPEC,) * 3,
        out_shape=(
            jax.ShapeDtypeStruct((GROUPS, PAD * PAD * CAP, LANES), F32),
            jax.ShapeDtypeStruct((GROUPS, ROWS, LANES), F32),
            jax.ShapeDtypeStruct((CAP, LANES), F32),
        ),
        scratch_shapes=[
            pltpu.VMEM((GROUPS, 6 * RIM_ROWS, LANES), F32),
            pltpu.SemaphoreType.DMA((5,)),
        ],
        compiler_params=params(),
        name="conv_forward",
    )(near, own, rim, *received, w, b, mask, member)


def exchange(x, send, recv, slots, first, mine, count, peer_of):
    copies = []
    for j in range(1, count):
        copies.append(
            pltpu.make_async_remote_copy(
                src_ref=x,
                dst_ref=slots.at[mine],
                send_sem=send.at[first + j],
                recv_sem=recv.at[first + j],
                device_id=(peer_of(j),),
                device_id_type=MESH,
            )
        )
    for copy in copies:
        copy.start()
    slots[mine] = x[...]
    for copy in copies:
        copy.wait()


INNER = 8
OUTER = 16


def merge_stats(parts):
    n = jnp.sum(parts[:, 0:1], axis=0)
    mean = jnp.sum(parts[:, 0:1] * parts[:, 1:2], axis=0) / jnp.maximum(n, 1.0)
    off = parts[:, 1:2] - mean[None]
    m2 = jnp.sum(parts[:, 2:3] + parts[:, 0:1] * off * off, axis=0)
    row_id = lax.broadcasted_iota(jnp.int32, (CAP, LANES), 0)
    return jnp.where(row_id == 0, n, jnp.where(row_id == 1, mean, jnp.where(row_id == 2, m2, 0.0)))


def merge_sums(parts):
    return jnp.sum(parts, axis=0)


def reduce_kernel(merge, x_ref, o_ref, inner, outer, partial, send, recv):
    me = lax.axis_index("tiles")
    group, place = me // INNER, me % INNER

    def inner_peer(j):
        return group * INNER + (place + j) % INNER

    def outer_peer(j):
        return ((group + j) % OUTER) * INNER + place

    barrier = pltpu.get_barrier_semaphore()
    for j in range(1, INNER):
        pl.semaphore_signal(barrier, inc=1, device_id=(inner_peer(j),), device_id_type=MESH)
    for j in range(1, OUTER):
        pl.semaphore_signal(barrier, inc=1, device_id=(outer_peer(j),), device_id_type=MESH)
    pl.semaphore_wait(barrier, INNER + OUTER - 2)
    exchange(x_ref, send, recv, inner, 0, place, INNER, inner_peer)
    partial[...] = merge(inner[...])
    exchange(partial, send, recv, outer, INNER, group, OUTER, outer_peer)
    o_ref[...] = merge(outer[...])


def reduce_small(x, merge, collective_id, name):
    return pl.pallas_call(
        functools.partial(reduce_kernel, merge),
        in_specs=[VMEM_SPEC],
        out_specs=VMEM_SPEC,
        out_shape=jax.ShapeDtypeStruct((CAP, LANES), F32),
        scratch_shapes=[
            pltpu.VMEM((INNER, CAP, LANES), F32),
            pltpu.VMEM((OUTER, CAP, LANES), F32),
            pltpu.VMEM((CAP, LANES), F32),
            pltpu.SemaphoreType.DMA((INNER + OUTER,)),
            pltpu.SemaphoreType.DMA((INNER + OUTER,)),
        ],
        compiler_params=pltpu.CompilerParams(collective_id=collective_id, has_side_effects=True),
        name=name,
    )(x)


def split(x):
    high = x.astype(BF16)
    return high, (x - high.astype(F32)).astype(BF16)


def dot3(a, b, lhs_dim, rhs_dim):
    dims = (((lhs_dim,), (rhs_dim,)), ((), ()))
    dot = functools.partial(lax.dot_general, dimension_numbers=dims, preferred_element_type=F32)
    return dot(a[0], b[0]) + dot(a[1], b[0]) + dot(a[0], b[1])


ERF_P = 0.3275911 * 0.7071067811865476
ERF_A = [0.5 * c for c in (1.061405429, -1.453152027, 1.421413741, -0.284496736, 0.254829592)]


def gelu_parts(x):
    size = jnp.abs(x)
    t = pl.reciprocal(1.0 + ERF_P * size)
    e = jnp.exp(-0.5 * (x * x))
    poly = ERF_A[0]
    for c in ERF_A[1:]:
        poly = poly * t + c
    tail = poly * t * e
    cdf = jnp.where(x < 0.0, tail, 1.0 - tail)
    return x * cdf, cdf + x * (e * 0.3989422804014327)


BLOCK_ROWS = 512
BLOCKS = ROWS // BLOCK_ROWS


def tile_values(stat_row, member):
    return jnp.broadcast_to(
        jnp.sum(member * stat_row, axis=1, keepdims=True), (CAP, LANES)
    )


def norm_values(stat, member):
    n = stat[0:1]
    variance = stat[2:3] / n
    inv = lax.rsqrt(variance + NORM_EPSILON)
    sample = lax.broadcasted_iota(jnp.int32, (1, LANES), 1) < SAMPLES
    inv = jnp.where(sample, inv, 0.0)
    return tile_values(stat[1:2], member), tile_values(inv, member)


def by_tile(x):
    return x.reshape(-1, CAP, LANES)


def dense_kernel(
    stat_ref, member_ref, conv_ref, tiles_ref, grad_ref, mask_ref,
    gain_ref, nbias_ref, win_ref, bin_ref, wout_ref, bout_ref,
    out_ref, gscaled_ref, dwin_ref, dwout_ref, vec_ref, hvec_ref, sums_ref,
    win_hi, win_lo, wout_hi, wout_lo,
):
    step = pl.program_id(0)

    @pl.when(step == 0)
    def _():
        win_hi[...], win_lo[...] = split(win_ref[...])
        wout_hi[...], wout_lo[...] = split(wout_ref[...])
        dwin_ref[...] = jnp.zeros_like(dwin_ref)
        dwout_ref[...] = jnp.zeros_like(dwout_ref)
        vec_ref[...] = jnp.zeros_like(vec_ref)
        hvec_ref[...] = jnp.zeros_like(hvec_ref)
        sums_ref[...] = jnp.zeros_like(sums_ref)

    win = (win_hi[...], win_lo[...])
    wout = (wout_hi[...], wout_lo[...])
    mean, inv = norm_values(stat_ref[...], member_ref[...])
    mask = mask_ref[...]
    normed = [(by_tile(conv_ref[g]) - mean[None]) * inv[None] for g in range(GROUPS)]
    flat = lambda parts: jnp.concatenate([p.reshape(-1, LANES) for p in parts], axis=1)
    scaled = split(
        flat([normed[g] * gain_ref[g][None, None] + nbias_ref[g][None, None] for g in range(GROUPS)])
    )
    pre = dot3(scaled, win, 1, 0) + bin_ref[...]
    hidden, slope = gelu_parts(pre)
    hidden = split(hidden)
    update = dot3(hidden, wout, 1, 0) + bout_ref[...]
    g_update = [by_tile(grad_ref[g]) * mask for g in range(GROUPS)]
    for g in range(GROUPS):
        out = mask * (by_tile(tiles_ref[g]) + by_tile(update[:, g * LANES : (g + 1) * LANES]))
        out_ref[g] = out.reshape(-1, LANES)
    g_flat = flat(g_update)
    g_split = split(g_flat)
    g_pre = dot3(g_split, wout, 1, 1) * slope
    hvec_ref[...] += jnp.sum(g_pre, axis=0, keepdims=True)
    g_pre = split(g_pre)
    dwout_ref[...] += dot3(g_split, hidden, 0, 0)
    dwin_ref[...] += dot3(scaled, g_pre, 0, 0)
    g_scaled = dot3(g_pre, win, 1, 1)
    first = jnp.zeros((CAP, LANES), F32)
    second = jnp.zeros((CAP, LANES), F32)
    rows = []
    for g in range(GROUPS):
        gs = by_tile(g_scaled[:, g * LANES : (g + 1) * LANES])
        gscaled_ref[g] = gs.reshape(-1, LANES)
        gain_sum = jnp.sum(gs * normed[g], axis=0)
        bias_sum = jnp.sum(gs, axis=0)
        first = first + bias_sum * gain_ref[g][None]
        second = second + gain_sum * gain_ref[g][None]
        rows.append((jnp.sum(g_update[g], axis=0), gain_sum, bias_sum))
    for g in range(GROUPS):
        for i in range(3):
            vec_ref[g, i] += rows[g][i]
    sums_ref[0] += first
    sums_ref[1] += second


def dense(stat, member, conv, tiles, grad, mask, gain, nbias, win, bin_, wout, bout):
    block = pl.BlockSpec((GROUPS, BLOCK_ROWS, LANES), lambda i: (0, i, 0))
    mask_block = pl.BlockSpec((BLOCK_ROWS // CAP, CAP, LANES), lambda i: (i, 0, 0))
    whole = lambda *shape: pl.BlockSpec(shape, lambda i: (0,) * len(shape))
    shape = lambda *dims: jax.ShapeDtypeStruct(dims, F32)
    return pl.pallas_call(
        dense_kernel,
        grid=(BLOCKS,),
        in_specs=[
            whole(CAP, LANES), whole(CAP, LANES), block, block, block, mask_block,
            whole(GROUPS, LANES), whole(GROUPS, LANES),
            whole(256, HIDDEN_PAD), whole(1, HIDDEN_PAD),
            whole(HIDDEN_PAD, 256), whole(1, 256),
        ],
        out_specs=(
            block, block, whole(256, HIDDEN_PAD), whole(256, HIDDEN_PAD),
            whole(GROUPS, 3, CAP, LANES), whole(1, HIDDEN_PAD), whole(2, CAP, LANES),
        ),
        out_shape=(
            shape(GROUPS, ROWS, LANES), shape(GROUPS, ROWS, LANES),
            shape(256, HIDDEN_PAD), shape(256, HIDDEN_PAD),
            shape(GROUPS, 3, CAP, LANES), shape(1, HIDDEN_PAD), shape(2, CAP, LANES),
        ),
        scratch_shapes=[
            pltpu.VMEM((256, HIDDEN_PAD), BF16), pltpu.VMEM((256, HIDDEN_PAD), BF16),
            pltpu.VMEM((HIDDEN_PAD, 256), BF16), pltpu.VMEM((HIDDEN_PAD, 256), BF16),
        ],
        compiler_params=params(),
        name="dense",
    )(stat, member, conv, tiles, grad, mask, gain, nbias, win, bin_, wout, bout)


def back_kernel(
    near_ref, stat_ref, sum_ref, member_ref, conv_ref, gscaled_ref, padded_ref, mask_ref,
    gain_ref, w_ref,
    own_out, p0, p1, p2, p3, dw_ref, db_ref, gconv, gpad, pool, sems,
):
    member = member_ref[...]
    stat = stat_ref[...]
    mean, inv = norm_values(stat, member)
    sums = sum_ref[...]
    sample = lax.broadcasted_iota(jnp.int32, (1, LANES), 1) < SAMPLES
    share = jnp.where(sample, 1.0 / stat[0:1], 0.0)
    first = tile_values(sums[0:1] * share, member)
    second = tile_values(sums[1:2] * share, member)
    for g in range(GROUPS):
        gain = gain_ref[g][None, None]

        def gradient(r, acc):
            rows = pl.ds(r * SIDE * CAP, SIDE * CAP)
            normed = (by_tile(conv_ref[g, rows, :]) - mean[None]) * inv[None]
            g_normed = by_tile(gscaled_ref[g, rows, :]) * gain
            value = (mask_ref[pl.ds(r * SIDE, SIDE)] * inv[None]) * (
                g_normed - first[None] - normed * second[None]
            )
            gconv[g, rows, :] = value.reshape(-1, LANES)
            return acc + jnp.sum(value, axis=0)

        db_ref[g] = lax.fori_loop(0, SIDE, gradient, jnp.zeros((CAP, LANES), F32)) * lane_mask(g)

        def input_row(r, carry):
            low = jnp.maximum(r - (SIDE - 1), 0)
            high = jnp.minimum(r, KSIZE - 1)

            def tap(a, acc):
                x = by_tile(gconv[g, pl.ds((r - a) * SIDE * CAP, SIDE * CAP), :])
                for b in range(KSIZE):
                    part = w_ref[g, a * KSIZE + b][None] * x
                    acc = acc[:b] + tuple(
                        acc[b + i] + part[i] for i in range(SIDE)
                    ) + acc[b + SIDE :]
                return acc

            acc = lax.fori_loop(
                low, high + 1, tap, tuple(jnp.zeros((CAP, LANES), F32) for _ in range(PAD))
            )
            for i in range(PAD):
                gpad[g, pl.ds((r * PAD + i) * CAP, CAP), :] = acc[i]
            return carry

        lax.fori_loop(0, PAD, input_row, 0)

        def zero(i, carry):
            pool[g, pl.ds(i * RIM_ROWS, RIM_ROWS), :] = jnp.zeros((RIM_ROWS, LANES), F32)
            return carry

        lax.fori_loop(0, 6, zero, 0)

    def scatter(t, carry):
        for k in range(8):
            q = near_ref[t, k]
            for src, src_step, dst, dst_step, length in RUNS[k]:
                for g in range(GROUPS):
                    place = pl.ds(q + dst * CAP, length, stride=dst_step * CAP)
                    pool[g, place, :] = (
                        pool[g, place, :]
                        + gpad[g, pl.ds(src * CAP + t, length, stride=src_step * CAP), :]
                    )
        return carry

    lax.fori_loop(0, CAP, scatter, 0)
    targets = [p0, p1, None, p2, p3]
    copies = [
        pltpu.make_async_copy(
            pool.at[:, pl.ds(i * RIM_ROWS, RIM_ROWS), :], target, sems.at[i]
        )
        for i, target in enumerate(targets)
        if target is not None
    ]
    for copy in copies:
        copy.start()
    for g in range(GROUPS):
        for r in range(SIDE):
            own_out[g, pl.ds(r * SIDE * CAP, SIDE * CAP), :] = gpad[
                g, pl.ds(((r + RIM) * PAD + RIM) * CAP, SIDE * CAP), :
            ]
    add_rims(own_out, [lambda g, rows: pool[g, pl.ds(2 * RIM_ROWS + rows.start, rows.size), :]])

    for g in range(GROUPS):

        def weight_row(a, carry):
            def one(r, acc):
                x = by_tile(padded_ref[g, pl.ds((r + a) * PAD * CAP, PAD * CAP), :])
                y = by_tile(gconv[g, pl.ds(r * SIDE * CAP, SIDE * CAP), :])
                return tuple(
                    acc[b] + jnp.sum(x[b : b + SIDE] * y, axis=0) for b in range(KSIZE)
                )

            acc = lax.fori_loop(
                0, SIDE, one, tuple(jnp.zeros((CAP, LANES), F32) for _ in range(KSIZE))
            )
            for b in range(KSIZE):
                dw_ref[g, a * KSIZE + b] = acc[b]
            return carry

        lax.fori_loop(0, KSIZE, weight_row, 0)
    for copy in copies:
        copy.wait()


def add_rims(own, sources):
    for g in range(GROUPS):
        spans = [(0, 0, 48), (13 * SIDE, 48, 48)]
        for r in range(RIM, SIDE - RIM):
            spans += [(r * SIDE + c, rim_index(r, c), RIM) for c in (0, SIDE - RIM)]
        for first, rim, cells in spans:
            rows = pl.ds(first * CAP, cells * CAP)
            value = own[g, rows, :]
            for source in sources:
                value = value + source(g, pl.ds(rim * CAP, cells * CAP))
            own[g, rows, :] = value


def conv_backward(near, stat, sums, member, conv, gscaled, padded, mask, gain, w):
    shape = lambda *dims: jax.ShapeDtypeStruct(dims, F32)
    rim = shape(GROUPS, RIM_ROWS, LANES)
    return pl.pallas_call(
        back_kernel,
        in_specs=[SMEM_SPEC] + [VMEM_SPEC] * 9,
        out_specs=(VMEM_SPEC,) + (ANY_SPEC,) * 4 + (VMEM_SPEC,) * 2,
        out_shape=(
            shape(GROUPS, ROWS, LANES), rim, rim, rim, rim,
            shape(GROUPS, KSIZE * KSIZE, CAP, LANES), shape(GROUPS, CAP, LANES),
        ),
        scratch_shapes=[
            pltpu.VMEM((GROUPS, ROWS, LANES), F32),
            pltpu.VMEM((GROUPS, PAD * PAD * CAP, LANES), F32),
            pltpu.VMEM((GROUPS, 6 * RIM_ROWS, LANES), F32),
            pltpu.SemaphoreType.DMA((5,)),
        ],
        compiler_params=params(),
        name="conv_backward",
    )(near, stat, sums, member, conv, gscaled, padded, mask, gain, w)


def final_kernel(own_ref, grad_ref, mask_ref, r0, r1, r2, r3, o_ref, total):
    t = pl.program_id(0)

    @pl.when(t == 0)
    def _():
        for g in range(GROUPS):

            def add(r, carry):
                rows = pl.ds(r * SIDE * CAP, SIDE * CAP)
                value = by_tile(grad_ref[g, rows, :]) * mask_ref[pl.ds(r * SIDE, SIDE)]
                total[g, rows, :] = own_ref[g, rows, :] + value.reshape(-1, LANES)
                return carry

            lax.fori_loop(0, SIDE, add, 0)
        add_rims(total, [lambda g, rows, ref=ref: ref[g, rows, :] for ref in (r0, r1, r2, r3)])

    for g in range(GROUPS):
        o_ref[0, g * LANES : (g + 1) * LANES, :] = total[g, pl.ds(t, CELLS, stride=CAP), :].T


def final(own, grad, mask, returned):
    return pl.pallas_call(
        final_kernel,
        grid=(CAP,),
        in_specs=[VMEM_SPEC] * 7,
        out_specs=pl.BlockSpec((1, 2 * LANES, CELLS), lambda t: (t, 0, 0)),
        out_shape=jax.ShapeDtypeStruct((CAP, 250, CELLS), F32),
        scratch_shapes=[pltpu.VMEM((GROUPS, ROWS, LANES), F32)],
        compiler_params=params(),
        name="final",
    )(own, grad, mask, *returned)


def passed_along(block, axis, distance):
    devices = range(lax.axis_size(axis))
    route = [(i - distance, i) for i in devices if i - distance in devices]
    return lax.ppermute(block, axis, route)


def lane_groups(x):
    x = jnp.pad(x, [(0, 0)] * (x.ndim - 1) + [(0, 6)])
    x = x.reshape(x.shape[:-1] + (GROUPS, LANES))
    return jnp.moveaxis(x, -2, 0)


def from_groups(x):
    x = jnp.moveaxis(x, 0, -2)
    return x.reshape(x.shape[:-2] + (GROUPS * LANES,))[..., :250]


def prepare(device, tile_counts, ocean_mask, neighbours, sample_ids):
    slot = lax.iota(jnp.int32, CAP)
    filled = (slot < tile_counts[0]).astype(F32)
    oceanic = ocean_mask.astype(F32) * filled[:, None]
    mask = jnp.broadcast_to(oceanic.T[:, :, None], (CELLS, CAP, LANES))
    lane = lax.iota(jnp.int32, LANES)
    member = (sample_ids[:, None] == lane[None, :]).astype(F32)
    source = neighbours // CAP - device + REACH
    place = source * RIM_ROWS + neighbours % CAP
    near = jnp.where(neighbours >= 0, place, 5 * RIM_ROWS)
    return mask, member, near


OFFSETS = [-2, -1, 1, 2]


def local(
    tiles_in, conv_weight, conv_bias, norm_gain, norm_bias, weight_in, bias_in,
    weight_out, bias_out, grad_out, tile_counts, ocean_mask, neighbours, sample_ids,
):
    device = lax.axis_index("tiles")
    mask, member, near = prepare(device, tile_counts, ocean_mask, neighbours, sample_ids)
    w = jnp.broadcast_to(
        lane_groups(conv_weight.T)[:, :, None, :], (GROUPS, KSIZE * KSIZE, CAP, LANES)
    )
    b = jnp.broadcast_to(lane_groups(conv_bias)[:, None, :], (GROUPS, CAP, LANES))
    gain, nbias = lane_groups(norm_gain), lane_groups(norm_bias)
    win = jnp.pad(weight_in, ((0, 6), (0, 24)))
    wout = jnp.pad(weight_out, ((0, 24), (0, 6)))
    bin_ = jnp.pad(bias_in, (0, 24))[None]
    bout = jnp.pad(bias_out, (0, 6))[None]

    tiles, rim = to_rows(tiles_in, True)
    received = [passed_along(rim, "tiles", -offset) for offset in OFFSETS]
    grad = to_rows(grad_out, False)
    padded, conv, stat = conv_forward(near, tiles, rim, received, w, b, mask, member)
    stat = reduce_small(stat, merge_stats, 1, "reduce_stats")
    out, gscaled, dwin, dwout, vec, hvec, sums = dense(
        stat, member, conv, tiles, grad, mask, gain, nbias, win, bin_, wout, bout
    )
    tile_sums = jnp.sum(sums, axis=2)
    sample_sums = jnp.pad(jnp.dot(tile_sums, member, precision="highest"), ((0, 6), (0, 0)))
    sample_sums = reduce_small(sample_sums, merge_sums, 2, "reduce_sums")
    dwin, dwout, vec, hvec = lax.psum((dwin, dwout, jnp.sum(vec, axis=2), hvec), "tiles")
    own, p0, p1, p2, p3, dw, db = conv_backward(
        near, stat, sample_sums, member, conv, gscaled, padded, mask, gain, w
    )
    returned = [
        passed_along(block, "tiles", offset) for block, offset in zip((p0, p1, p2, p3), OFFSETS)
    ]
    output = from_rows(out)
    dw, db = lax.psum((jnp.sum(dw, axis=2), jnp.sum(db, axis=1)), "tiles")
    grad_tiles = final(own, grad, mask, returned)
    active = jnp.sum(jnp.where(lax.iota(jnp.int32, LANES) < SAMPLES, stat[0], 0.0)) / 250.0
    share = 1.0 / active
    vec = from_groups(vec) * share
    return (
        output,
        grad_tiles,
        from_groups(dw).T * share,
        from_groups(db) * share,
        vec[1],
        vec[2],
        dwin[:250, :1000] * share,
        hvec[0, :1000] * share,
        dwout[:250, :1000].T * share,
        vec[0],
    )


def solution(mesh):
    tiles = P("tiles")
    whole = P()
    return jax.shard_map(
        local,
        mesh=mesh,
        in_specs=(tiles,) + (whole,) * 8 + (tiles,) * 5,
        out_specs=(tiles, tiles) + (whole,) * 8,
        check_vma=False,
    )
```

```python
import functools

import jax
import jax.numpy as jnp
from jax import lax
from jax.experimental import pallas as pl
from jax.experimental.pallas import tpu as pltpu
from jax.sharding import PartitionSpec as P

SIDE = 16
KSIZE = 7
RIM = 3
REACH = 2
SAMPLES = 5
CAP = 8
CELLS = SIDE * SIDE
PAD = SIDE + 2 * RIM
LANES = 128
GROUPS = 2
ROWS = CELLS * CAP
RIM_CELLS = 156
RIM_ROWS = RIM_CELLS * CAP
HIDDEN_PAD = 1024
NORM_EPSILON = 1e-05
F32 = jnp.float32
BF16 = jnp.bfloat16
MIB = 1 << 20
MESH = pl.DeviceIdType.MESH
VMEM_SPEC = pl.BlockSpec(memory_space=pltpu.VMEM)
SMEM_SPEC = pl.BlockSpec(memory_space=pltpu.SMEM)
ANY_SPEC = pl.BlockSpec(memory_space=pl.ANY)


def params(mib=56, **more):
    return pltpu.CompilerParams(vmem_limit_bytes=mib * MIB, **more)


HALF_RIM = RIM_ROWS // 2


def rim_spans(half):
    base = half * 78
    outer = 0 if half == 0 else SIDE - RIM
    inner = RIM if half == 0 else SIDE // 2
    spans = [(outer * SIDE, base, 48)]
    for i in range(5):
        spans.append(((inner + i) * SIDE, base + 48 + i * RIM, RIM))
        spans.append(((inner + i) * SIDE + SIDE - RIM, base + 63 + i * RIM, RIM))
    return spans


RIM_OF = {
    first + i: rim + i
    for half in range(2)
    for first, rim, cells in rim_spans(half)
    for i in range(cells)
}


def rim_index(r, c):
    return RIM_OF[r * SIDE + c]


def region_runs():
    spans = {-1: (0, SIDE - RIM, RIM), 0: (RIM, 0, SIDE), 1: (RIM + SIDE, 0, RIM)}
    order = [(-1, -1), (-1, 0), (-1, 1), (0, -1), (0, 1), (1, -1), (1, 0), (1, 1)]
    runs = []
    for dr, dc in order:
        dst_r, src_r, rows = spans[dr]
        dst_c, src_c, cols = spans[dc]
        found = []

        def add(cells):
            start = 0
            while start < len(cells):
                stop = start + 1
                while (
                    stop < len(cells)
                    and stop - start < 8
                    and cells[stop][0] - cells[stop - 1][0] == cells[1][0] - cells[0][0]
                    and cells[stop][1] - cells[stop - 1][1] == cells[1][1] - cells[0][1]
                ):
                    stop += 1
                step = (cells[1][0] - cells[0][0], cells[1][1] - cells[0][1])
                found.append((cells[start][0], step[0], cells[start][1], step[1], stop - start))
                start = stop

        if dr == 0:
            for j in range(cols):
                cells = [
                    ((dst_r + i) * PAD + dst_c + j, rim_index(src_r + i, src_c + j))
                    for i in range(rows)
                ]
                for low, high in ((0, RIM), (RIM, 8), (8, SIDE - RIM), (SIDE - RIM, SIDE)):
                    add(cells[low:high])
        else:
            for i in range(rows):
                add(
                    [
                        ((dst_r + i) * PAD + dst_c + j, rim_index(src_r + i, src_c + j))
                        for j in range(cols)
                    ]
                )
        runs.append(found)
    return runs


RUNS = region_runs()


ROLES = 6
PIECES = [(g, half) for half in range(2) for g in range(GROUPS)]


def piece(ref, role, p):
    g, half = PIECES[p]
    return ref.at[g, pl.ds(role * RIM_ROWS + half * HALF_RIM, HALF_RIM), :]


def halo_peers():
    me = lax.axis_index("tiles")
    total = lax.axis_size("tiles")
    sign = 2 * (me % 2) - 1
    ahead = (me + 2 * sign + total) % total
    behind = (me - 2 * sign + total) % total
    return ahead, behind, me - sign


def remote(src, dst, send, recv, peer):
    return pltpu.make_async_remote_copy(
        src_ref=src, dst_ref=dst, send_sem=send, recv_sem=recv,
        device_id=(peer,), device_id_type=MESH,
    )


def greet(peers):
    barrier = pltpu.get_barrier_semaphore()
    for peer in peers:
        pl.semaphore_signal(barrier, inc=1, device_id=(peer,), device_id_type=MESH)
    return lambda: pl.semaphore_wait(barrier, len(peers))


def load_native(x_ref, buf, sems, first=0):
    copies = []
    for g, half in PIECES:
        rows = 1024 if g == 0 else 976
        copies.append(
            pltpu.make_async_copy(
                x_ref.at[pl.ds(g * 1024, rows), pl.ds(half * LANES, LANES)],
                buf.at[half, pl.ds(g * 1024, rows), :],
                sems.at[first + len(copies)],
            )
        )
    return copies


def to_rows(buf, out, g, half):
    for t in range(CAP):
        block = buf[half, pl.ds(g * 1024 + t, LANES, stride=CAP), :]
        out[g, pl.ds(half * 1024 + t, LANES, stride=CAP), :] = block.T


def store_native(buf, out_ref, sems, first=0):
    copies = []
    for g, half in PIECES:
        rows = 1024 if g == 0 else 976
        copies.append(
            pltpu.make_async_copy(
                buf.at[half, pl.ds(g * 1024, rows), :],
                out_ref.at[pl.ds(g * 1024, rows), pl.ds(half * LANES, LANES)],
                sems.at[first + len(copies)],
            )
        )
    return copies


def from_rows(rows, buf, g, half):
    for t in range(CAP):
        block = rows[g, pl.ds(half * 1024 + t, LANES, stride=CAP), :]
        buf[half, pl.ds(g * 1024 + t, LANES, stride=CAP), :] = block.T


def lane_mask(g):
    lane = lax.broadcasted_iota(jnp.int32, (CAP, LANES), 1)
    return (lane < 250 - g * LANES).astype(F32)


def shape(*dims):
    return jax.ShapeDtypeStruct(dims, F32)


def buffer(*dims):
    return pltpu.VMEM(dims, F32)


def semaphores(count):
    return pltpu.SemaphoreType.DMA((count,))


INNER = 8
OUTER = 16


def inner_peers():
    me = lax.axis_index("tiles")
    group, place = me // INNER, me % INNER
    return [group * INNER + (place + j) % INNER for j in range(1, INNER)]


def outer_peers():
    me = lax.axis_index("tiles")
    group, place = me // INNER, me % INNER
    return [((group + j) % OUTER) * INNER + place for j in range(1, OUTER)]


def exchange(x, send, recv, slots, first, mine, peers):
    copies = [
        remote(x, slots.at[mine], send.at[first + j], recv.at[first + j], peer)
        for j, peer in enumerate(peers)
    ]
    for copy in copies:
        copy.start()
    slots[mine] = x[...]
    for copy in copies:
        copy.wait()


def reduce_vector(merge, partial, inner, outer, send, recv):
    me = lax.axis_index("tiles")
    exchange(partial, send, recv, inner, 0, me % INNER, inner_peers())
    partial[...] = merge(inner[...])
    exchange(partial, send, recv, outer, INNER, me // INNER, outer_peers())
    return merge(outer[...])


def merge_stats(parts):
    n = jnp.sum(parts[:, 0:1], axis=0)
    mean = jnp.sum(parts[:, 0:1] * parts[:, 1:2], axis=0) / jnp.maximum(n, 1.0)
    off = parts[:, 1:2] - mean[None]
    m2 = jnp.sum(parts[:, 2:3] + parts[:, 0:1] * off * off, axis=0)
    return stack_rows(n, mean, m2)


def stack_rows(*rows):
    row_id = lax.broadcasted_iota(jnp.int32, (CAP, LANES), 0)
    value = jnp.zeros((CAP, LANES), F32)
    for i, row in enumerate(rows):
        value = jnp.where(row_id == i, row, value)
    return value


def merge_sums(parts):
    return jnp.sum(parts, axis=0)


def by_tile(x):
    return x.reshape(-1, CAP, LANES)


def own_conv(g, padded, conv, w, lanes_ref):
    bias = jnp.broadcast_to(lanes_ref[g, 0:1, :], (CAP, LANES))[None]

    def row(r, carry):
        acc = jnp.broadcast_to(bias, (SIDE, CAP, LANES))
        for a in range(KSIZE):
            x = by_tile(padded[g, pl.ds((r + a) * PAD * CAP, PAD * CAP), :])
            for b in range(KSIZE):
                acc = acc + w[g, a * KSIZE + b][None] * x[b : b + SIDE]
        conv[g, pl.ds(r * SIDE * CAP, SIDE * CAP), :] = acc.reshape(-1, LANES)
        return carry

    lax.fori_loop(0, SIDE, row, 0)


def gather(near_ref, pool, padded):
    def fill(t, carry):
        for k in range(8):
            q = near_ref[t, k]
            for dst, dst_step, src, src_step, length in RUNS[k]:
                for g in range(GROUPS):
                    padded[g, pl.ds(dst * CAP + t, length, stride=dst_step * CAP), :] = pool[
                        g, pl.ds(q + src * CAP, length, stride=src_step * CAP), :
                    ]
        return carry

    lax.fori_loop(0, CAP, fill, 0)


def halo_conv(padded, conv, w):
    blank = jnp.zeros((RIM, CAP, LANES), F32)
    for g in range(GROUPS):
        for r in [0, 1, 2, 13, 14, 15]:
            rows = pl.ds(r * SIDE * CAP, SIDE * CAP)
            acc = by_tile(conv[g, rows, :])
            for a in range(KSIZE):
                if RIM <= r + a < RIM + SIDE:
                    continue
                x = by_tile(padded[g, pl.ds(((r + a) * PAD + RIM) * CAP, SIDE * CAP), :])
                x = jnp.concatenate([blank, x, blank], axis=0)
                for b in range(KSIZE):
                    acc = acc + w[g, a * KSIZE + b][None] * x[b : b + SIDE]
            conv[g, rows, :] = acc.reshape(-1, LANES)

        def columns(r, carry):
            left = [jnp.zeros((CAP, LANES), F32) for _ in range(RIM)]
            right = [jnp.zeros((CAP, LANES), F32) for _ in range(RIM)]
            for a in range(KSIZE):
                first = (r + a) * PAD * CAP
                xl = by_tile(padded[g, pl.ds(first, RIM * CAP), :])
                xr = by_tile(padded[g, pl.ds(first + (RIM + SIDE) * CAP, RIM * CAP), :])
                for c in range(RIM):
                    for b in range(RIM - c):
                        left[c] = left[c] + w[g, a * KSIZE + b] * xl[c + b]
                    for b in range(KSIZE - 1 - c, KSIZE):
                        right[c] = right[c] + w[g, a * KSIZE + b] * xr[c + b - KSIZE + 1]
            for c in range(RIM):
                cell = pl.ds((r * SIDE + c) * CAP, CAP)
                conv[g, cell, :] = conv[g, cell, :] + left[c]
                cell = pl.ds((r * SIDE + SIDE - RIM + c) * CAP, CAP)
                conv[g, cell, :] = conv[g, cell, :] + right[c]
            return carry

        lax.fori_loop(0, SIDE, columns, 0)


def local_stats(conv, mask, member):
    zero = jnp.zeros((CAP, LANES), F32)
    sums, cells = zero, zero
    for g in range(GROUPS):

        def add(r, carry):
            rows = pl.ds(r * SIDE * CAP, SIDE * CAP)
            m = by_tile(mask[rows, :])
            x = by_tile(conv[g, rows, :])
            return carry[0] + jnp.sum(x * m, axis=0), carry[1] + jnp.sum(m, axis=0)

        total, cells = lax.fori_loop(0, SIDE, add, (zero, zero))
        sums = sums + total
    entries = 250.0 * cells
    total = jnp.broadcast_to(jnp.sum(sums, axis=1, keepdims=True), (CAP, LANES))
    mean = total / jnp.maximum(entries, 1.0)
    squares = zero
    for g in range(GROUPS):

        def square(r, acc):
            rows = pl.ds(r * SIDE * CAP, SIDE * CAP)
            diff = by_tile(conv[g, rows, :]) - mean[None]
            return acc + jnp.sum(diff * diff * by_tile(mask[rows, :]), axis=0)

        squares = squares + lax.fori_loop(0, SIDE, square, zero) * lane_mask(g)
    spread = jnp.broadcast_to(jnp.sum(squares, axis=1, keepdims=True), (CAP, LANES))
    n_tile = member * entries
    n = jnp.sum(n_tile, axis=0, keepdims=True)
    centre = jnp.sum(n_tile * mean, axis=0, keepdims=True) / jnp.maximum(n, 1.0)
    off = mean - centre
    m2 = jnp.sum(member * spread + n_tile * off * off, axis=0, keepdims=True)
    return stack_rows(n, centre, m2)


def forward_kernel(
    near_ref, x_ref, g_ref, ocean_ref, member_ref, wt_ref, lanes_ref,
    tiles_out, grad_out, mask_out, conv_out, padded_out, stat_ref,
    xbuf, gbuf, tiles, grad, mask, pool, padded, conv, w, inner, outer, partial,
    load_sem, store_sem, send, recv, small_send, small_recv,
):
    ahead, behind, partner = halo_peers()
    ready = greet([ahead, behind, partner] + inner_peers() + outer_peers())
    loads = load_native(x_ref, xbuf, load_sem) + load_native(g_ref, gbuf, load_sem, 4)
    for copy in loads:
        copy.start()
    for half in range(2):
        xbuf[half, pl.ds(2000, 48), :] = jnp.zeros((48, LANES), F32)
        gbuf[half, pl.ds(2000, 48), :] = jnp.zeros((48, LANES), F32)
    for g in range(GROUPS):
        pool[g, pl.ds(5 * RIM_ROWS, RIM_ROWS), :] = jnp.zeros((RIM_ROWS, LANES), F32)

        def clear(i, carry):
            padded[g, pl.ds(i * PAD * CAP, PAD * CAP), :] = jnp.zeros((PAD * CAP, LANES), F32)
            return carry

        lax.fori_loop(0, PAD, clear, 0)
    taps = wt_ref[...]
    taps = jnp.concatenate([taps, jnp.zeros((KSIZE * KSIZE, 6), F32)], axis=1)
    for g in range(GROUPS):
        for k in range(KSIZE * KSIZE):
            w[g, k] = jnp.broadcast_to(
                taps[k : k + 1, g * LANES : (g + 1) * LANES], (CAP, LANES)
            )
    ready()

    sends = [[], [], []]
    for p, (g, half) in enumerate(PIECES):
        loads[p].wait()
        to_rows(xbuf, tiles, g, half)
        for first, rim, cells in rim_spans(half):
            pool[g, pl.ds(4 * RIM_ROWS + rim * CAP, cells * CAP), :] = tiles[
                g, pl.ds(first * CAP, cells * CAP), :
            ]
        for kind, (role, peer) in enumerate([(1, ahead), (0, behind), (3, partner)]):
            i = kind * 4 + p
            copy = remote(
                piece(pool, 4, p), piece(pool, role, p), send.at[i], recv.at[i], peer
            )
            copy.start()
            sends[kind].append(copy)
    stores = [pltpu.make_async_copy(tiles, tiles_out, store_sem.at[0])]
    stores[0].start()
    for g in range(GROUPS):

        def centre(r, carry):
            padded[g, pl.ds(((r + RIM) * PAD + RIM) * CAP, SIDE * CAP), :] = tiles[
                g, pl.ds(r * SIDE * CAP, SIDE * CAP), :
            ]
            return carry

        lax.fori_loop(0, SIDE, centre, 0)
    for p, (g, half) in enumerate(PIECES):
        loads[4 + p].wait()
        to_rows(gbuf, grad, g, half)
    for half in range(2):
        for t in range(CAP):
            row = ocean_ref[t : t + 1, half * LANES : (half + 1) * LANES]
            mask[pl.ds(half * 1024 + t, LANES, stride=CAP), :] = jnp.broadcast_to(
                row, (LANES, LANES)
            ).T
    for source, target in [(grad, grad_out), (mask, mask_out)]:
        stores.append(pltpu.make_async_copy(source, target, store_sem.at[len(stores)]))
        stores[-1].start()

    passed = []

    def pass_on(p):
        sends[0][p].wait_recv()
        copy = remote(
            piece(pool, 1, p), piece(pool, 2, p), send.at[12 + p], recv.at[12 + p], partner
        )
        copy.start()
        passed.append(copy)

    own_conv(0, padded, conv, w, lanes_ref)
    pass_on(0)
    own_conv(1, padded, conv, w, lanes_ref)
    for p in range(1, 4):
        pass_on(p)
    for copy in sends[1] + sends[2] + passed:
        copy.wait_recv()
    gather(near_ref, pool, padded)
    halo_conv(padded, conv, w)
    for source, target in [(conv, conv_out), (padded, padded_out)]:
        stores.append(pltpu.make_async_copy(source, target, store_sem.at[len(stores)]))
        stores[-1].start()
    partial[...] = local_stats(conv, mask, member_ref[...])
    stat_ref[...] = reduce_vector(merge_stats, partial, inner, outer, small_send, small_recv)
    for copy in sends[0] + sends[1] + sends[2] + passed:
        copy.wait_send()
    for copy in stores:
        copy.wait()


def forward(near, x, g, ocean, member, wt, lanes):
    rows = (GROUPS, ROWS, LANES)
    wide = (GROUPS, PAD * PAD * CAP, LANES)
    return pl.pallas_call(
        forward_kernel,
        in_specs=[SMEM_SPEC, ANY_SPEC, ANY_SPEC] + [VMEM_SPEC] * 4,
        out_specs=(ANY_SPEC,) * 5 + (VMEM_SPEC,),
        out_shape=(
            shape(*rows), shape(*rows), shape(ROWS, LANES), shape(*rows), shape(*wide),
            shape(CAP, LANES),
        ),
        scratch_shapes=[buffer(*rows)] * 4 + [
            buffer(ROWS, LANES), buffer(GROUPS, ROLES * RIM_ROWS, LANES), buffer(*wide),
            buffer(*rows), buffer(GROUPS, KSIZE * KSIZE, CAP, LANES),
            buffer(INNER, CAP, LANES), buffer(OUTER, CAP, LANES), buffer(CAP, LANES),
            semaphores(8), semaphores(5), semaphores(16), semaphores(16),
            semaphores(INNER + OUTER), semaphores(INNER + OUTER),
        ],
        compiler_params=params(collective_id=1, has_side_effects=True),
        name="forward",
    )(near, x, g, ocean, member, wt, lanes)


def sums_kernel(sums_ref, member_ref, o_ref, inner, outer, partial, send, recv):
    ready = greet(inner_peers() + outer_peers())
    rows = [
        jnp.sum(member_ref[...] * jnp.sum(sums_ref[i], axis=1, keepdims=True), axis=0, keepdims=True)
        for i in range(2)
    ]
    partial[...] = stack_rows(*rows)
    ready()
    o_ref[...] = reduce_vector(merge_sums, partial, inner, outer, send, recv)


def reduce_sums(sums, member):
    return pl.pallas_call(
        sums_kernel,
        in_specs=[VMEM_SPEC] * 2,
        out_specs=VMEM_SPEC,
        out_shape=shape(CAP, LANES),
        scratch_shapes=[
            buffer(INNER, CAP, LANES), buffer(OUTER, CAP, LANES), buffer(CAP, LANES),
            semaphores(INNER + OUTER), semaphores(INNER + OUTER),
        ],
        compiler_params=pltpu.CompilerParams(collective_id=2, has_side_effects=True),
        name="reduce_sums",
    )(sums, member)


def split(x):
    high = x.astype(BF16)
    return high, (x - high.astype(F32)).astype(BF16)


def dot3(a, b, lhs_dim, rhs_dim):
    dims = (((lhs_dim,), (rhs_dim,)), ((), ()))
    dot = functools.partial(lax.dot_general, dimension_numbers=dims, preferred_element_type=F32)
    return dot(a[0], b[0]) + dot(a[1], b[0]) + dot(a[0], b[1])


ERF_P = 0.3275911 * 0.7071067811865476
ERF_A = [0.5 * c for c in (1.061405429, -1.453152027, 1.421413741, -0.284496736, 0.254829592)]


def gelu_parts(x):
    size = jnp.abs(x)
    t = pl.reciprocal(1.0 + ERF_P * size)
    e = jnp.exp(-0.5 * (x * x))
    poly = ERF_A[0]
    for c in ERF_A[1:]:
        poly = poly * t + c
    tail = poly * t * e
    cdf = jnp.where(x < 0.0, tail, 1.0 - tail)
    return x * cdf, cdf + x * (e * 0.3989422804014327)


BLOCK_ROWS = 512
BLOCKS = ROWS // BLOCK_ROWS


def tile_values(stat_row, member):
    return jnp.broadcast_to(
        jnp.sum(member * stat_row, axis=1, keepdims=True), (CAP, LANES)
    )


def norm_values(stat, member):
    n = stat[0:1]
    variance = stat[2:3] / n
    inv = lax.rsqrt(variance + NORM_EPSILON)
    sample = lax.broadcasted_iota(jnp.int32, (1, LANES), 1) < SAMPLES
    inv = jnp.where(sample, inv, 0.0)
    return tile_values(stat[1:2], member), tile_values(inv, member)


def edge_zero(x, rows, columns):
    row = lax.broadcasted_iota(jnp.int32, x.shape, 0)
    column = lax.broadcasted_iota(jnp.int32, x.shape, 1)
    return jnp.where((row < rows) & (column < columns), x, 0.0)


def dense_kernel(
    stat_ref, member_ref, conv_ref, tiles_ref, grad_ref, mask_ref,
    lanes_ref, win_ref, bin_ref, wout_ref,
    out_ref, gscaled_ref, dw_ref, vec_ref, hvec_ref, sums_ref,
    win_hi, win_lo, wout_hi, wout_lo,
):
    step = pl.program_id(0)

    @pl.when(step == 0)
    def _():
        win_hi[...], win_lo[...] = split(edge_zero(win_ref[...], 1000, 250))
        wout_hi[...], wout_lo[...] = split(edge_zero(wout_ref[...], 1000, 250))
        dw_ref[...] = jnp.zeros_like(dw_ref)
        vec_ref[...] = jnp.zeros_like(vec_ref)
        hvec_ref[...] = jnp.zeros_like(hvec_ref)
        sums_ref[...] = jnp.zeros_like(sums_ref)

    win = (win_hi[...], win_lo[...])
    wout = (wout_hi[...], wout_lo[...])
    mean, inv = norm_values(stat_ref[...], member_ref[...])
    mask = by_tile(mask_ref[...])
    line = lambda g, i: lanes_ref[g, i : i + 1, :]
    normed = [(by_tile(conv_ref[g]) - mean[None]) * inv[None] for g in range(GROUPS)]
    flat = lambda parts: jnp.concatenate([p.reshape(-1, LANES) for p in parts], axis=1)
    scaled = split(
        flat([normed[g] * line(g, 1)[None] + line(g, 2)[None] for g in range(GROUPS)])
    )
    pre = dot3(scaled, win, 1, 1) + bin_ref[...]
    hidden, slope = gelu_parts(pre)
    hidden = split(hidden)
    update = dot3(hidden, wout, 1, 0)
    g_update = [by_tile(grad_ref[g]) * mask for g in range(GROUPS)]
    for g in range(GROUPS):
        part = by_tile(update[:, g * LANES : (g + 1) * LANES] + line(g, 3))
        out_ref[g] = (mask * (by_tile(tiles_ref[g]) + part)).reshape(-1, LANES)
    g_split = split(flat(g_update))
    g_pre = dot3(g_split, wout, 1, 1) * slope
    hvec_ref[...] += jnp.sum(g_pre, axis=0, keepdims=True)
    g_pre = split(g_pre)
    dw_ref[0:256, :] += dot3(scaled, g_pre, 0, 0)
    dw_ref[256:512, :] += dot3(g_split, hidden, 0, 0)
    g_scaled = dot3(g_pre, win, 1, 0)
    first = jnp.zeros((CAP, LANES), F32)
    second = jnp.zeros((CAP, LANES), F32)
    for g in range(GROUPS):
        gs = by_tile(g_scaled[:, g * LANES : (g + 1) * LANES])
        gscaled_ref[g] = gs.reshape(-1, LANES)
        gain_sum = jnp.sum(gs * normed[g], axis=0)
        bias_sum = jnp.sum(gs, axis=0)
        first = first + bias_sum * line(g, 1)
        second = second + gain_sum * line(g, 1)
        vec_ref[g, 0] += jnp.sum(g_update[g], axis=0)
        vec_ref[g, 1] += gain_sum
        vec_ref[g, 2] += bias_sum
    sums_ref[0] += first
    sums_ref[1] += second


def dense(stat, member, conv, tiles, grad, mask, lanes, win, bin_, wout):
    block = pl.BlockSpec((GROUPS, BLOCK_ROWS, LANES), lambda i: (0, i, 0))
    mask_block = pl.BlockSpec((BLOCK_ROWS, LANES), lambda i: (i, 0))
    whole = lambda *dims: pl.BlockSpec(dims, lambda i: (0,) * len(dims))
    return pl.pallas_call(
        dense_kernel,
        grid=(BLOCKS,),
        in_specs=[
            whole(CAP, LANES), whole(CAP, LANES), block, block, block, mask_block,
            whole(GROUPS, CAP, LANES), whole(HIDDEN_PAD, 256), whole(1, HIDDEN_PAD),
            whole(HIDDEN_PAD, 256),
        ],
        out_specs=(
            block, block, whole(512, HIDDEN_PAD),
            whole(GROUPS, 3, CAP, LANES), whole(1, HIDDEN_PAD), whole(2, CAP, LANES),
        ),
        out_shape=(
            shape(GROUPS, ROWS, LANES), shape(GROUPS, ROWS, LANES), shape(512, HIDDEN_PAD),
            shape(GROUPS, 3, CAP, LANES), shape(1, HIDDEN_PAD), shape(2, CAP, LANES),
        ),
        scratch_shapes=[pltpu.VMEM((HIDDEN_PAD, 256), BF16)] * 4,
        compiler_params=params(),
        name="dense",
    )(stat, member, conv, tiles, grad, mask, lanes, win, bin_, wout)


def back_kernel(
    near_ref, stat_ref, sum_ref, member_ref, conv_ref, gscaled_ref, mask_ref, lanes_ref, wt_ref,
    own_out, pool_out, gconv, db_ref, gpad, pool, w, sems,
):
    taps = wt_ref[...]
    taps = jnp.concatenate([taps, jnp.zeros((KSIZE * KSIZE, 6), F32)], axis=1)
    for g in range(GROUPS):
        for k in range(KSIZE * KSIZE):
            w[g, k] = jnp.broadcast_to(
                taps[k : k + 1, g * LANES : (g + 1) * LANES], (CAP, LANES)
            )
    member = member_ref[...]
    stat = stat_ref[...]
    mean, inv = norm_values(stat, member)
    sums = sum_ref[...]
    sample = lax.broadcasted_iota(jnp.int32, (1, LANES), 1) < SAMPLES
    share = jnp.where(sample, 1.0 / stat[0:1], 0.0)
    first = tile_values(sums[0:1] * share, member)
    second = tile_values(sums[1:2] * share, member)
    for g in range(GROUPS):
        gain = lanes_ref[g, 1:2, :][None]

        def gradient(r, acc):
            rows = pl.ds(r * SIDE * CAP, SIDE * CAP)
            normed = (by_tile(conv_ref[g, rows, :]) - mean[None]) * inv[None]
            g_normed = by_tile(gscaled_ref[g, rows, :]) * gain
            value = (by_tile(mask_ref[rows, :]) * inv[None]) * (
                g_normed - first[None] - normed * second[None]
            )
            gconv[g, rows, :] = value.reshape(-1, LANES)
            return acc + jnp.sum(value, axis=0)

        db_ref[g] = lax.fori_loop(0, SIDE, gradient, jnp.zeros((CAP, LANES), F32)) * lane_mask(g)

        def input_row(r, carry):
            low = jnp.maximum(r - (SIDE - 1), 0)
            high = jnp.minimum(r, KSIZE - 1)

            def tap(a, acc):
                x = by_tile(gconv[g, pl.ds((r - a) * SIDE * CAP, SIDE * CAP), :])
                for b in range(KSIZE):
                    part = w[g, a * KSIZE + b][None] * x
                    acc = (
                        acc[:b] + tuple(acc[b + i] + part[i] for i in range(SIDE)) + acc[b + SIDE :]
                    )
                return acc

            acc = lax.fori_loop(
                low, high + 1, tap, tuple(jnp.zeros((CAP, LANES), F32) for _ in range(PAD))
            )
            for i in range(PAD):
                gpad[g, pl.ds((r * PAD + i) * CAP, CAP), :] = acc[i]
            return carry

        lax.fori_loop(0, PAD, input_row, 0)

        def zero(i, carry):
            pool[g, pl.ds(i * RIM_ROWS, RIM_ROWS), :] = jnp.zeros((RIM_ROWS, LANES), F32)
            return carry

        lax.fori_loop(0, ROLES, zero, 0)

    def scatter(t, carry):
        for k in range(8):
            q = near_ref[t, k]
            for src, src_step, dst, dst_step, length in RUNS[k]:
                for g in range(GROUPS):
                    place = pl.ds(q + dst * CAP, length, stride=dst_step * CAP)
                    pool[g, place, :] = (
                        pool[g, place, :]
                        + gpad[g, pl.ds(src * CAP + t, length, stride=src_step * CAP), :]
                    )
        return carry

    lax.fori_loop(0, CAP, scatter, 0)
    copy = pltpu.make_async_copy(
        pool.at[:, pl.ds(0, (ROLES - 1) * RIM_ROWS), :], pool_out, sems.at[0]
    )
    copy.start()
    for g in range(GROUPS):
        for r in range(SIDE):
            own_out[g, pl.ds(r * SIDE * CAP, SIDE * CAP), :] = gpad[
                g, pl.ds(((r + RIM) * PAD + RIM) * CAP, SIDE * CAP), :
            ]
    copy.wait()


def conv_backward(near, stat, sums, member, conv, gscaled, mask, lanes, wt):
    rows = (GROUPS, ROWS, LANES)
    return pl.pallas_call(
        back_kernel,
        in_specs=[SMEM_SPEC] + [VMEM_SPEC] * 8,
        out_specs=(VMEM_SPEC, ANY_SPEC, VMEM_SPEC, VMEM_SPEC),
        out_shape=(
            shape(*rows), shape(GROUPS, (ROLES - 1) * RIM_ROWS, LANES), shape(*rows),
            shape(GROUPS, CAP, LANES),
        ),
        scratch_shapes=[
            buffer(GROUPS, PAD * PAD * CAP, LANES), buffer(GROUPS, ROLES * RIM_ROWS, LANES),
            buffer(GROUPS, KSIZE * KSIZE, CAP, LANES), semaphores(1),
        ],
        compiler_params=params(),
        name="conv_backward",
    )(near, stat, sums, member, conv, gscaled, mask, lanes, wt)


SMALL = 16
HALF = 256


def tail_kernel(
    pool_ref, gconv_ref, padded_ref, rows_ref, big_ref, vec_ref, hvec_ref, db_ref,
    rim_out, big_out, small_ref, native_out,
    pool, gconv, padded, rows, native, pay, got, half, other, slots, zslots, big, small, tile,
    sslots, zcslots, load_sem, store_sem, send, recv,
):
    me = lax.axis_index("tiles")
    core, z, xy = me % 2, (me // 2) % 4, me // INNER
    ahead, behind, partner = halo_peers()
    z_peers = [xy * INNER + ((z + j) % 4) * 2 + core for j in range(1, 4)]
    xy_peers = outer_peers()
    zc_peers = inner_peers()
    ready = greet([ahead, behind, partner] + zc_peers + xy_peers)
    mine = pl.multiple_of(core * HALF, HALF)
    theirs = pl.multiple_of((1 - core) * HALF, HALF)

    loads = [
        pltpu.make_async_copy(source, target, load_sem.at[i])
        for i, (source, target) in enumerate(
            [
                (rows_ref, rows),
                (pool_ref.at[:, pl.ds(RIM_ROWS, RIM_ROWS), :], pool.at[0]),
                (gconv_ref, gconv),
                (padded_ref, padded),
                (big_ref.at[pl.ds(mine, HALF), :], half),
                (pool_ref.at[:, pl.ds(4 * RIM_ROWS, RIM_ROWS), :], pool.at[1]),
            ]
        )
    ]
    for copy in loads:
        copy.start()
    loads[0].wait()
    stores = store_native(native, native_out, store_sem)
    for p, (g, part) in enumerate(PIECES):
        from_rows(rows, native, g, part)
        stores[p].start()
    ready()

    used = [0]

    def start(source, target, peer):
        i = used[0]
        used[0] += 1
        copy = remote(source, target, send.at[i], recv.at[i], peer)
        copy.start()
        return copy

    def part_of(ref, p):
        g, part = PIECES[p]
        return ref.at[g, pl.ds(part * HALF_RIM, HALF_RIM), :]

    payload = [start(piece(pool_ref, 2, p), part_of(pay, p), partner) for p in range(4)]
    direct = [start(piece(pool_ref, 0, p), part_of(got.at[0], p), ahead) for p in range(4)]
    halves = start(big_ref.at[pl.ds(theirs, HALF), :], other, partner)
    near = [start(piece(pool_ref, 3, p), part_of(got.at[2], p), partner) for p in range(4)]
    loads[1].wait()
    merged = []
    for p, (g, part) in enumerate(PIECES):
        payload[p].wait_recv()
        span = pl.ds(part * HALF_RIM, HALF_RIM)
        pool[0, g, span, :] = pool[0, g, span, :] + pay[g, span, :]
        merged.append(start(part_of(pool.at[0], p), part_of(got.at[1], p), behind))

    def weight_rows(g, low, high):
        def weight_row(a, carry):
            def one(r, acc):
                x = by_tile(padded[g, pl.ds((r + a) * PAD * CAP, PAD * CAP), :])
                y = by_tile(gconv[g, pl.ds(r * SIDE * CAP, SIDE * CAP), :])
                return tuple(
                    acc[b] + jnp.sum(x[b : b + SIDE] * y, axis=0) for b in range(KSIZE)
                )

            acc = lax.fori_loop(
                0, SIDE, one, tuple(jnp.zeros((CAP, LANES), F32) for _ in range(KSIZE))
            )
            for b in range(KSIZE):
                small[g, pl.ds(a * KSIZE + b, 1), :] = jnp.sum(acc[b], axis=0, keepdims=True)
            return carry

        lax.fori_loop(low, high, weight_row, 0)

    loads[2].wait()
    loads[3].wait()
    weight_rows(0, 0, 2)
    loads[4].wait()
    halves.wait_recv()
    half[...] = half[...] + other[...]
    scattered = [
        start(
            half.at[pl.ds(pl.multiple_of((peer // INNER) * 16, 16), 16), :], slots.at[xy], peer
        )
        for peer in xy_peers
    ]
    slots[xy] = half[pl.ds(pl.multiple_of(xy * 16, 16), 16), :]
    weight_rows(0, 2, KSIZE)
    weight_rows(1, 0, 4)
    for copy in scattered:
        copy.wait_recv()
    big_rows = pl.ds(pl.multiple_of(core * HALF + xy * 16, 16), 16)
    z_lanes = lambda i: pl.ds(pl.multiple_of(i * 256, 256), 256)
    for copy in scattered:
        copy.wait_send()
    half[0:16, :] = jnp.sum(slots[...], axis=0)
    z_scattered = [
        start(
            half.at[pl.ds(0, 16), z_lanes((peer // 2) % 4)], zslots.at[z], peer
        )
        for peer in z_peers
    ]
    zslots[z] = half[0:16, z_lanes(z)]
    weight_rows(1, 4, KSIZE)
    for g in range(GROUPS):
        lines = [jnp.sum(db_ref[g], axis=0, keepdims=True)]
        lines += [jnp.sum(vec_ref[g, i], axis=0, keepdims=True) for i in range(3)]
        lines += [hvec_ref[0:1, pl.ds((g * 4 + i) * LANES, LANES)] for i in range(4)]
        for i, line in enumerate(lines):
            small[g, pl.ds(49 + i, 1), :] = line
        small[g, pl.ds(57, 7), :] = jnp.zeros((7, LANES), F32)
    small_tile = lambda q: small.at[q // 8, pl.ds(pl.multiple_of((q % 8) * CAP, CAP), CAP), :]
    small_scattered = [
        start(small_tile(peer // INNER), sslots.at[xy], peer) for peer in xy_peers
    ]
    sslots[xy] = small[xy // 8, pl.ds(pl.multiple_of((xy % 8) * CAP, CAP), CAP), :]
    for copy in z_scattered:
        copy.wait_recv()
    big[big_rows, z_lanes(z)] = jnp.sum(zslots[...], axis=0)
    own = big.at[big_rows, z_lanes(z)]
    z_gathered = [start(own, own, peer) for peer in z_peers]
    for copy in small_scattered:
        copy.wait_recv()
    tile[...] = jnp.sum(sslots[...], axis=0)
    zc_gathered = [start(tile, zcslots.at[me % INNER], peer) for peer in zc_peers]
    zcslots[me % INNER] = tile[...]
    for copy in z_gathered:
        copy.wait_recv()
    own = big.at[big_rows, :]
    xy_gathered = [start(own, own, peer) for peer in xy_peers]
    for copy in zc_gathered:
        copy.wait_recv()
    small_ref[xy] = jnp.sum(zcslots[...], axis=0)
    small_gathered = [start(small_ref.at[xy], small_ref.at[xy], peer) for peer in xy_peers]
    for copy in xy_gathered:
        copy.wait_recv()
    own = big.at[pl.ds(mine, HALF), :]
    crossed = start(own, own, partner)
    loads[5].wait()
    for copy in near + direct:
        copy.wait_recv()
    for p, (g, part) in enumerate(PIECES):
        merged[p].wait_recv()
        span = pl.ds(part * HALF_RIM, HALF_RIM)
        pool[1, g, span, :] = (pool[1, g, span, :] + got[2, g, span, :]) + (
            got[0, g, span, :] + got[1, g, span, :]
        )
    finish = [pltpu.make_async_copy(pool.at[1], rim_out, store_sem.at[4])]
    finish[0].start()
    crossed.wait_recv()
    finish.append(pltpu.make_async_copy(big, big_out, store_sem.at[5]))
    finish[1].start()
    for copy in small_gathered:
        copy.wait_recv()
    every = payload + direct + [halves] + near + merged + z_scattered + small_scattered
    every += z_gathered + zc_gathered + xy_gathered + small_gathered + [crossed]
    for copy in every:
        copy.wait_send()
    for copy in stores + finish:
        copy.wait()


def tail(pool, gconv, padded, rows, big, vec, hvec, db):
    rim = (GROUPS, RIM_ROWS, LANES)
    count = 17 + 15 + 3 + 15 + 3 + 7 + 15 + 15 + 1
    return pl.pallas_call(
        tail_kernel,
        in_specs=[ANY_SPEC] * 5 + [VMEM_SPEC] * 3,
        out_specs=(ANY_SPEC, ANY_SPEC, VMEM_SPEC, ANY_SPEC),
        out_shape=(
            shape(*rim), shape(512, HIDDEN_PAD), shape(SMALL, CAP, LANES), shape(2000, 256),
        ),
        scratch_shapes=[
            buffer(2, *rim), buffer(GROUPS, ROWS, LANES),
            buffer(GROUPS, PAD * PAD * CAP, LANES), buffer(GROUPS, ROWS, LANES),
            buffer(GROUPS, ROWS, LANES), buffer(*rim), buffer(3, *rim),
            buffer(HALF, HIDDEN_PAD), buffer(HALF, HIDDEN_PAD), buffer(OUTER, 16, HIDDEN_PAD),
            buffer(4, 16, 256), buffer(512, HIDDEN_PAD), buffer(GROUPS, 64, LANES),
            buffer(CAP, LANES), buffer(OUTER, CAP, LANES), buffer(INNER, CAP, LANES),
            semaphores(6), semaphores(6), semaphores(count), semaphores(count),
        ],
        compiler_params=params(collective_id=3, has_side_effects=True),
        name="tail",
    )(pool, gconv, padded, rows, big, vec, hvec, db)


def final_kernel(
    own_ref, grad_ref, mask_ref, rim_ref, big_ref, small_ref, stat_ref, native_ref,
    out_ref, tiles_ref, dwin_ref, dwout_ref, dconv_ref, lines_ref, hline_ref,
    total, buf, through, sems,
):
    whole = pltpu.make_async_copy(native_ref, through, sems.at[4])
    whole.start()
    stores = store_native(buf, tiles_ref, sems)
    for p, (g, half) in enumerate(PIECES):

        def add(r, carry):
            rows = pl.ds(r * SIDE * CAP, SIDE * CAP)
            total[g, rows, :] = own_ref[g, rows, :] + grad_ref[g, rows, :] * mask_ref[rows, :]
            return carry

        lax.fori_loop(half * 8, half * 8 + 8, add, 0)
        for first, rim, cells in rim_spans(half):
            rows = pl.ds(first * CAP, cells * CAP)
            total[g, rows, :] = total[g, rows, :] + rim_ref[g, pl.ds(rim * CAP, cells * CAP), :]
        from_rows(total, buf, g, half)
        stores[p].start()
    whole.wait()
    whole = pltpu.make_async_copy(through, out_ref, sems.at[5])
    whole.start()
    sample = lax.broadcasted_iota(jnp.int32, (1, LANES), 1) < SAMPLES
    cells = jnp.sum(jnp.where(sample, stat_ref[0:1, :], 0.0), axis=1, keepdims=True)
    share = 250.0 / cells
    dwin_ref[...] = big_ref[0:256, :].T[:1000, :250] * share
    dwout_ref[...] = big_ref[256:512, :].T[:1000, :250] * share
    flat = []
    for g in range(GROUPS):
        flat.append(
            jnp.concatenate([small_ref[g * 8 + i] for i in range(8)], axis=0) * share
        )
    flat = jnp.concatenate(flat, axis=1)
    dconv_ref[...] = flat[0:49, :250]
    lines_ref[...] = flat[48:56, :250]
    for g in range(GROUPS):
        for i in range(4):
            j = 53 + i
            hline_ref[0:1, pl.ds((g * 4 + i) * LANES, LANES)] = (
                flat[j : j + 1, g * LANES : (g + 1) * LANES]
            )
    whole.wait()
    for copy in stores:
        copy.wait()


def final(own, grad, mask, rim, big, small, stat, native):
    return pl.pallas_call(
        final_kernel,
        in_specs=[VMEM_SPEC] * 7 + [ANY_SPEC],
        out_specs=(ANY_SPEC,) * 2 + (VMEM_SPEC,) * 5,
        out_shape=(
            shape(2000, 256), shape(2000, 256), shape(1000, 250), shape(1000, 250),
            shape(49, 250), shape(8, 250), shape(1, HIDDEN_PAD),
        ),
        scratch_shapes=[
            buffer(GROUPS, ROWS, LANES), buffer(GROUPS, ROWS, LANES), buffer(2000, 256), semaphores(6)
        ],
        compiler_params=params(),
        name="final",
    )(own, grad, mask, rim, big, small, stat, native)


def native(x):
    return jnp.transpose(x, (1, 0, 2)).reshape(2000, CELLS)


def from_native(x):
    return jnp.transpose(x.reshape(250, CAP, CELLS), (1, 0, 2))


def prepare(device, tile_counts, ocean_mask, neighbours, sample_ids):
    slot = lax.iota(jnp.int32, CAP)
    filled = (slot < tile_counts[0]).astype(F32)
    ocean = ocean_mask.astype(F32) * filled[:, None]
    lane = lax.iota(jnp.int32, LANES)
    member = (sample_ids[:, None] == lane[None, :]).astype(F32)
    offset = (neighbours // CAP - device) * (2 * (device % 2) - 1)
    role = jnp.full_like(offset, 4)
    for i, value in enumerate((2, -2, 1, -1)):
        role = jnp.where(offset == value, i, role)
    place = role * RIM_ROWS + neighbours % CAP
    near = jnp.where(neighbours >= 0, place, 5 * RIM_ROWS)
    return ocean, member, near


def local(
    tiles_in, conv_weight, conv_bias, norm_gain, norm_bias, weight_in, bias_in,
    weight_out, bias_out, grad_out, tile_counts, ocean_mask, neighbours, sample_ids,
):
    device = lax.axis_index("tiles")
    ocean, member, near = prepare(device, tile_counts, ocean_mask, neighbours, sample_ids)
    lanes = jnp.stack([conv_bias, norm_gain, norm_bias, bias_out])
    lanes = jnp.pad(lanes, ((0, 4), (0, 6))).reshape(CAP, GROUPS, LANES).transpose(1, 0, 2)
    bin_ = jnp.pad(bias_in, (0, 24))[None]
    wt = conv_weight.T
    tiles, grad, mask, conv, padded, stat = forward(
        near, native(tiles_in), native(grad_out), ocean, member, wt, lanes
    )
    out, gscaled, big, vec, hvec, sums = dense(
        stat, member, conv, tiles, grad, mask, lanes, weight_in.T, bin_, weight_out
    )
    sample_sums = reduce_sums(sums, member)
    own, pool, gconv, db = conv_backward(
        near, stat, sample_sums, member, conv, gscaled, mask, lanes, wt
    )
    rim, big, small, out = tail(pool, gconv, padded, out, big, vec, hvec, db)
    output, grad_tiles, dwin, dwout, dconv, lines, hline = final(
        own, grad, mask, rim, big, small, stat, out
    )
    return (
        from_native(output),
        from_native(grad_tiles),
        dconv.T,
        lines[1],
        lines[3],
        lines[4],
        dwin.T,
        hline[0, :1000],
        dwout,
        lines[2],
    )


def solution(mesh):
    tiles = P("tiles")
    whole = P()
    return jax.shard_map(
        local,
        mesh=mesh,
        in_specs=(tiles,) + (whole,) * 8 + (tiles,) * 5,
        out_specs=(tiles, tiles) + (whole,) * 8,
        check_vma=False,
    )
```

```python
import functools

import jax
import jax.numpy as jnp
from jax import lax
from jax.experimental import pallas as pl
from jax.experimental.pallas import tpu as pltpu
from jax.sharding import PartitionSpec as P

SIDE = 16
KSIZE = 7
RIM = 3
REACH = 2
SAMPLES = 5
CAP = 8
CELLS = SIDE * SIDE
PAD = SIDE + 2 * RIM
LANES = 128
GROUPS = 2
ROWS = CELLS * CAP
RIM_CELLS = 156
RIM_ROWS = RIM_CELLS * CAP
HIDDEN_PAD = 1024
NORM_EPSILON = 1e-05
F32 = jnp.float32
BF16 = jnp.bfloat16
MIB = 1 << 20
MESH = pl.DeviceIdType.MESH
VMEM_SPEC = pl.BlockSpec(memory_space=pltpu.VMEM)
SMEM_SPEC = pl.BlockSpec(memory_space=pltpu.SMEM)
ANY_SPEC = pl.BlockSpec(memory_space=pl.ANY)


def params(mib=60, **more):
    return pltpu.CompilerParams(vmem_limit_bytes=mib * MIB, **more)


HALF_RIM = RIM_ROWS // 2


def rim_spans(half):
    base = half * 78
    outer = 0 if half == 0 else SIDE - RIM
    inner = RIM if half == 0 else SIDE // 2
    spans = [(outer * SIDE, base, 48)]
    for i in range(5):
        spans.append(((inner + i) * SIDE, base + 48 + i * RIM, RIM))
        spans.append(((inner + i) * SIDE + SIDE - RIM, base + 63 + i * RIM, RIM))
    return spans


RIM_OF = {
    first + i: rim + i
    for half in range(2)
    for first, rim, cells in rim_spans(half)
    for i in range(cells)
}


def rim_index(r, c):
    return RIM_OF[r * SIDE + c]


def region_runs():
    spans = {-1: (0, SIDE - RIM, RIM), 0: (RIM, 0, SIDE), 1: (RIM + SIDE, 0, RIM)}
    order = [(-1, -1), (-1, 0), (-1, 1), (0, -1), (0, 1), (1, -1), (1, 0), (1, 1)]
    runs = []
    for dr, dc in order:
        dst_r, src_r, rows = spans[dr]
        dst_c, src_c, cols = spans[dc]
        found = []

        def add(cells):
            start = 0
            while start < len(cells):
                stop = start + 1
                while (
                    stop < len(cells)
                    and stop - start < 8
                    and cells[stop][0] - cells[stop - 1][0] == cells[1][0] - cells[0][0]
                    and cells[stop][1] - cells[stop - 1][1] == cells[1][1] - cells[0][1]
                ):
                    stop += 1
                step = (cells[1][0] - cells[0][0], cells[1][1] - cells[0][1])
                found.append((cells[start][0], step[0], cells[start][1], step[1], stop - start))
                start = stop

        if dr == 0:
            for j in range(cols):
                cells = [
                    ((dst_r + i) * PAD + dst_c + j, rim_index(src_r + i, src_c + j))
                    for i in range(rows)
                ]
                for low, high in ((0, RIM), (RIM, 8), (8, SIDE - RIM), (SIDE - RIM, SIDE)):
                    add(cells[low:high])
        else:
            for i in range(rows):
                add(
                    [
                        ((dst_r + i) * PAD + dst_c + j, rim_index(src_r + i, src_c + j))
                        for j in range(cols)
                    ]
                )
        runs.append(found)
    return runs


RUNS = region_runs()


ROLES = 6
PIECES = [(g, half) for g in range(GROUPS) for half in range(2)]


def piece(ref, role, p):
    g, half = PIECES[p]
    return ref[g].at[pl.ds(role * RIM_ROWS + half * HALF_RIM, HALF_RIM), :]


def halo_peers():
    me = lax.axis_index("tiles")
    total = lax.axis_size("tiles")
    sign = 2 * (me % 2) - 1
    ahead = (me + 2 * sign + total) % total
    behind = (me - 2 * sign + total) % total
    return ahead, behind, me - sign


def remote(src, dst, send, recv, peer):
    return pltpu.make_async_remote_copy(
        src_ref=src, dst_ref=dst, send_sem=send, recv_sem=recv,
        device_id=(peer,), device_id_type=MESH,
    )


def greet(peers):
    barrier = pltpu.get_barrier_semaphore()
    for peer in peers:
        pl.semaphore_signal(barrier, inc=1, device_id=(peer,), device_id_type=MESH)
    return lambda: pl.semaphore_wait(barrier, len(peers))


def load_native(x_ref, buf, sems, first=0):
    copies = []
    for g, half in PIECES:
        rows = 1024 if g == 0 else 976
        copies.append(
            pltpu.make_async_copy(
                x_ref.at[pl.ds(g * 1024, rows), pl.ds(half * LANES, LANES)],
                buf.at[half, pl.ds(g * 1024, rows), :],
                sems.at[first + len(copies)],
            )
        )
    return copies


def to_rows(buf, out, g, half):
    for t in range(CAP):
        block = buf[half, pl.ds(g * 1024 + t, LANES, stride=CAP), :]
        out[g, pl.ds(half * 1024 + t, LANES, stride=CAP), :] = block.T


def store_native(buf, out_ref, sems, first=0):
    copies = []
    for g, half in PIECES:
        rows = 1024 if g == 0 else 976
        copies.append(
            pltpu.make_async_copy(
                buf.at[half, pl.ds(g * 1024, rows), :],
                out_ref.at[pl.ds(g * 1024, rows), pl.ds(half * LANES, LANES)],
                sems.at[first + len(copies)],
            )
        )
    return copies


def from_rows(rows, buf, g, half):
    for t in range(CAP):
        block = rows[g, pl.ds(half * 1024 + t, LANES, stride=CAP), :]
        buf[half, pl.ds(g * 1024 + t, LANES, stride=CAP), :] = block.T


def lane_mask(g):
    lane = lax.broadcasted_iota(jnp.int32, (CAP, LANES), 1)
    return (lane < 250 - g * LANES).astype(F32)


def shape(*dims):
    return jax.ShapeDtypeStruct(dims, F32)


def buffer(*dims):
    return pltpu.VMEM(dims, F32)


def semaphores(count):
    return pltpu.SemaphoreType.DMA((count,))


INNER = 8
OUTER = 16


def inner_peers():
    me = lax.axis_index("tiles")
    group, place = me // INNER, me % INNER
    return [group * INNER + (place + j) % INNER for j in range(1, INNER)]


def outer_peers():
    me = lax.axis_index("tiles")
    group, place = me // INNER, me % INNER
    return [((group + j) % OUTER) * INNER + place for j in range(1, OUTER)]


def exchange_start(x, send, recv, slots, first, mine, peers):
    copies = [
        remote(x, slots.at[mine], send.at[first + j], recv.at[first + j], peer)
        for j, peer in enumerate(peers)
    ]
    for copy in copies:
        copy.start()
    slots[mine] = x[...]
    return copies


def merge_stats(parts):
    n = jnp.sum(parts[:, 0:1], axis=0)
    mean = jnp.sum(parts[:, 0:1] * parts[:, 1:2], axis=0) / jnp.maximum(n, 1.0)
    off = parts[:, 1:2] - mean[None]
    m2 = jnp.sum(parts[:, 2:3] + parts[:, 0:1] * off * off, axis=0)
    return stack_rows(n, mean, m2)


def stack_rows(*rows):
    row_id = lax.broadcasted_iota(jnp.int32, (CAP, LANES), 0)
    value = jnp.zeros((CAP, LANES), F32)
    for i, row in enumerate(rows):
        value = jnp.where(row_id == i, row, value)
    return value


def merge_sums(parts):
    return jnp.sum(parts, axis=0)


def by_tile(x):
    return x.reshape(-1, CAP, LANES)


def own_conv(g, padded, conv, w, lanes_ref):
    bias = jnp.broadcast_to(lanes_ref[g, 0:1, :], (CAP, LANES))[None]

    def row(r, carry):
        acc = jnp.broadcast_to(bias, (SIDE, CAP, LANES))
        for a in range(KSIZE):
            x = by_tile(padded[g, pl.ds((r + a) * PAD * CAP, PAD * CAP), :])
            for b in range(KSIZE):
                acc = acc + w[g, a * KSIZE + b][None] * x[b : b + SIDE]
        conv[g, pl.ds(r * SIDE * CAP, SIDE * CAP), :] = acc.reshape(-1, LANES)
        return carry

    lax.fori_loop(0, SIDE, row, 0)


def place_of(n, me):
    offset = (n // CAP - me) * (2 * (me % 2) - 1)
    role = jnp.where(offset == 2, 0, jnp.where(offset == -2, 1, 4))
    role = jnp.where(offset == 1, 2, jnp.where(offset == -1, 3, role))
    valid = n >= 0
    return jnp.where(valid, role, 5), jnp.where(valid, n % CAP, 0)


def gather(g, near_ref, me, pool, padded):
    def fill(t, carry):
        for k in range(8):
            role, slot = place_of(near_ref[t, k], me)
            q = role * RIM_ROWS + slot
            for dst, dst_step, src, src_step, length in RUNS[k]:
                padded[g, pl.ds(dst * CAP + t, length, stride=dst_step * CAP), :] = pool[g][
                    pl.ds(q + src * CAP, length, stride=src_step * CAP), :
                ]
        return carry

    lax.fori_loop(0, CAP, fill, 0)


def halo_conv(g, padded, conv, w):
    blank = jnp.zeros((RIM, CAP, LANES), F32)
    for r in [0, 1, 2, 13, 14, 15]:
        rows = pl.ds(r * SIDE * CAP, SIDE * CAP)
        acc = by_tile(conv[g, rows, :])
        for a in range(KSIZE):
            if RIM <= r + a < RIM + SIDE:
                continue
            x = by_tile(padded[g, pl.ds(((r + a) * PAD + RIM) * CAP, SIDE * CAP), :])
            x = jnp.concatenate([blank, x, blank], axis=0)
            for b in range(KSIZE):
                acc = acc + w[g, a * KSIZE + b][None] * x[b : b + SIDE]
        conv[g, rows, :] = acc.reshape(-1, LANES)

    def columns(r, carry):
        left = [jnp.zeros((CAP, LANES), F32) for _ in range(RIM)]
        right = [jnp.zeros((CAP, LANES), F32) for _ in range(RIM)]
        for a in range(KSIZE):
            first = (r + a) * PAD * CAP
            xl = by_tile(padded[g, pl.ds(first, RIM * CAP), :])
            xr = by_tile(padded[g, pl.ds(first + (RIM + SIDE) * CAP, RIM * CAP), :])
            for c in range(RIM):
                for b in range(RIM - c):
                    left[c] = left[c] + w[g, a * KSIZE + b] * xl[c + b]
                for b in range(KSIZE - 1 - c, KSIZE):
                    right[c] = right[c] + w[g, a * KSIZE + b] * xr[c + b - KSIZE + 1]
        for c in range(RIM):
            cell = pl.ds((r * SIDE + c) * CAP, CAP)
            conv[g, cell, :] = conv[g, cell, :] + left[c]
            cell = pl.ds((r * SIDE + SIDE - RIM + c) * CAP, CAP)
            conv[g, cell, :] = conv[g, cell, :] + right[c]
        return carry

    lax.fori_loop(0, SIDE, columns, 0)


def masked_sum(g, conv, mask):
    zero = jnp.zeros((CAP, LANES), F32)

    def add(r, carry):
        rows = pl.ds(r * SIDE * CAP, SIDE * CAP)
        m = by_tile(mask[rows, :])
        x = by_tile(conv[g, rows, :])
        return carry[0] + jnp.sum(x * m, axis=0), carry[1] + jnp.sum(m, axis=0)

    return lax.fori_loop(0, SIDE, add, (zero, zero))


def local_stats(sums, cells, conv, mask, member):
    entries = 250.0 * cells
    total = jnp.broadcast_to(jnp.sum(sums, axis=1, keepdims=True), (CAP, LANES))
    mean = total / jnp.maximum(entries, 1.0)
    zero = jnp.zeros((CAP, LANES), F32)
    squares = zero
    for g in range(GROUPS):

        def square(r, acc):
            rows = pl.ds(r * SIDE * CAP, SIDE * CAP)
            diff = by_tile(conv[g, rows, :]) - mean[None]
            return acc + jnp.sum(diff * diff * by_tile(mask[rows, :]), axis=0)

        squares = squares + lax.fori_loop(0, SIDE, square, zero) * lane_mask(g)
    spread = jnp.broadcast_to(jnp.sum(squares, axis=1, keepdims=True), (CAP, LANES))
    n_tile = member * entries
    n = jnp.sum(n_tile, axis=0, keepdims=True)
    centre = jnp.sum(n_tile * mean, axis=0, keepdims=True) / jnp.maximum(n, 1.0)
    off = mean - centre
    m2 = jnp.sum(member * spread + n_tile * off * off, axis=0, keepdims=True)
    return stack_rows(n, centre, m2)


def split(x):
    high = x.astype(BF16)
    return high, (x - high.astype(F32)).astype(BF16)


def dot3(a, b, lhs_dim, rhs_dim):
    dims = (((lhs_dim,), (rhs_dim,)), ((), ()))
    left = jnp.concatenate([a[0], a[1], a[0]], axis=lhs_dim)
    right = jnp.concatenate([b[0], b[0], b[1]], axis=rhs_dim)
    return lax.dot_general(left, right, dimension_numbers=dims, preferred_element_type=F32)


ERF_P = 0.3275911 * 0.7071067811865476
ERF_A = [0.5 * c for c in (1.061405429, -1.453152027, 1.421413741, -0.284496736, 0.254829592)]


def gelu_parts(x):
    size = jnp.abs(x)
    t = pl.reciprocal(1.0 + ERF_P * size)
    e = jnp.exp(-0.5 * (x * x))
    poly = ERF_A[0]
    for c in ERF_A[1:]:
        poly = poly * t + c
    tail = poly * t * e
    cdf = jnp.where(x < 0.0, tail, 1.0 - tail)
    return x * cdf, cdf + x * (e * 0.3989422804014327)


BLOCK_ROWS = 512
BLOCKS = ROWS // BLOCK_ROWS
HIDDEN_PART = 512


def tile_values(stat_row, member):
    return jnp.broadcast_to(
        jnp.sum(member * stat_row, axis=1, keepdims=True), (CAP, LANES)
    )


def norm_values(stat, member):
    n = stat[0:1]
    variance = stat[2:3] / n
    inv = lax.rsqrt(variance + NORM_EPSILON)
    sample = lax.broadcasted_iota(jnp.int32, (1, LANES), 1) < SAMPLES
    inv = jnp.where(sample, inv, 0.0)
    return tile_values(stat[1:2], member), tile_values(inv, member)


def edge_zero(x, rows, columns):
    row = lax.broadcasted_iota(jnp.int32, x.shape, 0)
    column = lax.broadcasted_iota(jnp.int32, x.shape, 1)
    return jnp.where((row < rows) & (column < columns), x, 0.0)


def dense(
    stat, member, conv, tiles, grad, mask, lanes, bias_in, weights, out, gscaled, dw, vec, hvec
):
    win_hi, win_lo, wout_hi, wout_lo = weights
    mean, inv = norm_values(stat, member)
    line = lambda g, i: lanes[g, i : i + 1, :]
    flat = lambda parts: jnp.concatenate([p.reshape(-1, LANES) for p in parts], axis=1)
    zero = jnp.zeros((CAP, LANES), F32)

    def block(i, carry):
        first, second = carry
        rows = pl.ds(pl.multiple_of(i * BLOCK_ROWS, BLOCK_ROWS), BLOCK_ROWS)
        m = by_tile(mask[rows, :])
        normed = [(by_tile(conv[g, rows, :]) - mean[None]) * inv[None] for g in range(GROUPS)]
        scaled = split(
            flat([normed[g] * line(g, 1)[None] + line(g, 2)[None] for g in range(GROUPS)])
        )
        g_update = [by_tile(grad[g, rows, :]) * m for g in range(GROUPS)]
        g_split = split(flat(g_update))
        update = 0.0
        g_scaled = 0.0
        for h in range(0, HIDDEN_PAD, HIDDEN_PART):
            part = slice(h, h + HIDDEN_PART)
            win = (win_hi[part, :], win_lo[part, :])
            wout = (wout_hi[part, :], wout_lo[part, :])
            pre = dot3(scaled, win, 1, 1) + bias_in[:, part]
            g_hidden = dot3(g_split, wout, 1, 1)
            hidden, slope = gelu_parts(pre)
            hidden = split(hidden)
            g_pre = g_hidden * slope
            hvec[:, part] += jnp.sum(g_pre, axis=0, keepdims=True)
            g_pre = split(g_pre)
            update = update + dot3(hidden, wout, 1, 0)
            g_scaled = g_scaled + dot3(g_pre, win, 1, 0)
            dw[0:256, part] += dot3(scaled, g_pre, 0, 0)
            dw[256:512, part] += dot3(g_split, hidden, 0, 0)
        for g in range(GROUPS):
            span = slice(g * LANES, (g + 1) * LANES)
            value = m * (by_tile(tiles[g, rows, :]) + by_tile(update[:, span] + line(g, 3)))
            out[g, rows, :] = value.reshape(-1, LANES)
            gs = by_tile(g_scaled[:, span])
            gscaled[g, rows, :] = gs.reshape(-1, LANES)
            gain_sum = jnp.sum(gs * normed[g], axis=0)
            bias_sum = jnp.sum(gs, axis=0)
            first = first + bias_sum * line(g, 1)
            second = second + gain_sum * line(g, 1)
            vec[g, 0] += jnp.sum(g_update[g], axis=0)
            vec[g, 1] += gain_sum
            vec[g, 2] += bias_sum
        return first, second

    return lax.fori_loop(0, BLOCKS, block, (zero, zero))


def conv_gradient(stat, sums, member, conv, gscaled, mask, lanes, db):
    mean, inv = norm_values(stat, member)
    sample = lax.broadcasted_iota(jnp.int32, (1, LANES), 1) < SAMPLES
    share = jnp.where(sample, 1.0 / stat[0:1], 0.0)
    first = tile_values(sums[0:1] * share, member)
    second = tile_values(sums[1:2] * share, member)
    for g in range(GROUPS):
        gain = lanes[g, 1:2, :][None]

        def gradient(r, acc):
            rows = pl.ds(r * SIDE * CAP, SIDE * CAP)
            normed = (by_tile(conv[g, rows, :]) - mean[None]) * inv[None]
            g_normed = by_tile(gscaled[g, rows, :]) * gain
            value = (by_tile(mask[rows, :]) * inv[None]) * (
                g_normed - first[None] - normed * second[None]
            )
            gscaled[g, rows, :] = value.reshape(-1, LANES)
            return acc + jnp.sum(value, axis=0)

        db[g] = lax.fori_loop(0, SIDE, gradient, jnp.zeros((CAP, LANES), F32)) * lane_mask(g)


def input_gradient(g, gconv, w, gpad):
    def input_row(r, carry):
        low = jnp.maximum(r - (SIDE - 1), 0)
        high = jnp.minimum(r, KSIZE - 1)

        def tap(a, acc):
            x = by_tile(gconv[g, pl.ds((r - a) * SIDE * CAP, SIDE * CAP), :])
            for b in range(KSIZE):
                part = w[g, a * KSIZE + b][None] * x
                acc = acc[:b] + tuple(acc[b + i] + part[i] for i in range(SIDE)) + acc[b + SIDE :]
            return acc

        acc = lax.fori_loop(
            low, high + 1, tap, tuple(jnp.zeros((CAP, LANES), F32) for _ in range(PAD))
        )
        for i in range(PAD):
            gpad[pl.ds((r * PAD + i) * CAP, CAP), :] = acc[i]
        return carry

    lax.fori_loop(0, PAD, input_row, 0)


def own_gradient(g, gpad, grad, mask):
    def add(r, carry):
        rows = pl.ds(r * SIDE * CAP, SIDE * CAP)
        centre = gpad[pl.ds(((r + RIM) * PAD + RIM) * CAP, SIDE * CAP), :]
        grad[g, rows, :] = grad[g, rows, :] * mask[rows, :] + centre
        return carry

    lax.fori_loop(0, SIDE, add, 0)


def scatter_chunks():
    spans = {-1: (0, SIDE - RIM), 0: (RIM, 0), 1: (RIM + SIDE, 0)}
    order = [(-1, -1), (-1, 0), (-1, 1), (0, -1), (0, 1), (1, -1), (1, 0), (1, 1)]
    chunks = []
    for dr, dc in order:
        dst_r, src_r = spans[dr]
        dst_c, src_c = spans[dc]
        cols = RIM if dc else SIDE
        if dr == 0:
            groups = [range(0, 3), range(3, 8), range(8, 13), range(13, 16)]
        elif dc == 0:
            groups = [[0], [1], [2]]
        else:
            groups = [range(3)]
        chunks.append(
            [
                [
                    ((dst_r + i) * PAD + dst_c, rim_index(src_r + i, src_c), cols)
                    for i in group
                ]
                for group in groups
            ]
        )
    return chunks


CHUNKS = scatter_chunks()
CHUNK = 16
BACK_ROLES = 5


def onehots(near_ref, me, spread):
    size = (BACK_ROLES, CHUNK, CAP, LANES)
    role = lax.broadcasted_iota(jnp.int32, size, 0)
    cell = lax.broadcasted_iota(jnp.int32, size, 1)
    slot = lax.broadcasted_iota(jnp.int32, size, 2)
    lane = lax.broadcasted_iota(jnp.int32, size, 3)
    code = jnp.where(lane // CAP == cell, role * CAP + slot, -1)
    code = code.reshape(BACK_ROLES * LANES, LANES)
    lane = lax.broadcasted_iota(jnp.int32, (1, LANES), 1) % CAP
    for k in range(8):
        wanted = jnp.full((1, LANES), -2, jnp.int32)
        for t in range(CAP):
            n = near_ref[t, k]
            role, slot = place_of(n, me)
            wanted = jnp.where(lane == t, jnp.where(n >= 0, role * CAP + slot, -2), wanted)
        spread[k] = jnp.where(code == wanted, 1.0, 0.0).astype(BF16)


def scatter(g, gpad, spread, pool):
    for k in range(8):
        hot = spread[k]
        hot = jnp.concatenate([hot, hot], axis=1)
        for chunk in CHUNKS[k]:
            parts = [gpad[pl.ds(dst * CAP, cells * CAP), :] for dst, _, cells in chunk]
            used = sum(cells for _, _, cells in chunk)
            if used < CHUNK:
                parts.append(jnp.zeros(((CHUNK - used) * CAP, LANES), F32))
            value = parts[0] if len(parts) == 1 else jnp.concatenate(parts, axis=0)
            value = jnp.concatenate(split(value), axis=0)
            moved = jnp.dot(hot, value, preferred_element_type=F32)
            for role in range(BACK_ROLES):
                first = role * LANES
                for _, rim, cells in chunk:
                    rows = pl.ds(role * RIM_ROWS + rim * CAP, cells * CAP)
                    pool[g][rows, :] = pool[g][rows, :] + moved[first : first + cells * CAP]
                    first += cells * CAP


def weight_gradient(g, padded, gconv, small):
    def weight_row(a, carry):
        def one(r, acc):
            x = by_tile(padded[g, pl.ds((r + a) * PAD * CAP, PAD * CAP), :])
            y = by_tile(gconv[g, pl.ds(r * SIDE * CAP, SIDE * CAP), :])
            return tuple(acc[b] + jnp.sum(x[b : b + SIDE] * y, axis=0) for b in range(KSIZE))

        acc = lax.fori_loop(
            0, SIDE, one, tuple(jnp.zeros((CAP, LANES), F32) for _ in range(KSIZE))
        )
        for b in range(KSIZE):
            small[g, pl.ds(a * KSIZE + b, 1), :] = jnp.sum(acc[b], axis=0, keepdims=True)
        return carry

    lax.fori_loop(0, KSIZE, weight_row, 0)


HALF = 256
SLAB = 16


def block_kernel(
    near_ref, count_ref, sample_ref, x_ref, g_ref, ocean_ref, wt_ref, cb_ref, gain_ref, nbias_ref,
    bout_ref, bin_ref, win_ref, wout_ref,
    native_out, total_out, big_out, small_ref, stat_ref,
    xbuf, gbuf, tiles, grad, mask, pool0, pool1, padded, conv, w, lanes, member, bias_in,
    win_hi, win_lo, wout_hi, wout_lo, dw, vec, hvec, db, gpad, spread, pay, got,
    other, slots, zslots, slab, big, small, tile, sslots, zcslots, inner, outer, partial,
    load_sem, store_sem, send, recv,
):
    pool = (pool0, pool1)
    me = lax.axis_index("tiles")
    core, z, xy = me % 2, (me // 2) % 4, me // INNER
    ahead, behind, partner = halo_peers()
    z_peers = [xy * INNER + ((z + j) % 4) * 2 + core for j in range(1, 4)]
    xy_peers = outer_peers()
    zc_peers = inner_peers()
    ready = greet([ahead, behind, partner] + zc_peers + xy_peers)

    used = [0]
    started = []

    def start(source, target, peer):
        i = used[0]
        used[0] += 1
        copy = remote(source, target, send.at[i], recv.at[i], peer)
        copy.start()
        started.append(copy)
        return copy

    def arrived(copies):
        for copy in copies:
            copy.wait_recv()

    def sent():
        for copy in started:
            copy.wait_send()
        started.clear()

    loads = load_native(x_ref, xbuf, load_sem) + load_native(g_ref, gbuf, load_sem, 4)
    for copy in loads:
        copy.start()
    for half in range(2):
        xbuf[half, pl.ds(2000, 48), :] = jnp.zeros((48, LANES), F32)
        gbuf[half, pl.ds(2000, 48), :] = jnp.zeros((48, LANES), F32)
    for g in range(GROUPS):
        pool[g][pl.ds(5 * RIM_ROWS, RIM_ROWS), :] = jnp.zeros((RIM_ROWS, LANES), F32)

        def clear(i, carry):
            padded[g, pl.ds(i * PAD * CAP, PAD * CAP), :] = jnp.zeros((PAD * CAP, LANES), F32)
            return carry

        lax.fori_loop(0, PAD, clear, 0)
    taps = wt_ref[...]
    taps = jnp.concatenate([taps, jnp.zeros((KSIZE * KSIZE, 6), F32)], axis=1)
    for g in range(GROUPS):
        for k in range(KSIZE * KSIZE):
            w[g, k] = jnp.broadcast_to(
                taps[k : k + 1, g * LANES : (g + 1) * LANES], (CAP, LANES)
            )
    ready()

    out_ahead, out_behind, out_partner = [], [], []
    for p, (g, half) in enumerate(PIECES):
        loads[p].wait()
        to_rows(xbuf, tiles, g, half)
        for first, rim, cells in rim_spans(half):
            pool[g][pl.ds(4 * RIM_ROWS + rim * CAP, cells * CAP), :] = tiles[
                g, pl.ds(first * CAP, cells * CAP), :
            ]
        own = piece(pool, 4, p)
        out_ahead.append(start(own, piece(pool, 1, p), ahead))
        out_behind.append(start(own, piece(pool, 0, p), behind))
        out_partner.append(start(own, piece(pool, 3, p), partner))

    for i, ref in enumerate((cb_ref, gain_ref, nbias_ref, bout_ref)):
        line = jnp.concatenate([ref[...], jnp.zeros((1, 6), F32)], axis=1)
        for g in range(GROUPS):
            lanes[g, i : i + 1, :] = line[:, g * LANES : (g + 1) * LANES]
    bias_in[...] = jnp.concatenate([bin_ref[...], jnp.zeros((1, 24), F32)], axis=1)
    row = lax.broadcasted_iota(jnp.int32, (CAP, LANES), 0)
    lane = lax.broadcasted_iota(jnp.int32, (CAP, LANES), 1)
    sample = jnp.zeros((CAP, LANES), jnp.int32)
    for t in range(CAP):
        sample = jnp.where(row == t, sample_ref[t], sample)
    member[...] = (sample == lane).astype(F32)
    for g in range(GROUPS):

        def centre(r, carry):
            padded[g, pl.ds(((r + RIM) * PAD + RIM) * CAP, SIDE * CAP), :] = tiles[
                g, pl.ds(r * SIDE * CAP, SIDE * CAP), :
            ]
            return carry

        lax.fori_loop(0, SIDE, centre, 0)
    for p, (g, half) in enumerate(PIECES):
        loads[4 + p].wait()
        to_rows(gbuf, grad, g, half)
    slot = lax.broadcasted_iota(jnp.int32, (CAP, CELLS), 0)
    ocean = jnp.where(slot < count_ref[0], ocean_ref[...].astype(F32), 0.0)
    for half in range(2):
        for t in range(CAP):
            mask[pl.ds(half * 1024 + t, LANES, stride=CAP), :] = jnp.broadcast_to(
                ocean[t : t + 1, half * LANES : (half + 1) * LANES], (LANES, LANES)
            ).T
    own_conv(0, padded, conv, w, lanes)
    passed = []

    def pass_on(p):
        out_ahead[p].wait_recv()
        passed.append(start(piece(pool, 1, p), piece(pool, 2, p), partner))

    pass_on(0)
    own_conv(1, padded, conv, w, lanes)
    pass_on(1)
    win_hi[...], win_lo[...] = split(edge_zero(win_ref[...], 1000, 250))
    wout_hi[...], wout_lo[...] = split(edge_zero(wout_ref[...], 1000, 250))
    onehots(near_ref, me, spread)
    for ref in (dw, vec, hvec):
        ref[...] = jnp.zeros_like(ref)
    sums = []
    for g in range(GROUPS):
        if g == 1:
            pass_on(2)
            pass_on(3)
        for copies in (out_behind, out_partner, passed):
            arrived(copies[2 * g : 2 * g + 2])
        gather(g, near_ref, me, pool, padded)
        halo_conv(g, padded, conv, w)
        sums.append(masked_sum(g, conv, mask))

    def reduce_vector(i, vector, merge, between):
        partial[i] = vector
        copies = exchange_start(
            partial.at[i], send, recv, inner.at[i], used[0], me % INNER, zc_peers
        )
        used[0] += INNER - 1
        between()
        for copy in copies:
            copy.wait()
        partial[2 + i] = merge(inner[i])
        copies = exchange_start(
            partial.at[2 + i], send, recv, outer.at[i], used[0], xy, xy_peers
        )
        used[0] += OUTER - 1
        for copy in copies:
            copy.wait()
        return merge(outer[i])

    stats = local_stats(sums[0][0] + sums[1][0], sums[0][1], conv, mask, member[...])
    stat_ref[...] = reduce_vector(0, stats, merge_stats, sent)

    def clear_pool():
        for g in range(GROUPS):

            def zero(i, carry):
                pool[g][pl.ds(i * HALF_RIM, HALF_RIM), :] = jnp.zeros((HALF_RIM, LANES), F32)
                return carry

            lax.fori_loop(0, 2 * BACK_ROLES, zero, 0)

    first, second = dense(
        stat_ref[...], member[...], conv, tiles, grad, mask, lanes, bias_in,
        (win_hi, win_lo, wout_hi, wout_lo), tiles, gbuf, dw, vec, hvec,
    )
    theirs = pl.multiple_of((1 - core) * HALF, HALF)
    mine = pl.multiple_of(core * HALF, HALF)
    halves = start(dw.at[pl.ds(theirs, HALF), :], other, partner)
    rows = [
        jnp.sum(member[...] * jnp.sum(x, axis=1, keepdims=True), axis=0, keepdims=True)
        for x in (first, second)
    ]
    scattered = []

    def scatter_weights():
        halves.wait_recv()
        dw[pl.ds(mine, HALF), :] = dw[pl.ds(mine, HALF), :] + other[...]
        for peer in xy_peers:
            at = pl.multiple_of(core * HALF + (peer // INNER) * SLAB, SLAB)
            scattered.append(start(dw.at[pl.ds(at, SLAB), :], slots.at[xy], peer))
        slots[xy] = dw[pl.ds(pl.multiple_of(core * HALF + xy * SLAB, SLAB), SLAB), :]
        clear_pool()

    sums = reduce_vector(1, stack_rows(*rows), merge_sums, scatter_weights)
    conv_gradient(stat_ref[...], sums, member[...], conv, gbuf, mask, lanes, db)

    payload, direct, near, merged = [], [], [], []

    def part_of(ref, p):
        g, part = PIECES[p]
        return ref.at[g, pl.ds(part * HALF_RIM, HALF_RIM), :]

    def on_chip(p):
        payload.append(start(piece(pool, 2, p), part_of(pay, p), partner))
        near.append(start(piece(pool, 3, p), part_of(got.at[2], p), partner))

    def off_chip(p):
        direct.append(start(piece(pool, 0, p), part_of(got.at[0], p), ahead))
        payload[p].wait_recv()
        g, part = PIECES[p]
        at = pl.ds(RIM_ROWS + part * HALF_RIM, HALF_RIM)
        pool[g][at, :] = pool[g][at, :] + pay[g, pl.ds(part * HALF_RIM, HALF_RIM), :]
        merged.append(start(piece(pool, 1, p), part_of(got.at[1], p), behind))

    input_gradient(0, gbuf, w, gpad)
    own_gradient(0, gpad, grad, mask)
    scatter(0, gpad, spread, pool)
    on_chip(0)
    on_chip(1)
    arrived(scattered)
    slab[...] = jnp.sum(slots[...], axis=0)
    z_gathered = [start(slab, zslots.at[z], peer) for peer in z_peers]
    zslots[z] = slab[...]
    off_chip(0)
    off_chip(1)
    input_gradient(1, gbuf, w, gpad)
    own_gradient(1, gpad, grad, mask)
    scatter(1, gpad, spread, pool)
    on_chip(2)
    on_chip(3)
    off_chip(2)
    arrived(z_gathered)
    big_rows = pl.ds(pl.multiple_of(core * HALF + xy * SLAB, SLAB), SLAB)
    big[big_rows, :] = jnp.sum(zslots[...], axis=0)
    own = big.at[big_rows, :]
    xy_gathered = [start(own, own, peer) for peer in xy_peers]

    for g in range(GROUPS):
        weight_gradient(g, padded, gbuf, small)
        lines = [jnp.sum(db[g], axis=0, keepdims=True)]
        lines += [jnp.sum(vec[g, i], axis=0, keepdims=True) for i in range(3)]
        lines += [hvec[0:1, pl.ds((g * 4 + i) * LANES, LANES)] for i in range(4)]
        for i, line in enumerate(lines):
            small[g, pl.ds(49 + i, 1), :] = line
        small[g, pl.ds(57, 7), :] = jnp.zeros((7, LANES), F32)
    small_tile = lambda q: small.at[q // 8, pl.ds(pl.multiple_of((q % 8) * CAP, CAP), CAP), :]
    small_scattered = [start(small_tile(peer // INNER), sslots.at[xy], peer) for peer in xy_peers]
    sslots[xy] = small[xy // 8, pl.ds(pl.multiple_of((xy % 8) * CAP, CAP), CAP), :]
    stores = store_native(xbuf, native_out, store_sem)
    for p in range(2):
        from_rows(tiles, xbuf, *PIECES[p])
        stores[p].start()
    arrived(small_scattered)
    tile[...] = jnp.sum(sslots[...], axis=0)
    zc_gathered = [start(tile, zcslots.at[me % INNER], peer) for peer in zc_peers]
    zcslots[me % INNER] = tile[...]
    off_chip(3)
    for p in range(2, 4):
        from_rows(tiles, xbuf, *PIECES[p])
        stores[p].start()
    arrived(xy_gathered)
    own = big.at[pl.ds(mine, HALF), :]
    crossed = start(own, own, partner)
    arrived(zc_gathered)
    small_ref[xy] = jnp.sum(zcslots[...], axis=0)
    small_gathered = [start(small_ref.at[xy], small_ref.at[xy], peer) for peer in xy_peers]
    crossed.wait_recv()
    stores.append(pltpu.make_async_copy(big, big_out, store_sem.at[4]))
    stores[4].start()
    for p, (g, half) in enumerate(PIECES):
        arrived([near[p], direct[p], merged[p]])
        for first, rim, cells in rim_spans(half):
            rows = pl.ds(first * CAP, cells * CAP)
            span = pl.ds(rim * CAP, cells * CAP)
            mine_at = pl.ds(4 * RIM_ROWS + rim * CAP, cells * CAP)
            grad[g, rows, :] = (grad[g, rows, :] + pool[g][mine_at, :]) + (
                got[2, g, span, :] + (got[0, g, span, :] + got[1, g, span, :])
            )
        rows = pl.ds(half * 1024, 1024)
        stores.append(
            pltpu.make_async_copy(grad.at[g, rows, :], total_out.at[g, rows, :], store_sem.at[5 + p])
        )
        stores[-1].start()
    arrived(small_gathered)
    sent()
    for copy in stores:
        copy.wait()


def block(near, count, sample, x, g, ocean, wt, cb, gain, nbias, bout, bin_, win, wout):
    rows = (GROUPS, ROWS, LANES)
    rim = (GROUPS, RIM_ROWS, LANES)
    vector = (CAP, LANES)
    weight = pltpu.VMEM((HIDDEN_PAD, 256), BF16)
    copies = 16 + 2 * (INNER + OUTER - 2) + 1 + 15 + 16 + 3 + 15 + 15 + 7 + 1 + 15
    weight_block = pl.BlockSpec((HIDDEN_PAD, 256), lambda i: (0, 0))
    return pl.pallas_call(
        block_kernel,
        grid=(1,),
        in_specs=[SMEM_SPEC] * 3 + [ANY_SPEC] * 2 + [VMEM_SPEC] * 7 + [weight_block] * 2,
        out_specs=(ANY_SPEC,) * 3 + (VMEM_SPEC,) * 2,
        out_shape=(
            shape(2000, 256), shape(*rows), shape(512, HIDDEN_PAD), shape(16, *vector),
            shape(*vector),
        ),
        scratch_shapes=[
            buffer(*rows), buffer(*rows), buffer(*rows), buffer(*rows),
            buffer(ROWS, LANES), buffer(ROLES * RIM_ROWS, LANES), buffer(ROLES * RIM_ROWS, LANES),
            buffer(GROUPS, PAD * PAD * CAP, LANES), buffer(*rows),
            buffer(GROUPS, KSIZE * KSIZE, CAP, LANES), buffer(GROUPS, *vector),
            buffer(*vector), buffer(1, HIDDEN_PAD), weight, weight, weight, weight,
            buffer(512, HIDDEN_PAD), buffer(GROUPS, 3, *vector), buffer(1, HIDDEN_PAD),
            buffer(GROUPS, *vector), buffer(PAD * PAD * CAP, LANES),
            pltpu.VMEM((8, BACK_ROLES * LANES, LANES), BF16), buffer(*rim), buffer(3, *rim),
            buffer(HALF, HIDDEN_PAD), buffer(OUTER, SLAB, HIDDEN_PAD),
            buffer(4, SLAB, HIDDEN_PAD), buffer(SLAB, HIDDEN_PAD), buffer(512, HIDDEN_PAD),
            buffer(GROUPS, 64, LANES), buffer(*vector), buffer(OUTER, *vector),
            buffer(INNER, *vector), buffer(2, INNER, *vector), buffer(2, OUTER, *vector),
            buffer(4, *vector), semaphores(8), semaphores(9), semaphores(copies),
            semaphores(copies),
        ],
        compiler_params=params(collective_id=1, has_side_effects=True),
        name="block",
    )(near, count, sample, x, g, ocean, wt, cb, gain, nbias, bout, bin_, win, wout)


def final_kernel(
    total_ref, native_ref, big_ref, small_ref, stat_ref,
    out_ref, tiles_ref, dwin_ref, dwout_ref, dconv_ref, lines_ref, hline_ref,
    total, buf, through, big, load_sem, store_sem,
):
    loads = [
        pltpu.make_async_copy(
            total_ref.at[g, pl.ds(half * 1024, 1024), :],
            total.at[g, pl.ds(half * 1024, 1024), :],
            load_sem.at[p],
        )
        for p, (g, half) in enumerate(PIECES)
    ]
    loads.append(pltpu.make_async_copy(big_ref, big, load_sem.at[4]))
    loads.append(pltpu.make_async_copy(native_ref, through, load_sem.at[5]))
    for copy in loads:
        copy.start()
    stores = store_native(buf, tiles_ref, store_sem)
    for p, (g, half) in enumerate(PIECES):
        loads[p].wait()
        from_rows(total, buf, g, half)
        stores[p].start()
    loads[5].wait()
    stores.append(pltpu.make_async_copy(through, out_ref, store_sem.at[4]))
    stores[4].start()
    sample = lax.broadcasted_iota(jnp.int32, (1, LANES), 1) < SAMPLES
    cells = jnp.sum(jnp.where(sample, stat_ref[0:1, :], 0.0), axis=1, keepdims=True)
    share = 250.0 / cells
    loads[4].wait()
    dwin_ref[...] = big[0:256, :].T[:1000, :250] * share
    dwout_ref[...] = big[256:512, :].T[:1000, :250] * share
    flat = [
        jnp.concatenate([small_ref[g * 8 + i] for i in range(8)], axis=0) * share
        for g in range(GROUPS)
    ]
    flat = jnp.concatenate(flat, axis=1)
    dconv_ref[...] = flat[0:49, :250]
    lines_ref[...] = flat[48:56, :250]
    for g in range(GROUPS):
        for i in range(4):
            j = 53 + i
            hline_ref[0:1, pl.ds((g * 4 + i) * LANES, LANES)] = (
                flat[j : j + 1, g * LANES : (g + 1) * LANES]
            )
    for copy in stores:
        copy.wait()


def final(total, out, big, small, stat):
    return pl.pallas_call(
        final_kernel,
        in_specs=[ANY_SPEC] * 3 + [VMEM_SPEC] * 2,
        out_specs=(ANY_SPEC,) * 2 + (VMEM_SPEC,) * 5,
        out_shape=(
            shape(2000, 256), shape(2000, 256), shape(1000, 250), shape(1000, 250),
            shape(49, 250), shape(8, 250), shape(1, HIDDEN_PAD),
        ),
        scratch_shapes=[
            buffer(GROUPS, ROWS, LANES), buffer(GROUPS, ROWS, LANES), buffer(2000, 256),
            buffer(512, HIDDEN_PAD), semaphores(6), semaphores(5),
        ],
        compiler_params=params(),
        name="final",
    )(total, out, big, small, stat)


def native(x):
    return jnp.transpose(x, (1, 0, 2)).reshape(2000, CELLS)


def from_native(x):
    return jnp.transpose(x.reshape(250, CAP, CELLS), (1, 0, 2))


def local(
    tiles_in, conv_weight, conv_bias, norm_gain, norm_bias, weight_in, bias_in,
    weight_out, bias_out, grad_out, tile_counts, ocean_mask, neighbours, sample_ids,
):
    out, total, big, small, stat = block(
        neighbours, tile_counts, sample_ids, native(tiles_in), native(grad_out), ocean_mask,
        conv_weight.T, conv_bias[None], norm_gain[None], norm_bias[None], bias_out[None],
        bias_in[None], weight_in.T, weight_out,
    )
    output, grad_tiles, dwin, dwout, dconv, lines, hline = final(total, out, big, small, stat)
    return (
        from_native(output),
        from_native(grad_tiles),
        dconv.T,
        lines[1],
        lines[3],
        lines[4],
        dwin.T,
        hline[0, :1000],
        dwout,
        lines[2],
    )


def solution(mesh):
    tiles = P("tiles")
    whole = P()
    return jax.shard_map(
        local,
        mesh=mesh,
        in_specs=(tiles,) + (whole,) * 8 + (tiles,) * 5,
        out_specs=(tiles, tiles) + (whole,) * 8,
        check_vma=False,
    )
```

```python
import functools

import jax
import jax.numpy as jnp
from jax import lax
from jax.experimental import pallas as pl
from jax.experimental.pallas import tpu as pltpu
from jax.sharding import PartitionSpec as P

SIDE = 16
KSIZE = 7
RIM = 3
REACH = 2
SAMPLES = 5
CAP = 8
CELLS = SIDE * SIDE
PAD = SIDE + 2 * RIM
LANES = 128
GROUPS = 2
ROWS = CELLS * CAP
RIM_CELLS = 156
RIM_ROWS = RIM_CELLS * CAP
HIDDEN_PAD = 1024
NORM_EPSILON = 1e-05
F32 = jnp.float32
BF16 = jnp.bfloat16
MIB = 1 << 20
MESH = pl.DeviceIdType.MESH
VMEM_SPEC = pl.BlockSpec(memory_space=pltpu.VMEM)
SMEM_SPEC = pl.BlockSpec(memory_space=pltpu.SMEM)
ANY_SPEC = pl.BlockSpec(memory_space=pl.ANY)


def params(mib=62, **more):
    return pltpu.CompilerParams(vmem_limit_bytes=mib * MIB, **more)


HALF_RIM = RIM_ROWS // 2


def rim_spans(half):
    base = half * 78
    outer = 0 if half == 0 else SIDE - RIM
    inner = RIM if half == 0 else SIDE // 2
    spans = [(outer * SIDE, base, 48)]
    for i in range(5):
        spans.append(((inner + i) * SIDE, base + 48 + i * RIM, RIM))
        spans.append(((inner + i) * SIDE + SIDE - RIM, base + 63 + i * RIM, RIM))
    return spans


RIM_OF = {
    first + i: rim + i
    for half in range(2)
    for first, rim, cells in rim_spans(half)
    for i in range(cells)
}


def rim_index(r, c):
    return RIM_OF[r * SIDE + c]


def region_runs():
    spans = {-1: (0, SIDE - RIM, RIM), 0: (RIM, 0, SIDE), 1: (RIM + SIDE, 0, RIM)}
    order = [(-1, -1), (-1, 0), (-1, 1), (0, -1), (0, 1), (1, -1), (1, 0), (1, 1)]
    runs = []
    for dr, dc in order:
        dst_r, src_r, rows = spans[dr]
        dst_c, src_c, cols = spans[dc]
        found = []

        def add(cells):
            start = 0
            while start < len(cells):
                stop = start + 1
                while (
                    stop < len(cells)
                    and stop - start < 8
                    and cells[stop][0] - cells[stop - 1][0] == cells[1][0] - cells[0][0]
                    and cells[stop][1] - cells[stop - 1][1] == cells[1][1] - cells[0][1]
                ):
                    stop += 1
                step = (cells[1][0] - cells[0][0], cells[1][1] - cells[0][1])
                found.append((cells[start][0], step[0], cells[start][1], step[1], stop - start))
                start = stop

        if dr == 0:
            for j in range(cols):
                cells = [
                    ((dst_r + i) * PAD + dst_c + j, rim_index(src_r + i, src_c + j))
                    for i in range(rows)
                ]
                for low, high in ((0, RIM), (RIM, 8), (8, SIDE - RIM), (SIDE - RIM, SIDE)):
                    add(cells[low:high])
        else:
            for i in range(rows):
                add(
                    [
                        ((dst_r + i) * PAD + dst_c + j, rim_index(src_r + i, src_c + j))
                        for j in range(cols)
                    ]
                )
        runs.append(found)
    return runs


RUNS = region_runs()


ROLES = 6
PIECES = [(g, half) for g in range(GROUPS) for half in range(2)]


def piece(ref, role, p):
    g, half = PIECES[p]
    return ref[g].at[pl.ds(role * RIM_ROWS + half * HALF_RIM, HALF_RIM), :]


def halo_peers():
    me = lax.axis_index("tiles")
    total = lax.axis_size("tiles")
    sign = 2 * (me % 2) - 1
    ahead = (me + 2 * sign + total) % total
    behind = (me - 2 * sign + total) % total
    return ahead, behind, me - sign


def remote(src, dst, send, recv, peer):
    return pltpu.make_async_remote_copy(
        src_ref=src, dst_ref=dst, send_sem=send, recv_sem=recv,
        device_id=(peer,), device_id_type=MESH,
    )


def greet(peers):
    barrier = pltpu.get_barrier_semaphore()
    for peer in peers:
        pl.semaphore_signal(barrier, inc=1, device_id=(peer,), device_id_type=MESH)
    return lambda: pl.semaphore_wait(barrier, len(peers))


def load_native(x_ref, buf, sems, first=0):
    copies = []
    for g, half in PIECES:
        rows = 1024 if g == 0 else 976
        copies.append(
            pltpu.make_async_copy(
                x_ref.at[pl.ds(g * 1024, rows), pl.ds(half * LANES, LANES)],
                buf.at[half, pl.ds(g * 1024, rows), :],
                sems.at[first + len(copies)],
            )
        )
    return copies


def to_rows(buf, out, g, half):
    for t in range(CAP):
        block = buf[half, pl.ds(g * 1024 + t, LANES, stride=CAP), :]
        out[g, pl.ds(half * 1024 + t, LANES, stride=CAP), :] = block.T


def store_native(buf, out_ref, sems, first=0):
    copies = []
    for g, half in PIECES:
        rows = 1024 if g == 0 else 976
        copies.append(
            pltpu.make_async_copy(
                buf.at[half, pl.ds(g * 1024, rows), :],
                out_ref.at[pl.ds(g * 1024, rows), pl.ds(half * LANES, LANES)],
                sems.at[first + len(copies)],
            )
        )
    return copies


def from_rows(rows, buf, g, half):
    for t in range(CAP):
        block = rows[g, pl.ds(half * 1024 + t, LANES, stride=CAP), :]
        buf[half, pl.ds(g * 1024 + t, LANES, stride=CAP), :] = block.T


def lane_mask(g):
    lane = lax.broadcasted_iota(jnp.int32, (CAP, LANES), 1)
    return (lane < 250 - g * LANES).astype(F32)


def shape(*dims):
    return jax.ShapeDtypeStruct(dims, F32)


def buffer(*dims):
    return pltpu.VMEM(dims, F32)


def semaphores(count):
    return pltpu.SemaphoreType.DMA((count,))


INNER = 8
OUTER = 16


def inner_peers():
    me = lax.axis_index("tiles")
    group, place = me // INNER, me % INNER
    return [group * INNER + (place + j) % INNER for j in range(1, INNER)]


def outer_peers():
    me = lax.axis_index("tiles")
    group, place = me // INNER, me % INNER
    return [((group + j) % OUTER) * INNER + place for j in range(1, OUTER)]


def exchange_start(x, send, recv, slots, first, mine, peers):
    copies = [
        remote(x, slots.at[mine], send.at[first + j], recv.at[first + j], peer)
        for j, peer in enumerate(peers)
    ]
    for copy in copies:
        copy.start()
    slots[mine] = x[...]
    return copies


def merge_stats(parts):
    n = jnp.sum(parts[:, 0:1], axis=0)
    mean = jnp.sum(parts[:, 0:1] * parts[:, 1:2], axis=0) / jnp.maximum(n, 1.0)
    off = parts[:, 1:2] - mean[None]
    m2 = jnp.sum(parts[:, 2:3] + parts[:, 0:1] * off * off, axis=0)
    return stack_rows(n, mean, m2)


def stack_rows(*rows):
    row_id = lax.broadcasted_iota(jnp.int32, (CAP, LANES), 0)
    value = jnp.zeros((CAP, LANES), F32)
    for i, row in enumerate(rows):
        value = jnp.where(row_id == i, row, value)
    return value


def merge_sums(parts):
    return jnp.sum(parts, axis=0)


def by_tile(x):
    return x.reshape(-1, CAP, LANES)


def own_conv(g, padded, conv, w, lanes_ref):
    bias = jnp.broadcast_to(lanes_ref[g, 0:1, :], (CAP, LANES))[None]

    def row(r, carry):
        acc = jnp.broadcast_to(bias, (SIDE, CAP, LANES))
        for a in range(KSIZE):
            x = by_tile(padded[g, pl.ds((r + a) * PAD * CAP, PAD * CAP), :])
            for b in range(KSIZE):
                acc = acc + w[g, a * KSIZE + b][None] * x[b : b + SIDE]
        conv[g, pl.ds(r * SIDE * CAP, SIDE * CAP), :] = acc.reshape(-1, LANES)
        return carry

    lax.fori_loop(0, SIDE, row, 0)


def place_of(n, me):
    offset = (n // CAP - me) * (2 * (me % 2) - 1)
    role = jnp.where(offset == 2, 0, jnp.where(offset == -2, 1, 4))
    role = jnp.where(offset == 1, 2, jnp.where(offset == -1, 3, role))
    valid = n >= 0
    return jnp.where(valid, role, 5), jnp.where(valid, n % CAP, 0)


def gather(g, near_ref, me, pool, padded):
    def fill(t, carry):
        for k in range(8):
            role, slot = place_of(near_ref[t, k], me)
            q = role * RIM_ROWS + slot
            for dst, dst_step, src, src_step, length in RUNS[k]:
                padded[g, pl.ds(dst * CAP + t, length, stride=dst_step * CAP), :] = pool[g][
                    pl.ds(q + src * CAP, length, stride=src_step * CAP), :
                ]
        return carry

    lax.fori_loop(0, CAP, fill, 0)


def halo_conv(g, padded, conv, w):
    blank = jnp.zeros((RIM, CAP, LANES), F32)
    for r in [0, 1, 2, 13, 14, 15]:
        rows = pl.ds(r * SIDE * CAP, SIDE * CAP)
        acc = by_tile(conv[g, rows, :])
        for a in range(KSIZE):
            if RIM <= r + a < RIM + SIDE:
                continue
            x = by_tile(padded[g, pl.ds(((r + a) * PAD + RIM) * CAP, SIDE * CAP), :])
            x = jnp.concatenate([blank, x, blank], axis=0)
            for b in range(KSIZE):
                acc = acc + w[g, a * KSIZE + b][None] * x[b : b + SIDE]
        conv[g, rows, :] = acc.reshape(-1, LANES)

    def columns(r, carry):
        left = [jnp.zeros((CAP, LANES), F32) for _ in range(RIM)]
        right = [jnp.zeros((CAP, LANES), F32) for _ in range(RIM)]
        for a in range(KSIZE):
            first = (r + a) * PAD * CAP
            xl = by_tile(padded[g, pl.ds(first, RIM * CAP), :])
            xr = by_tile(padded[g, pl.ds(first + (RIM + SIDE) * CAP, RIM * CAP), :])
            for c in range(RIM):
                for b in range(RIM - c):
                    left[c] = left[c] + w[g, a * KSIZE + b] * xl[c + b]
                for b in range(KSIZE - 1 - c, KSIZE):
                    right[c] = right[c] + w[g, a * KSIZE + b] * xr[c + b - KSIZE + 1]
        for c in range(RIM):
            cell = pl.ds((r * SIDE + c) * CAP, CAP)
            conv[g, cell, :] = conv[g, cell, :] + left[c]
            cell = pl.ds((r * SIDE + SIDE - RIM + c) * CAP, CAP)
            conv[g, cell, :] = conv[g, cell, :] + right[c]
        return carry

    lax.fori_loop(0, SIDE, columns, 0)


def masked_sum(g, conv, mask):
    zero = jnp.zeros((CAP, LANES), F32)

    def add(r, carry):
        rows = pl.ds(r * SIDE * CAP, SIDE * CAP)
        m = by_tile(mask[rows, :])
        x = by_tile(conv[g, rows, :])
        return carry[0] + jnp.sum(x * m, axis=0), carry[1] + jnp.sum(m, axis=0)

    return lax.fori_loop(0, SIDE, add, (zero, zero))


def tile_average(sums, cells):
    total = jnp.broadcast_to(jnp.sum(sums, axis=1, keepdims=True), (CAP, LANES))
    return total / jnp.maximum(250.0 * cells, 1.0)


def local_stats(mean, cells, conv, mask, member):
    entries = 250.0 * cells
    zero = jnp.zeros((CAP, LANES), F32)
    squares = zero
    for g in range(GROUPS):

        def square(r, acc):
            rows = pl.ds(r * SIDE * CAP, SIDE * CAP)
            diff = by_tile(conv[g, rows, :]) - mean[None]
            return acc + jnp.sum(diff * diff * by_tile(mask[rows, :]), axis=0)

        squares = squares + lax.fori_loop(0, SIDE, square, zero) * lane_mask(g)
    spread = jnp.broadcast_to(jnp.sum(squares, axis=1, keepdims=True), (CAP, LANES))
    n_tile = member * entries
    n = jnp.sum(n_tile, axis=0, keepdims=True)
    centre = jnp.sum(n_tile * mean, axis=0, keepdims=True) / jnp.maximum(n, 1.0)
    off = mean - centre
    m2 = jnp.sum(member * spread + n_tile * off * off, axis=0, keepdims=True)
    return stack_rows(n, centre, m2)


def split(x):
    high = x.astype(BF16)
    return high, (x - high.astype(F32)).astype(BF16)


def dot3(a, b, lhs_dim, rhs_dim):
    dims = (((lhs_dim,), (rhs_dim,)), ((), ()))
    left = jnp.concatenate([a[0], a[1], a[0]], axis=lhs_dim)
    right = jnp.concatenate([b[0], b[0], b[1]], axis=rhs_dim)
    return lax.dot_general(left, right, dimension_numbers=dims, preferred_element_type=F32)


ERF_P = 0.3275911 * 0.7071067811865476
ERF_A = [0.5 * c for c in (1.061405429, -1.453152027, 1.421413741, -0.284496736, 0.254829592)]


def gelu_parts(x):
    size = jnp.abs(x)
    t = pl.reciprocal(1.0 + ERF_P * size)
    e = jnp.exp(-0.5 * (x * x))
    poly = ERF_A[0]
    for c in ERF_A[1:]:
        poly = poly * t + c
    tail = poly * t * e
    cdf = jnp.where(x < 0.0, tail, 1.0 - tail)
    return x * cdf, cdf + x * (e * 0.3989422804014327)


BLOCK_ROWS = 512
BLOCKS = ROWS // BLOCK_ROWS
HIDDEN_PART = 512


def tile_values(stat_row, member):
    return jnp.broadcast_to(
        jnp.sum(member * stat_row, axis=1, keepdims=True), (CAP, LANES)
    )


def norm_values(stat, member):
    n = stat[0:1]
    variance = stat[2:3] / n
    inv = lax.rsqrt(variance + NORM_EPSILON)
    sample = lax.broadcasted_iota(jnp.int32, (1, LANES), 1) < SAMPLES
    inv = jnp.where(sample, inv, 0.0)
    return tile_values(stat[1:2], member), tile_values(inv, member)


HIDDEN_CHUNKS = HIDDEN_PAD // LANES


def wide(x, parts):
    return jnp.concatenate([x] * parts, axis=1)


def flat(parts):
    return jnp.concatenate([p.reshape(-1, LANES) for p in parts], axis=1)


def block_rows(i):
    return pl.ds(pl.multiple_of(i * BLOCK_ROWS, BLOCK_ROWS), BLOCK_ROWS)


def hidden_gradient(grad, mask, wout, update_hi, update_lo, back, vec):
    def block(i, carry):
        rows = block_rows(i)
        m = by_tile(mask[rows, :])
        g_update = [by_tile(grad[g, rows, :]) * m for g in range(GROUPS)]
        for g in range(GROUPS):
            vec[g, 0] += jnp.sum(g_update[g], axis=0)
        update_hi[rows, :], update_lo[rows, :] = split(flat(g_update))
        operand = (update_hi[rows, :], update_lo[rows, :])
        for h in range(0, HIDDEN_PAD, HIDDEN_PART):
            part = slice(h, h + HIDDEN_PART)
            back[rows, part] = dot3(operand, (wout[0][part, :], wout[1][part, :]), 1, 1)
        return carry

    lax.fori_loop(0, BLOCKS, block, 0)


def centred_product(low, high, tile_mean, conv, lanes, win, ahead):
    def block(i, carry):
        rows = block_rows(i)
        operand = split(
            flat(
                [
                    (by_tile(conv[g, rows, :]) - tile_mean[None]) * lanes[g, 1:2, :][None]
                    for g in range(GROUPS)
                ]
            )
        )
        for h in range(0, HIDDEN_PAD, HIDDEN_PART):
            part = slice(h, h + HIDDEN_PART)
            value = dot3(operand, (win[0][part, :], win[1][part, :]), 1, 1)
            for c in range(HIDDEN_PART // LANES):
                ahead[h // LANES + c, rows, :] = value[:, c * LANES : (c + 1) * LANES]
        return carry

    lax.fori_loop(low, high, block, 0)


def scaled_operand(stat, member, conv, lanes, scaled_hi, scaled_lo):
    mean, inv = norm_values(stat, member)

    def block(i, carry):
        rows = block_rows(i)
        scaled_hi[rows, :], scaled_lo[rows, :] = split(
            flat(
                [
                    (by_tile(conv[g, rows, :]) - mean[None]) * inv[None] * lanes[g, 1:2, :][None]
                    + lanes[g, 2:3, :][None]
                    for g in range(GROUPS)
                ]
            )
        )
        return carry

    lax.fori_loop(0, BLOCKS, block, 0)


def dense_part(
    h, low, high, stat, member, tile_mean, lines, weights, scaled, update, ahead, back, tiles,
    gscaled, dw, hvec,
):
    win_hi, win_lo, wout_hi, wout_lo = weights
    mean, inv = norm_values(stat, member)
    part = slice(h, h + HIDDEN_PART)
    count = HIDDEN_PART // LANES
    win = (win_hi[part, :], win_lo[part, :])
    wout = (wout_hi[part, :], wout_lo[part, :])
    offset = lines[1:2, part] + wide((tile_mean - mean) * inv, count) * lines[0:1, part]
    inv = wide(inv, count)

    def block(i, carry):
        rows = block_rows(i)
        pre = jnp.concatenate([ahead[h // LANES + c, rows, :] for c in range(count)], axis=1)
        pre = pre.reshape(-1, CAP, HIDDEN_PART) * inv[None] + offset[None]
        hidden, slope = gelu_parts(pre.reshape(-1, HIDDEN_PART))
        hidden = split(hidden)
        g_pre = back[rows, part] * slope
        hvec[:, part] += jnp.sum(g_pre, axis=0, keepdims=True)
        g_pre = split(g_pre)
        dw[0:256, part] += dot3((scaled[0][rows, :], scaled[1][rows, :]), g_pre, 0, 0)
        dw[256:512, part] += dot3((update[0][rows, :], update[1][rows, :]), hidden, 0, 0)
        value = dot3(hidden, wout, 1, 0)
        g_scaled = dot3(g_pre, win, 1, 0)
        for g in range(GROUPS):
            span = slice(g * LANES, (g + 1) * LANES)
            tiles[g, rows, :] += value[:, span]
            if h == 0:
                gscaled[g, rows, :] = g_scaled[:, span]
            else:
                gscaled[g, rows, :] += g_scaled[:, span]
        return carry

    lax.fori_loop(low, high, block, 0)


def scaled_sums(stat, member, conv, gscaled, lanes, vec):
    mean, inv = norm_values(stat, member)
    zero = jnp.zeros((CAP, LANES), F32)
    first, second = zero, zero
    for g in range(GROUPS):

        def add(r, carry):
            rows = pl.ds(r * SIDE * CAP, SIDE * CAP)
            gs = by_tile(gscaled[g, rows, :])
            normed = (by_tile(conv[g, rows, :]) - mean[None]) * inv[None]
            return carry[0] + jnp.sum(gs, axis=0), carry[1] + jnp.sum(gs * normed, axis=0)

        bias_sum, gain_sum = lax.fori_loop(0, SIDE, add, (zero, zero))
        vec[g, 1] = gain_sum
        vec[g, 2] = bias_sum
        first = first + bias_sum * lanes[g, 1:2, :]
        second = second + gain_sum * lanes[g, 1:2, :]
    return first, second


def finish_output(p, tiles, mask, lanes):
    g, half = PIECES[p]

    def finish(r, carry):
        rows = pl.ds(r * SIDE * CAP, SIDE * CAP)
        tiles[g, rows, :] = mask[rows, :] * (tiles[g, rows, :] + lanes[g, 3:4, :])
        return carry

    lax.fori_loop(half * 8, half * 8 + 8, finish, 0)


def conv_gradient(stat, sums, member, conv, gscaled, mask, lanes, db):
    mean, inv = norm_values(stat, member)
    sample = lax.broadcasted_iota(jnp.int32, (1, LANES), 1) < SAMPLES
    share = jnp.where(sample, 1.0 / stat[0:1], 0.0)
    first = tile_values(sums[0:1] * share, member)
    second = tile_values(sums[1:2] * share, member)
    for g in range(GROUPS):
        gain = lanes[g, 1:2, :][None]

        def gradient(r, acc):
            rows = pl.ds(r * SIDE * CAP, SIDE * CAP)
            normed = (by_tile(conv[g, rows, :]) - mean[None]) * inv[None]
            g_normed = by_tile(gscaled[g, rows, :]) * gain
            value = (by_tile(mask[rows, :]) * inv[None]) * (
                g_normed - first[None] - normed * second[None]
            )
            gscaled[g, rows, :] = value.reshape(-1, LANES)
            return acc + jnp.sum(value, axis=0)

        db[g] = lax.fori_loop(0, SIDE, gradient, jnp.zeros((CAP, LANES), F32)) * lane_mask(g)


def input_gradient(g, gconv, w, gpad):
    def input_row(r, carry):
        low = jnp.maximum(r - (SIDE - 1), 0)
        high = jnp.minimum(r, KSIZE - 1)

        def tap(a, acc):
            x = by_tile(gconv[g, pl.ds((r - a) * SIDE * CAP, SIDE * CAP), :])
            for b in range(KSIZE):
                part = w[g, a * KSIZE + b][None] * x
                acc = acc[:b] + tuple(acc[b + i] + part[i] for i in range(SIDE)) + acc[b + SIDE :]
            return acc

        acc = lax.fori_loop(
            low, high + 1, tap, tuple(jnp.zeros((CAP, LANES), F32) for _ in range(PAD))
        )
        for i in range(PAD):
            gpad[pl.ds((r * PAD + i) * CAP, CAP), :] = acc[i]
        return carry

    lax.fori_loop(0, PAD, input_row, 0)


def own_gradient(g, gpad, grad, mask):
    def add(r, carry):
        rows = pl.ds(r * SIDE * CAP, SIDE * CAP)
        centre = gpad[pl.ds(((r + RIM) * PAD + RIM) * CAP, SIDE * CAP), :]
        grad[g, rows, :] = grad[g, rows, :] * mask[rows, :] + centre
        return carry

    lax.fori_loop(0, SIDE, add, 0)


def scatter_chunks():
    spans = {-1: (0, SIDE - RIM), 0: (RIM, 0), 1: (RIM + SIDE, 0)}
    order = [(-1, -1), (-1, 0), (-1, 1), (0, -1), (0, 1), (1, -1), (1, 0), (1, 1)]
    chunks = []
    for dr, dc in order:
        dst_r, src_r = spans[dr]
        dst_c, src_c = spans[dc]
        cols = RIM if dc else SIDE
        if dr == 0:
            groups = [range(0, 3), range(3, 8), range(8, 13), range(13, 16)]
        elif dc == 0:
            groups = [[0], [1], [2]]
        else:
            groups = [range(3)]
        chunks.append(
            [
                [
                    ((dst_r + i) * PAD + dst_c, rim_index(src_r + i, src_c), cols)
                    for i in group
                ]
                for group in groups
            ]
        )
    return chunks


CHUNKS = scatter_chunks()
CHUNK = 16
BACK_ROLES = 5


def onehots(near_ref, me, spread):
    size = (BACK_ROLES, CHUNK, CAP, LANES)
    role = lax.broadcasted_iota(jnp.int32, size, 0)
    cell = lax.broadcasted_iota(jnp.int32, size, 1)
    slot = lax.broadcasted_iota(jnp.int32, size, 2)
    lane = lax.broadcasted_iota(jnp.int32, size, 3)
    code = jnp.where(lane // CAP == cell, role * CAP + slot, -1)
    code = code.reshape(BACK_ROLES * LANES, LANES)
    lane = lax.broadcasted_iota(jnp.int32, (1, LANES), 1) % CAP
    for k in range(8):
        wanted = jnp.full((1, LANES), -2, jnp.int32)
        for t in range(CAP):
            n = near_ref[t, k]
            role, slot = place_of(n, me)
            wanted = jnp.where(lane == t, jnp.where(n >= 0, role * CAP + slot, -2), wanted)
        spread[k] = jnp.where(code == wanted, 1.0, 0.0).astype(BF16)


def scatter(g, gpad, spread, pool):
    for k in range(8):
        hot = spread[k]
        hot = jnp.concatenate([hot, hot], axis=1)
        for chunk in CHUNKS[k]:
            parts = [gpad[pl.ds(dst * CAP, cells * CAP), :] for dst, _, cells in chunk]
            used = sum(cells for _, _, cells in chunk)
            if used < CHUNK:
                parts.append(jnp.zeros(((CHUNK - used) * CAP, LANES), F32))
            value = parts[0] if len(parts) == 1 else jnp.concatenate(parts, axis=0)
            value = jnp.concatenate(split(value), axis=0)
            moved = jnp.dot(hot, value, preferred_element_type=F32)
            for role in range(BACK_ROLES):
                first = role * LANES
                for _, rim, cells in chunk:
                    rows = pl.ds(role * RIM_ROWS + rim * CAP, cells * CAP)
                    pool[g][rows, :] = pool[g][rows, :] + moved[first : first + cells * CAP]
                    first += cells * CAP


def weight_gradient(g, padded, gconv, small):
    def weight_row(a, carry):
        def one(r, acc):
            x = by_tile(padded[g, pl.ds((r + a) * PAD * CAP, PAD * CAP), :])
            y = by_tile(gconv[g, pl.ds(r * SIDE * CAP, SIDE * CAP), :])
            return tuple(acc[b] + jnp.sum(x[b : b + SIDE] * y, axis=0) for b in range(KSIZE))

        acc = lax.fori_loop(
            0, SIDE, one, tuple(jnp.zeros((CAP, LANES), F32) for _ in range(KSIZE))
        )
        for b in range(KSIZE):
            small[g, pl.ds(a * KSIZE + b, 1), :] = jnp.sum(acc[b], axis=0, keepdims=True)
        return carry

    lax.fori_loop(0, KSIZE, weight_row, 0)


HALF = 256


def block_kernel(
    near_ref, count_ref, sample_ref, x_ref, g_ref, win_ref, wout_ref, ocean_ref, wt_ref, cb_ref,
    gain_ref, nbias_ref, bout_ref, bin_ref,
    native_out, total_out, big_out, small_ref, stat_ref,
    xbuf, gbuf, tiles, grad, mask, pool0, pool1, padded, conv, w, lanes, member,
    weight_buf, win_hi, win_lo, wout_hi, wout_lo, update_hi, update_lo, scaled_hi, scaled_lo,
    back, arena, dw, vec, hvec, db, gpad, spread,
    other, slots1, sum1, slots2, sum2, zslots, big, small, tile, sslots, zcslots,
    inner, outer, partial, load_sem, store_sem, send, recv,
):
    pool = (pool0, pool1)
    me = lax.axis_index("tiles")
    core, z, x, y, xy = me % 2, (me // 2) % 4, (me // INNER) % 4, me // 32, me // INNER
    ahead, behind, partner = halo_peers()
    z_peers = [me + (((z + j) % 4) - z) * 2 for j in range(1, 4)]
    x_peers = [me + (((x + j) % 4) - x) * INNER for j in range(1, 4)]
    y_peers = [me + (((y + j) % 4) - y) * 32 for j in range(1, 4)]
    xy_peers = outer_peers()
    zc_peers = inner_peers()
    ready = greet([ahead, behind, partner] + zc_peers + xy_peers)

    used = [0]
    started = []

    def start(source, target, peer):
        i = used[0]
        used[0] += 1
        copy = remote(source, target, send.at[i], recv.at[i], peer)
        copy.start()
        started.append(copy)
        return copy

    def arrived(copies):
        for copy in copies:
            copy.wait_recv()

    def sent():
        for copy in started:
            copy.wait_send()
        started.clear()

    loads = load_native(x_ref, xbuf, load_sem) + load_native(g_ref, gbuf, load_sem, 4)
    loads.append(pltpu.make_async_copy(win_ref, weight_buf.at[0], load_sem.at[8]))
    loads.append(pltpu.make_async_copy(wout_ref, weight_buf.at[1], load_sem.at[9]))
    for copy in loads:
        copy.start()
    for half in range(2):
        xbuf[half, pl.ds(2000, 48), :] = jnp.zeros((48, LANES), F32)
        gbuf[half, pl.ds(2000, 48), :] = jnp.zeros((48, LANES), F32)
    for p, (g, half) in enumerate(PIECES):
        loads[p].wait()
        to_rows(xbuf, tiles, g, half)
        for first, rim, cells in rim_spans(half):
            pool[g][pl.ds(4 * RIM_ROWS + rim * CAP, cells * CAP), :] = tiles[
                g, pl.ds(first * CAP, cells * CAP), :
            ]
    ready()

    out_ahead, out_behind, out_partner = [], [], []
    for p in range(4):
        own = piece(pool, 4, p)
        out_ahead.append(start(own, piece(pool, 1, p), ahead))
        out_behind.append(start(own, piece(pool, 0, p), behind))
        out_partner.append(start(own, piece(pool, 3, p), partner))

    taps = wt_ref[...]
    taps = jnp.concatenate([taps, jnp.zeros((KSIZE * KSIZE, 6), F32)], axis=1)
    for g in range(GROUPS):
        for k in range(KSIZE * KSIZE):
            w[g, k] = jnp.broadcast_to(
                taps[k : k + 1, g * LANES : (g + 1) * LANES], (CAP, LANES)
            )
    for g in range(GROUPS):
        pool[g][pl.ds(5 * RIM_ROWS, RIM_ROWS), :] = jnp.zeros((RIM_ROWS, LANES), F32)

        def clear(i, carry):
            padded[g, pl.ds(i * PAD * CAP, PAD * CAP), :] = jnp.zeros((PAD * CAP, LANES), F32)
            return carry

        lax.fori_loop(0, PAD, clear, 0)

        def centre(r, carry):
            padded[g, pl.ds(((r + RIM) * PAD + RIM) * CAP, SIDE * CAP), :] = tiles[
                g, pl.ds(r * SIDE * CAP, SIDE * CAP), :
            ]
            return carry

        lax.fori_loop(0, SIDE, centre, 0)
    for i, ref in enumerate((cb_ref, gain_ref, nbias_ref, bout_ref)):
        line = jnp.concatenate([ref[...], jnp.zeros((1, 6), F32)], axis=1)
        for g in range(GROUPS):
            lanes[g, i : i + 1, :] = line[:, g * LANES : (g + 1) * LANES]
    row = lax.broadcasted_iota(jnp.int32, (CAP, LANES), 0)
    lane = lax.broadcasted_iota(jnp.int32, (CAP, LANES), 1)
    sample = jnp.zeros((CAP, LANES), jnp.int32)
    for t in range(CAP):
        sample = jnp.where(row == t, sample_ref[t], sample)
    member[...] = (sample == lane).astype(F32)
    for ref in (dw, vec, hvec):
        ref[...] = jnp.zeros_like(ref)
    passed = []

    def pass_on(p):
        out_ahead[p].wait_recv()
        passed.append(start(piece(pool, 1, p), piece(pool, 2, p), partner))

    own_conv(0, padded, conv, w, lanes)
    pass_on(0)
    own_conv(1, padded, conv, w, lanes)
    pass_on(1)
    for p, (g, half) in enumerate(PIECES):
        loads[4 + p].wait()
        to_rows(gbuf, grad, g, half)
    slot = lax.broadcasted_iota(jnp.int32, (CAP, CELLS), 0)
    ocean = jnp.where(slot < count_ref[0], ocean_ref[...].astype(F32), 0.0)
    for half in range(2):
        for t in range(CAP):
            mask[pl.ds(half * 1024 + t, LANES, stride=CAP), :] = jnp.broadcast_to(
                ocean[t : t + 1, half * LANES : (half + 1) * LANES], (LANES, LANES)
            ).T
    for i, (high, low) in enumerate(((win_hi, win_lo), (wout_hi, wout_lo))):
        loads[8 + i].wait()
        value = jnp.concatenate([weight_buf[i], jnp.zeros((1000, 6), F32)], axis=1)
        value = jnp.concatenate([value, jnp.zeros((24, 256), F32)], axis=0)
        high[...], low[...] = split(value)
    win, wout = (win_hi, win_lo), (wout_hi, wout_lo)
    scaled, update = (scaled_hi, scaled_lo), (update_hi, update_lo)
    hidden_gradient(grad, mask, wout, update_hi, update_lo, back, vec)
    ends = jnp.concatenate(
        [flat([lanes[g, 1:3, :] for g in range(GROUPS)]), jnp.zeros((14, 256), F32)], axis=0
    )
    lines = dot3(split(ends), (win_hi[...], win_lo[...]), 1, 1)
    bias_in = jnp.concatenate([bin_ref[...], jnp.zeros((1, 24), F32)], axis=1)
    lines = jnp.concatenate([lines[0:1], lines[1:2] + bias_in], axis=0)
    onehots(near_ref, me, spread)
    sums = []
    for g in range(GROUPS):
        if g == 1:
            pass_on(2)
            pass_on(3)
        for copies in (out_behind, out_partner, passed):
            arrived(copies[2 * g : 2 * g + 2])
        gather(g, near_ref, me, pool, padded)
        halo_conv(g, padded, conv, w)
        sums.append(masked_sum(g, conv, mask))

    def reduce_vector(i, vector, merge, between, later):
        partial[i] = vector
        copies = exchange_start(
            partial.at[i], send, recv, inner.at[i], used[0], me % INNER, zc_peers
        )
        used[0] += INNER - 1
        between()
        for copy in copies:
            copy.wait()
        partial[2 + i] = merge(inner[i])
        copies = exchange_start(
            partial.at[2 + i], send, recv, outer.at[i], used[0], xy, xy_peers
        )
        used[0] += OUTER - 1
        later()
        for copy in copies:
            copy.wait()
        return merge(outer[i])

    tile_mean = tile_average(sums[0][0] + sums[1][0], sums[0][1])
    stats = local_stats(tile_mean, sums[0][1], conv, mask, member[...])
    product = lambda low, high: centred_product(low, high, tile_mean, conv, lanes, win, arena)

    def first_blocks():
        product(0, BLOCKS // 2)
        sent()

    stat = reduce_vector(0, stats, merge_stats, first_blocks, lambda: product(BLOCKS // 2, BLOCKS))
    stat_ref[...] = stat

    mine = pl.multiple_of(core * HALF, HALF)
    theirs = pl.multiple_of((1 - core) * HALF, HALF)
    orders = [((y, y_peers, 32), (x, x_peers, INNER)), ((x, x_peers, INNER), (y, y_peers, 32))]

    def at(q, i, j, rows):
        (first, _, _), (second, _, _) = orders[q]
        i = first if i is None else i
        first_row = core * HALF + q * 128 + i * 32 + (0 if j is None else j * 8)
        return pl.ds(pl.multiple_of(first_row, 8), rows)

    def weight_sum(h):
        k = h // HIDDEN_PART
        part = pl.ds(h, HIDDEN_PART)
        halves = start(dw.at[pl.ds(theirs, HALF), part], other.at[k], partner)
        yield
        halves.wait_recv()
        dw[pl.ds(mine, HALF), part] = dw[pl.ds(mine, HALF), part] + other[k]
        yield
        copies = []
        for q, ((i, peers, stride), _) in enumerate(orders):
            for peer in peers:
                rows = at(q, (peer // stride) % 4, None, 32)
                copies.append(start(dw.at[rows, part], slots1.at[k, q, i], peer))
            slots1[k, q, i] = dw[at(q, None, None, 32), part]
        yield
        arrived(copies)
        copies = []
        for q, (_, (j, peers, stride)) in enumerate(orders):
            sum1[k, q] = jnp.sum(slots1[k, q], axis=0)
            for peer in peers:
                rows = pl.ds(pl.multiple_of(((peer // stride) % 4) * 8, 8), 8)
                copies.append(start(sum1.at[k, q, rows, :], slots2.at[k, q, j], peer))
            slots2[k, q, j] = sum1[k, q, pl.ds(pl.multiple_of(j * 8, 8), 8), :]
        yield
        arrived(copies)
        for q in range(2):
            sum2[k, q] = jnp.sum(slots2[k, q], axis=0)
        copies = [start(sum2.at[k], zslots.at[k, z], peer) for peer in z_peers]
        zslots[k, z] = sum2[k]
        yield
        arrived(copies)
        copies = []
        for q, (_, (j, peers, _)) in enumerate(orders):
            rows = at(q, None, j, 8)
            big[rows, part] = zslots[k, 0, q] + zslots[k, 1, q] + zslots[k, 2, q] + zslots[k, 3, q]
            copies += [start(big.at[rows, part], big.at[rows, part], peer) for peer in peers]
        yield
        arrived(copies)
        copies = []
        for q, ((_, peers, _), _) in enumerate(orders):
            rows = at(q, None, None, 32)
            copies += [start(big.at[rows, part], big.at[rows, part], peer) for peer in peers]
        yield
        arrived(copies)
        own = big.at[pl.ds(mine, HALF), part]
        crossed = start(own, own, partner)
        yield
        crossed.wait_recv()
        yield

    scaled_operand(stat, member[...], conv, lanes, scaled_hi, scaled_lo)

    def projections(h, low, high):
        dense_part(
            h, low, high, stat, member[...], tile_mean, lines, (win_hi, win_lo, wout_hi, wout_lo),
            scaled, update, arena, back, tiles, gbuf, dw, hvec,
        )

    projections(0, 0, BLOCKS)
    early = weight_sum(0)
    next(early)
    projections(HIDDEN_PART, 0, BLOCKS // 2)
    next(early)
    next(early)
    projections(HIDDEN_PART, BLOCKS // 2, BLOCKS)
    next(early)
    late = weight_sum(HIDDEN_PART)
    next(late)
    first, second = scaled_sums(stat, member[...], conv, gbuf, lanes, vec)
    rows = [
        jnp.sum(member[...] * jnp.sum(value, axis=1, keepdims=True), axis=0, keepdims=True)
        for value in (first, second)
    ]

    def clear_pool():
        for g in range(GROUPS):

            def zero(i, carry):
                pool[g][pl.ds(i * HALF_RIM, HALF_RIM), :] = jnp.zeros((HALF_RIM, LANES), F32)
                return carry

            lax.fori_loop(0, 2 * BACK_ROLES, zero, 0)

    def before_outer():
        next(late)
        next(early)

    def after_outer():
        next(late)
        clear_pool()
        next(early)

    sums = reduce_vector(1, stack_rows(*rows), merge_sums, before_outer, after_outer)
    conv_gradient(stat, sums, member[...], conv, gbuf, mask, lanes, db)
    next(late)
    next(early)

    payload, direct, near, merged = [], [], [], []

    def pay(p):
        g, part = PIECES[p]
        return arena.at[g, pl.ds(part * HALF_RIM, HALF_RIM), :]

    def got(i, p):
        g, part = PIECES[p]
        return arena.at[2 + 2 * i + g, pl.ds(part * HALF_RIM, HALF_RIM), :]

    def on_chip(p):
        payload.append(start(piece(pool, 2, p), pay(p), partner))
        near.append(start(piece(pool, 3, p), got(2, p), partner))

    def off_chip(p):
        direct.append(start(piece(pool, 0, p), got(0, p), ahead))
        payload[p].wait_recv()
        g, part = PIECES[p]
        rows = pl.ds(RIM_ROWS + part * HALF_RIM, HALF_RIM)
        pool[g][rows, :] = pool[g][rows, :] + arena[g, pl.ds(part * HALF_RIM, HALF_RIM), :]
        merged.append(start(piece(pool, 1, p), got(1, p), behind))

    input_gradient(0, gbuf, w, gpad)
    next(late)
    next(early)
    own_gradient(0, gpad, grad, mask)
    scatter(0, gpad, spread, pool)
    on_chip(0)
    on_chip(1)
    next(late)
    off_chip(0)
    off_chip(1)
    input_gradient(1, gbuf, w, gpad)
    next(late)
    next(early)
    own_gradient(1, gpad, grad, mask)
    scatter(1, gpad, spread, pool)
    on_chip(2)
    on_chip(3)
    off_chip(2)

    for g in range(GROUPS):
        weight_gradient(g, padded, gbuf, small)
        lines = [jnp.sum(db[g], axis=0, keepdims=True)]
        lines += [jnp.sum(vec[g, i], axis=0, keepdims=True) for i in range(3)]
        lines += [hvec[0:1, pl.ds((g * 4 + i) * LANES, LANES)] for i in range(4)]
        for i, line in enumerate(lines):
            small[g, pl.ds(49 + i, 1), :] = line
        small[g, pl.ds(57, 7), :] = jnp.zeros((7, LANES), F32)
    small_tile = lambda q: small.at[q // 8, pl.ds(pl.multiple_of((q % 8) * CAP, CAP), CAP), :]
    small_scattered = [start(small_tile(peer // INNER), sslots.at[xy], peer) for peer in xy_peers]
    sslots[xy] = small[xy // 8, pl.ds(pl.multiple_of((xy % 8) * CAP, CAP), CAP), :]
    stores = store_native(xbuf, native_out, store_sem)
    for p in range(2):
        finish_output(p, tiles, mask, lanes)
        from_rows(tiles, xbuf, *PIECES[p])
        stores[p].start()
    arrived(small_scattered)
    tile[...] = jnp.sum(sslots[...], axis=0)
    zc_gathered = [start(tile, zcslots.at[me % INNER], peer) for peer in zc_peers]
    zcslots[me % INNER] = tile[...]
    off_chip(3)
    next(late)
    for p in range(2, 4):
        finish_output(p, tiles, mask, lanes)
        from_rows(tiles, xbuf, *PIECES[p])
        stores[p].start()
    arrived(zc_gathered)
    small_ref[xy] = jnp.sum(zcslots[...], axis=0)
    small_gathered = [start(small_ref.at[xy], small_ref.at[xy], peer) for peer in xy_peers]
    next(late)
    stores.append(pltpu.make_async_copy(big, big_out, store_sem.at[4]))
    stores[4].start()
    for p, (g, half) in enumerate(PIECES):
        arrived([near[p], direct[p], merged[p]])
        for first, rim, cells in rim_spans(half):
            rows = pl.ds(first * CAP, cells * CAP)
            span = pl.ds(rim * CAP, cells * CAP)
            mine_at = pl.ds(4 * RIM_ROWS + rim * CAP, cells * CAP)
            grad[g, rows, :] = (grad[g, rows, :] + pool[g][mine_at, :]) + (
                arena[6 + g, span, :] + (arena[2 + g, span, :] + arena[4 + g, span, :])
            )
        rows = pl.ds(half * 1024, 1024)
        stores.append(
            pltpu.make_async_copy(grad.at[g, rows, :], total_out.at[g, rows, :], store_sem.at[5 + p])
        )
        stores[-1].start()
    arrived(small_gathered)
    sent()
    for copy in stores:
        copy.wait()


def block(near, count, sample, x, g, win, wout, ocean, wt, cb, gain, nbias, bout, bin_):
    rows = (GROUPS, ROWS, LANES)
    vector = (CAP, LANES)
    weight = pltpu.VMEM((HIDDEN_PAD, 256), BF16)
    operand = pltpu.VMEM((ROWS, 256), BF16)
    copies = 16 + 2 * (INNER + OUTER - 2) + 2 * 29 + 16 + 15 + 7 + 15
    return pl.pallas_call(
        block_kernel,
        in_specs=[SMEM_SPEC] * 3 + [ANY_SPEC] * 4 + [VMEM_SPEC] * 7,
        out_specs=(ANY_SPEC,) * 3 + (VMEM_SPEC,) * 2,
        out_shape=(
            shape(2000, 256), shape(*rows), shape(512, HIDDEN_PAD), shape(16, *vector),
            shape(*vector),
        ),
        scratch_shapes=[
            buffer(*rows), buffer(*rows), buffer(*rows), buffer(*rows),
            buffer(ROWS, LANES), buffer(ROLES * RIM_ROWS, LANES), buffer(ROLES * RIM_ROWS, LANES),
            buffer(GROUPS, PAD * PAD * CAP, LANES), buffer(*rows),
            buffer(GROUPS, KSIZE * KSIZE, CAP, LANES), buffer(GROUPS, *vector),
            buffer(*vector), buffer(2, 1000, 250), weight, weight, weight, weight,
            operand, operand, operand, operand,
            buffer(ROWS, HIDDEN_PAD), buffer(HIDDEN_CHUNKS, ROWS, LANES),
            buffer(512, HIDDEN_PAD), buffer(GROUPS, 3, *vector), buffer(1, HIDDEN_PAD),
            buffer(GROUPS, *vector), buffer(PAD * PAD * CAP, LANES),
            pltpu.VMEM((8, BACK_ROLES * LANES, LANES), BF16),
            buffer(2, HALF, HIDDEN_PART), buffer(2, 2, 4, 32, HIDDEN_PART),
            buffer(2, 2, 32, HIDDEN_PART), buffer(2, 2, 4, 8, HIDDEN_PART),
            buffer(2, 2, 8, HIDDEN_PART), buffer(2, 4, 2, 8, HIDDEN_PART),
            buffer(512, HIDDEN_PAD),
            buffer(GROUPS, 64, LANES), buffer(*vector), buffer(OUTER, *vector),
            buffer(INNER, *vector), buffer(2, INNER, *vector), buffer(2, OUTER, *vector),
            buffer(4, *vector), semaphores(10), semaphores(9), semaphores(copies),
            semaphores(copies),
        ],
        compiler_params=params(collective_id=1, has_side_effects=True),
        name="block",
    )(near, count, sample, x, g, win, wout, ocean, wt, cb, gain, nbias, bout, bin_)


def final_kernel(
    total_ref, native_ref, big_ref, small_ref, stat_ref,
    out_ref, tiles_ref, dwin_ref, dwout_ref, dconv_ref, lines_ref, hline_ref,
    total, buf, through, big, load_sem, store_sem,
):
    loads = [
        pltpu.make_async_copy(
            total_ref.at[g, pl.ds(half * 1024, 1024), :],
            total.at[g, pl.ds(half * 1024, 1024), :],
            load_sem.at[p],
        )
        for p, (g, half) in enumerate(PIECES)
    ]
    loads.append(pltpu.make_async_copy(big_ref, big, load_sem.at[4]))
    loads.append(pltpu.make_async_copy(native_ref, through, load_sem.at[5]))
    for copy in loads:
        copy.start()
    stores = store_native(buf, tiles_ref, store_sem)
    for p, (g, half) in enumerate(PIECES):
        loads[p].wait()
        from_rows(total, buf, g, half)
        stores[p].start()
    loads[5].wait()
    stores.append(pltpu.make_async_copy(through, out_ref, store_sem.at[4]))
    stores[4].start()
    sample = lax.broadcasted_iota(jnp.int32, (1, LANES), 1) < SAMPLES
    cells = jnp.sum(jnp.where(sample, stat_ref[0:1, :], 0.0), axis=1, keepdims=True)
    share = 250.0 / cells
    loads[4].wait()
    dwin_ref[...] = big[0:256, :].T[:1000, :250] * share
    dwout_ref[...] = big[256:512, :].T[:1000, :250] * share
    flat = [
        jnp.concatenate([small_ref[g * 8 + i] for i in range(8)], axis=0) * share
        for g in range(GROUPS)
    ]
    flat = jnp.concatenate(flat, axis=1)
    dconv_ref[...] = flat[0:49, :250]
    lines_ref[...] = flat[48:56, :250]
    for g in range(GROUPS):
        for i in range(4):
            j = 53 + i
            hline_ref[0:1, pl.ds((g * 4 + i) * LANES, LANES)] = (
                flat[j : j + 1, g * LANES : (g + 1) * LANES]
            )
    for copy in stores:
        copy.wait()


def final(total, out, big, small, stat):
    return pl.pallas_call(
        final_kernel,
        in_specs=[ANY_SPEC] * 3 + [VMEM_SPEC] * 2,
        out_specs=(ANY_SPEC,) * 2 + (VMEM_SPEC,) * 5,
        out_shape=(
            shape(2000, 256), shape(2000, 256), shape(1000, 250), shape(1000, 250),
            shape(49, 250), shape(8, 250), shape(1, HIDDEN_PAD),
        ),
        scratch_shapes=[
            buffer(GROUPS, ROWS, LANES), buffer(GROUPS, ROWS, LANES), buffer(2000, 256),
            buffer(512, HIDDEN_PAD), semaphores(6), semaphores(5),
        ],
        compiler_params=params(),
        name="final",
    )(total, out, big, small, stat)


def native(x):
    return jnp.transpose(x, (1, 0, 2)).reshape(2000, CELLS)


def from_native(x):
    return jnp.transpose(x.reshape(250, CAP, CELLS), (1, 0, 2))


def local(
    tiles_in, conv_weight, conv_bias, norm_gain, norm_bias, weight_in, bias_in,
    weight_out, bias_out, grad_out, tile_counts, ocean_mask, neighbours, sample_ids,
):
    out, total, big, small, stat = block(
        neighbours, tile_counts, sample_ids, native(tiles_in), native(grad_out), weight_in.T,
        weight_out, ocean_mask, conv_weight.T, conv_bias[None], norm_gain[None], norm_bias[None],
        bias_out[None], bias_in[None],
    )
    output, grad_tiles, dwin, dwout, dconv, lines, hline = final(total, out, big, small, stat)
    return (
        from_native(output),
        from_native(grad_tiles),
        dconv.T,
        lines[1],
        lines[3],
        lines[4],
        dwin.T,
        hline[0, :1000],
        dwout,
        lines[2],
    )


def solution(mesh):
    tiles = P("tiles")
    whole = P()
    return jax.shard_map(
        local,
        mesh=mesh,
        in_specs=(tiles,) + (whole,) * 8 + (tiles,) * 5,
        out_specs=(tiles, tiles) + (whole,) * 8,
        check_vma=False,
    )
```

```python
import functools

import jax
import jax.numpy as jnp
from jax import lax
from jax.experimental import pallas as pl
from jax.experimental.pallas import tpu as pltpu
from jax.sharding import PartitionSpec as P

SIDE = 16
KSIZE = 7
RIM = 3
REACH = 2
SAMPLES = 5
CAP = 8
CELLS = SIDE * SIDE
PAD = SIDE + 2 * RIM
LANES = 128
GROUPS = 2
ROWS = CELLS * CAP
RIM_CELLS = 156
RIM_ROWS = RIM_CELLS * CAP
HIDDEN_PAD = 1024
NORM_EPSILON = 1e-05
F32 = jnp.float32
BF16 = jnp.bfloat16
MIB = 1 << 20
MESH = pl.DeviceIdType.MESH
VMEM_SPEC = pl.BlockSpec(memory_space=pltpu.VMEM)
SMEM_SPEC = pl.BlockSpec(memory_space=pltpu.SMEM)
ANY_SPEC = pl.BlockSpec(memory_space=pl.ANY)


def params(mib=62, **more):
    return pltpu.CompilerParams(vmem_limit_bytes=mib * MIB, **more)


HALF_RIM = RIM_ROWS // 2


def rim_spans(half):
    base = half * 78
    outer = 0 if half == 0 else SIDE - RIM
    inner = RIM if half == 0 else SIDE // 2
    spans = [(outer * SIDE, base, 48)]
    for i in range(5):
        spans.append(((inner + i) * SIDE, base + 48 + i * RIM, RIM))
        spans.append(((inner + i) * SIDE + SIDE - RIM, base + 63 + i * RIM, RIM))
    return spans


RIM_OF = {
    first + i: rim + i
    for half in range(2)
    for first, rim, cells in rim_spans(half)
    for i in range(cells)
}


def rim_index(r, c):
    return RIM_OF[r * SIDE + c]


def region_runs():
    spans = {-1: (0, SIDE - RIM, RIM), 0: (RIM, 0, SIDE), 1: (RIM + SIDE, 0, RIM)}
    order = [(-1, -1), (-1, 0), (-1, 1), (0, -1), (0, 1), (1, -1), (1, 0), (1, 1)]
    runs = []
    for dr, dc in order:
        dst_r, src_r, rows = spans[dr]
        dst_c, src_c, cols = spans[dc]
        found = []

        def add(cells):
            start = 0
            while start < len(cells):
                stop = start + 1
                while (
                    stop < len(cells)
                    and stop - start < 8
                    and cells[stop][0] - cells[stop - 1][0] == cells[1][0] - cells[0][0]
                    and cells[stop][1] - cells[stop - 1][1] == cells[1][1] - cells[0][1]
                ):
                    stop += 1
                step = (cells[1][0] - cells[0][0], cells[1][1] - cells[0][1])
                found.append((cells[start][0], step[0], cells[start][1], step[1], stop - start))
                start = stop

        if dr == 0:
            for j in range(cols):
                cells = [
                    ((dst_r + i) * PAD + dst_c + j, rim_index(src_r + i, src_c + j))
                    for i in range(rows)
                ]
                for low, high in ((0, RIM), (RIM, 8), (8, SIDE - RIM), (SIDE - RIM, SIDE)):
                    add(cells[low:high])
        else:
            for i in range(rows):
                add(
                    [
                        ((dst_r + i) * PAD + dst_c + j, rim_index(src_r + i, src_c + j))
                        for j in range(cols)
                    ]
                )
        runs.append(found)
    return runs


RUNS = region_runs()


ROLES = 6
PIECES = [(g, half) for g in range(GROUPS) for half in range(2)]


def piece(ref, role, p):
    g, half = PIECES[p]
    return ref[g].at[pl.ds(role * RIM_ROWS + half * HALF_RIM, HALF_RIM), :]


def halo_peers():
    me = lax.axis_index("tiles")
    total = lax.axis_size("tiles")
    sign = 2 * (me % 2) - 1
    ahead = (me + 2 * sign + total) % total
    behind = (me - 2 * sign + total) % total
    return ahead, behind, me - sign


def remote(src, dst, send, recv, peer):
    return pltpu.make_async_remote_copy(
        src_ref=src, dst_ref=dst, send_sem=send, recv_sem=recv,
        device_id=(peer,), device_id_type=MESH,
    )


def greet(peers):
    barrier = pltpu.get_barrier_semaphore()
    for peer in peers:
        pl.semaphore_signal(barrier, inc=1, device_id=(peer,), device_id_type=MESH)
    return lambda: pl.semaphore_wait(barrier, len(peers))


def load_native(x_ref, buf, sems, first=0):
    copies = []
    for g, half in PIECES:
        rows = 1024 if g == 0 else 976
        copies.append(
            pltpu.make_async_copy(
                x_ref.at[pl.ds(g * 1024, rows), pl.ds(half * LANES, LANES)],
                buf.at[half, pl.ds(g * 1024, rows), :],
                sems.at[first + len(copies)],
            )
        )
    return copies


def to_rows(buf, out, g, half):
    for t in range(CAP):
        block = buf[half, pl.ds(g * 1024 + t, LANES, stride=CAP), :]
        out[g, pl.ds(half * 1024 + t, LANES, stride=CAP), :] = block.T


def store_native(buf, out_ref, sems, first=0):
    copies = []
    for g, half in PIECES:
        rows = 1024 if g == 0 else 976
        copies.append(
            pltpu.make_async_copy(
                buf.at[half, pl.ds(g * 1024, rows), :],
                out_ref.at[pl.ds(g * 1024, rows), pl.ds(half * LANES, LANES)],
                sems.at[first + len(copies)],
            )
        )
    return copies


def from_rows(rows, buf, g, half):
    for t in range(CAP):
        block = rows[g, pl.ds(half * 1024 + t, LANES, stride=CAP), :]
        buf[half, pl.ds(g * 1024 + t, LANES, stride=CAP), :] = block.T


def lane_mask(g):
    lane = lax.broadcasted_iota(jnp.int32, (CAP, LANES), 1)
    return (lane < 250 - g * LANES).astype(F32)


def shape(*dims):
    return jax.ShapeDtypeStruct(dims, F32)


def buffer(*dims):
    return pltpu.VMEM(dims, F32)


def semaphores(count):
    return pltpu.SemaphoreType.DMA((count,))


INNER = 8
OUTER = 16


def inner_peers():
    me = lax.axis_index("tiles")
    group, place = me // INNER, me % INNER
    return [group * INNER + (place + j) % INNER for j in range(1, INNER)]


def outer_peers():
    me = lax.axis_index("tiles")
    group, place = me // INNER, me % INNER
    return [((group + j) % OUTER) * INNER + place for j in range(1, OUTER)]


def exchange_start(x, send, recv, slots, first, mine, peers):
    copies = [
        remote(x, slots.at[mine], send.at[first + j], recv.at[first + j], peer)
        for j, peer in enumerate(peers)
    ]
    for copy in copies:
        copy.start()
    slots[mine] = x[...]
    return copies


def merge_stats(parts):
    n = jnp.sum(parts[:, 0:1], axis=0)
    mean = jnp.sum(parts[:, 0:1] * parts[:, 1:2], axis=0) / jnp.maximum(n, 1.0)
    off = parts[:, 1:2] - mean[None]
    m2 = jnp.sum(parts[:, 2:3] + parts[:, 0:1] * off * off, axis=0)
    return stack_rows(n, mean, m2)


def stack_rows(*rows):
    row_id = lax.broadcasted_iota(jnp.int32, (CAP, LANES), 0)
    value = jnp.zeros((CAP, LANES), F32)
    for i, row in enumerate(rows):
        value = jnp.where(row_id == i, row, value)
    return value


def merge_sums(parts):
    return jnp.sum(parts, axis=0)


def by_tile(x):
    return x.reshape(-1, CAP, LANES)


def own_conv(g, padded, conv, w, lanes_ref):
    bias = jnp.broadcast_to(lanes_ref[g, 0:1, :], (CAP, LANES))[None]

    def row(r, carry):
        acc = jnp.broadcast_to(bias, (SIDE, CAP, LANES))
        for a in range(KSIZE):
            x = by_tile(padded[g, pl.ds((r + a) * PAD * CAP, PAD * CAP), :])
            for b in range(KSIZE):
                acc = acc + w[g, a * KSIZE + b][None] * x[b : b + SIDE]
        conv[g, pl.ds(r * SIDE * CAP, SIDE * CAP), :] = acc.reshape(-1, LANES)
        return carry

    lax.fori_loop(0, SIDE, row, 0)


def place_of(n, me):
    offset = (n // CAP - me) * (2 * (me % 2) - 1)
    role = jnp.where(offset == 2, 0, jnp.where(offset == -2, 1, 4))
    role = jnp.where(offset == 1, 2, jnp.where(offset == -1, 3, role))
    valid = n >= 0
    return jnp.where(valid, role, 5), jnp.where(valid, n % CAP, 0)


def gather(g, near_ref, me, pool, padded):
    def fill(t, carry):
        for k in range(8):
            role, slot = place_of(near_ref[t, k], me)
            q = role * RIM_ROWS + slot
            for dst, dst_step, src, src_step, length in RUNS[k]:
                padded[g, pl.ds(dst * CAP + t, length, stride=dst_step * CAP), :] = pool[g][
                    pl.ds(q + src * CAP, length, stride=src_step * CAP), :
                ]
        return carry

    lax.fori_loop(0, CAP, fill, 0)


def halo_conv(g, padded, conv, w):
    blank = jnp.zeros((RIM, CAP, LANES), F32)
    for r in [0, 1, 2, 13, 14, 15]:
        rows = pl.ds(r * SIDE * CAP, SIDE * CAP)
        acc = by_tile(conv[g, rows, :])
        for a in range(KSIZE):
            if RIM <= r + a < RIM + SIDE:
                continue
            x = by_tile(padded[g, pl.ds(((r + a) * PAD + RIM) * CAP, SIDE * CAP), :])
            x = jnp.concatenate([blank, x, blank], axis=0)
            for b in range(KSIZE):
                acc = acc + w[g, a * KSIZE + b][None] * x[b : b + SIDE]
        conv[g, rows, :] = acc.reshape(-1, LANES)

    def columns(r, carry):
        left = [jnp.zeros((CAP, LANES), F32) for _ in range(RIM)]
        right = [jnp.zeros((CAP, LANES), F32) for _ in range(RIM)]
        for a in range(KSIZE):
            first = (r + a) * PAD * CAP
            xl = by_tile(padded[g, pl.ds(first, RIM * CAP), :])
            xr = by_tile(padded[g, pl.ds(first + (RIM + SIDE) * CAP, RIM * CAP), :])
            for c in range(RIM):
                for b in range(RIM - c):
                    left[c] = left[c] + w[g, a * KSIZE + b] * xl[c + b]
                for b in range(KSIZE - 1 - c, KSIZE):
                    right[c] = right[c] + w[g, a * KSIZE + b] * xr[c + b - KSIZE + 1]
        for c in range(RIM):
            cell = pl.ds((r * SIDE + c) * CAP, CAP)
            conv[g, cell, :] = conv[g, cell, :] + left[c]
            cell = pl.ds((r * SIDE + SIDE - RIM + c) * CAP, CAP)
            conv[g, cell, :] = conv[g, cell, :] + right[c]
        return carry

    lax.fori_loop(0, SIDE, columns, 0)


def masked_sum(g, conv, mask):
    zero = jnp.zeros((CAP, LANES), F32)

    def add(r, carry):
        rows = pl.ds(r * SIDE * CAP, SIDE * CAP)
        m = by_tile(mask[rows, :])
        x = by_tile(conv[g, rows, :])
        return carry[0] + jnp.sum(x * m, axis=0), carry[1] + jnp.sum(m, axis=0)

    return lax.fori_loop(0, SIDE, add, (zero, zero))


def tile_average(sums, cells):
    total = jnp.broadcast_to(jnp.sum(sums, axis=1, keepdims=True), (CAP, LANES))
    return total / jnp.maximum(250.0 * cells, 1.0)


def local_stats(mean, cells, conv, mask, member):
    entries = 250.0 * cells
    zero = jnp.zeros((CAP, LANES), F32)
    squares = zero
    for g in range(GROUPS):

        def square(r, acc):
            rows = pl.ds(r * SIDE * CAP, SIDE * CAP)
            diff = by_tile(conv[g, rows, :]) - mean[None]
            return acc + jnp.sum(diff * diff * by_tile(mask[rows, :]), axis=0)

        squares = squares + lax.fori_loop(0, SIDE, square, zero) * lane_mask(g)
    spread = jnp.broadcast_to(jnp.sum(squares, axis=1, keepdims=True), (CAP, LANES))
    n_tile = member * entries
    n = jnp.sum(n_tile, axis=0, keepdims=True)
    centre = jnp.sum(n_tile * mean, axis=0, keepdims=True) / jnp.maximum(n, 1.0)
    off = mean - centre
    m2 = jnp.sum(member * spread + n_tile * off * off, axis=0, keepdims=True)
    return stack_rows(n, centre, m2)


def split(x):
    high = x.astype(BF16)
    return high, (x - high.astype(F32)).astype(BF16)


def dot3(a, b, lhs_dim, rhs_dim):
    dims = (((lhs_dim,), (rhs_dim,)), ((), ()))
    left = jnp.concatenate([a[0], a[1], a[0]], axis=lhs_dim)
    right = jnp.concatenate([b[0], b[0], b[1]], axis=rhs_dim)
    return lax.dot_general(left, right, dimension_numbers=dims, preferred_element_type=F32)


def gelu_parts(x):
    cdf = 0.5 + 0.5 * lax.erf(x * 0.7071067811865476)
    density = 0.3989422804014327 * jnp.exp2((-0.5 * 1.4426950408889634) * (x * x))
    return x * cdf, cdf + x * density


BLOCK_ROWS = 512
BLOCKS = ROWS // BLOCK_ROWS
HIDDEN_PART = 512
WEIGHT_PART = 256
PRODUCT_ROWS = 1024


def tile_values(stat_row, member):
    return jnp.broadcast_to(
        jnp.sum(member * stat_row, axis=1, keepdims=True), (CAP, LANES)
    )


def norm_values(stat, member):
    n = stat[0:1]
    variance = stat[2:3] / n
    inv = lax.rsqrt(variance + NORM_EPSILON)
    sample = lax.broadcasted_iota(jnp.int32, (1, LANES), 1) < SAMPLES
    inv = jnp.where(sample, inv, 0.0)
    return tile_values(stat[1:2], member), tile_values(inv, member)


HIDDEN_CHUNKS = HIDDEN_PAD // LANES


def wide(x, parts):
    return jnp.concatenate([x] * parts, axis=1)


def flat(parts):
    return jnp.concatenate([p.reshape(-1, LANES) for p in parts], axis=1)


def block_rows(i):
    return pl.ds(pl.multiple_of(i * BLOCK_ROWS, BLOCK_ROWS), BLOCK_ROWS)


def hidden_gradient(grad, mask, wout, update_hi, update_lo, back, vec):
    def block(i, carry):
        rows = block_rows(i)
        m = by_tile(mask[rows, :])
        g_update = [by_tile(grad[g, rows, :]) * m for g in range(GROUPS)]
        for g in range(GROUPS):
            vec[g, 0] += jnp.sum(g_update[g], axis=0)
        operand = split(flat(g_update))
        update_hi[rows, :], update_lo[rows, :] = operand
        for h in range(0, HIDDEN_PAD, HIDDEN_PART):
            part = slice(h, h + HIDDEN_PART)
            value = dot3(operand, (wout[0][part, :], wout[1][part, :]), 1, 1)
            for c in range(HIDDEN_PART // LANES):
                back[h // LANES + c, rows, :] = value[:, c * LANES : (c + 1) * LANES]
        return carry

    lax.fori_loop(0, BLOCKS, block, 0)


def centred_product(first, tile_mean, conv, lanes, win, ahead):
    rows = pl.ds(first, PRODUCT_ROWS)
    operand = split(
        flat(
            [
                (by_tile(conv[g, rows, :]) - tile_mean[None]) * lanes[g, 1:2, :][None]
                for g in range(GROUPS)
            ]
        )
    )
    for h in range(0, HIDDEN_PAD, HIDDEN_PART):
        part = slice(h, h + HIDDEN_PART)
        value = dot3(operand, (win[0][part, :], win[1][part, :]), 1, 1)
        for c in range(HIDDEN_PART // LANES):
            ahead[h // LANES + c][rows, :] = value[:, c * LANES : (c + 1) * LANES]


def scaled_operand(stat, member, conv, lanes, scaled_hi, scaled_lo):
    mean, inv = norm_values(stat, member)

    def block(i, carry):
        rows = block_rows(i)
        scaled_hi[rows, :], scaled_lo[rows, :] = split(
            flat(
                [
                    (by_tile(conv[g, rows, :]) - mean[None]) * inv[None] * lanes[g, 1:2, :][None]
                    + lanes[g, 2:3, :][None]
                    for g in range(GROUPS)
                ]
            )
        )
        return carry

    lax.fori_loop(0, BLOCKS, block, 0)


def weight_products(h, stat, member, tile_mean, lines, scaled, update, ahead, back, dw, hvec):
    mean, inv = norm_values(stat, member)
    part = slice(h, h + WEIGHT_PART)
    chunks = range(h // LANES, (h + WEIGHT_PART) // LANES)
    offset = lines[1:2, part] + wide((tile_mean - mean) * inv, len(chunks)) * lines[0:1, part]
    pre = jnp.concatenate([ahead[c][...] for c in chunks], axis=1)
    pre = pre.reshape(-1, CAP, WEIGHT_PART) * wide(inv, len(chunks))[None] + offset[None]
    hidden, slope = gelu_parts(pre.reshape(-1, WEIGHT_PART))
    g_pre = jnp.concatenate([back[c] for c in chunks], axis=1) * slope
    for i, c in enumerate(chunks):
        span = slice(i * LANES, (i + 1) * LANES)
        ahead[c][...] = hidden[:, span]
        back[c] = g_pre[:, span]
    hvec[:, part] = jnp.sum(g_pre, axis=0, keepdims=True)
    dw[0:256, part] = dot3((scaled[0][...], scaled[1][...]), split(g_pre), 0, 0)
    dw[256:512, part] = dot3((update[0][...], update[1][...]), split(hidden), 0, 0)


def scaled_gradient(low, high, sums, stat, member, win, back, conv, lanes, gscaled, vec):
    mean, inv = norm_values(stat, member)
    win = (win[0][...], win[1][...])

    def block(i, carry):
        rows = block_rows(i)
        g_pre = split(jnp.concatenate([back[c, rows, :] for c in range(HIDDEN_CHUNKS)], axis=1))
        value = dot3(g_pre, win, 1, 0)
        first, second = carry
        for g in range(GROUPS):
            gs = by_tile(value[:, g * LANES : (g + 1) * LANES])
            normed = (by_tile(conv[g, rows, :]) - mean[None]) * inv[None]
            gscaled[g, rows, :] = gs.reshape(-1, LANES)
            gain_sum = jnp.sum(gs * normed, axis=0)
            bias_sum = jnp.sum(gs, axis=0)
            vec[g, 1] += gain_sum
            vec[g, 2] += bias_sum
            first = first + bias_sum * lanes[g, 1:2, :]
            second = second + gain_sum * lanes[g, 1:2, :]
        return first, second

    return lax.fori_loop(low, high, block, sums)


def output_block(i, ahead, wout, tiles, mask, lanes):
    rows = pl.ds(i * BLOCK_ROWS, BLOCK_ROWS)
    hidden = split(jnp.concatenate([chunk[rows, :] for chunk in ahead], axis=1))
    value = dot3(hidden, (wout[0][...], wout[1][...]), 1, 0)
    for g in range(GROUPS):
        part = value[:, g * LANES : (g + 1) * LANES] + lanes[g, 3:4, :]
        tiles[g, rows, :] = mask[rows, :] * (tiles[g, rows, :] + part)


def conv_gradient(stat, sums, member, conv, gscaled, mask, lanes, db):
    mean, inv = norm_values(stat, member)
    sample = lax.broadcasted_iota(jnp.int32, (1, LANES), 1) < SAMPLES
    share = jnp.where(sample, 1.0 / stat[0:1], 0.0)
    first = tile_values(sums[0:1] * share, member)
    second = tile_values(sums[1:2] * share, member)
    for g in range(GROUPS):
        gain = lanes[g, 1:2, :][None]

        def gradient(r, acc):
            rows = pl.ds(r * SIDE * CAP, SIDE * CAP)
            normed = (by_tile(conv[g, rows, :]) - mean[None]) * inv[None]
            g_normed = by_tile(gscaled[g, rows, :]) * gain
            value = (by_tile(mask[rows, :]) * inv[None]) * (
                g_normed - first[None] - normed * second[None]
            )
            gscaled[g, rows, :] = value.reshape(-1, LANES)
            return acc + jnp.sum(value, axis=0)

        db[g] = lax.fori_loop(0, SIDE, gradient, jnp.zeros((CAP, LANES), F32)) * lane_mask(g)


def input_gradient(g, ranges, gconv, w, gpad):
    def input_row(r, carry):
        low = jnp.maximum(r - (SIDE - 1), 0)
        high = jnp.minimum(r, KSIZE - 1)

        def tap(a, acc):
            x = by_tile(gconv[g, pl.ds((r - a) * SIDE * CAP, SIDE * CAP), :])
            for b in range(KSIZE):
                part = w[g, a * KSIZE + b][None] * x
                acc = acc[:b] + tuple(acc[b + i] + part[i] for i in range(SIDE)) + acc[b + SIDE :]
            return acc

        acc = lax.fori_loop(
            low, high + 1, tap, tuple(jnp.zeros((CAP, LANES), F32) for _ in range(PAD))
        )
        for i in range(PAD):
            gpad[pl.ds((r * PAD + i) * CAP, CAP), :] = acc[i]
        return carry

    for low_row, high_row in ranges:
        lax.fori_loop(low_row, high_row, input_row, 0)


HALF_ROWS = [((RIM, RIM + 8), (RIM + SIDE, PAD)), ((0, RIM), (RIM + 8, RIM + SIDE))]


def own_gradient(g, gpad, grad, mask):
    def add(r, carry):
        rows = pl.ds(r * SIDE * CAP, SIDE * CAP)
        centre = gpad[pl.ds(((r + RIM) * PAD + RIM) * CAP, SIDE * CAP), :]
        grad[g, rows, :] = grad[g, rows, :] * mask[rows, :] + centre
        return carry

    lax.fori_loop(0, SIDE, add, 0)


def scatter_chunks():
    spans = {-1: (0, SIDE - RIM), 0: (RIM, 0), 1: (RIM + SIDE, 0)}
    order = [(-1, -1), (-1, 0), (-1, 1), (0, -1), (0, 1), (1, -1), (1, 0), (1, 1)]
    chunks = [[], []]
    for dr, dc in order:
        dst_r, src_r = spans[dr]
        dst_c, src_c = spans[dc]
        cols = RIM if dc else SIDE
        groups = [[], []]
        if dr == 0:
            groups = [[range(0, 3), range(3, 8)], [range(8, 13), range(13, 16)]]
        elif dc == 0:
            groups[dr < 0] = [[0], [1], [2]]
        else:
            groups[dr < 0] = [range(3)]
        for half in range(2):
            chunks[half].append(
                [
                    [
                        ((dst_r + i) * PAD + dst_c, rim_index(src_r + i, src_c), cols)
                        for i in group
                    ]
                    for group in groups[half]
                ]
            )
    return chunks


CHUNKS = scatter_chunks()
CHUNK = 16
BACK_ROLES = 5


def onehots(near_ref, me, spread):
    size = (BACK_ROLES, CHUNK, CAP, LANES)
    role = lax.broadcasted_iota(jnp.int32, size, 0)
    cell = lax.broadcasted_iota(jnp.int32, size, 1)
    slot = lax.broadcasted_iota(jnp.int32, size, 2)
    lane = lax.broadcasted_iota(jnp.int32, size, 3)
    code = jnp.where(lane // CAP == cell, role * CAP + slot, -1)
    code = code.reshape(BACK_ROLES * LANES, LANES)
    lane = lax.broadcasted_iota(jnp.int32, (1, LANES), 1) % CAP
    for k in range(8):
        wanted = jnp.full((1, LANES), -2, jnp.int32)
        for t in range(CAP):
            n = near_ref[t, k]
            role, slot = place_of(n, me)
            wanted = jnp.where(lane == t, jnp.where(n >= 0, role * CAP + slot, -2), wanted)
        spread[k] = jnp.where(code == wanted, 1.0, 0.0).astype(BF16)


def scatter(g, half, gpad, spread, pool):
    for k in range(8):
        if not CHUNKS[half][k]:
            continue
        hot = spread[k]
        hot = jnp.concatenate([hot, hot], axis=1)
        for chunk in CHUNKS[half][k]:
            parts = [gpad[pl.ds(dst * CAP, cells * CAP), :] for dst, _, cells in chunk]
            used = sum(cells for _, _, cells in chunk)
            if used < CHUNK:
                parts.append(jnp.zeros(((CHUNK - used) * CAP, LANES), F32))
            value = parts[0] if len(parts) == 1 else jnp.concatenate(parts, axis=0)
            value = jnp.concatenate(split(value), axis=0)
            moved = jnp.dot(hot, value, preferred_element_type=F32)
            for role in range(BACK_ROLES):
                first = role * LANES
                for _, rim, cells in chunk:
                    rows = pl.ds(role * RIM_ROWS + rim * CAP, cells * CAP)
                    pool[g][rows, :] = pool[g][rows, :] + moved[first : first + cells * CAP]
                    first += cells * CAP


def weight_gradient(g, padded, gconv, small):
    def weight_row(a, carry):
        def one(r, acc):
            x = by_tile(padded[g, pl.ds((r + a) * PAD * CAP, PAD * CAP), :])
            y = by_tile(gconv[g, pl.ds(r * SIDE * CAP, SIDE * CAP), :])
            return tuple(acc[b] + jnp.sum(x[b : b + SIDE] * y, axis=0) for b in range(KSIZE))

        acc = lax.fori_loop(
            0, SIDE, one, tuple(jnp.zeros((CAP, LANES), F32) for _ in range(KSIZE))
        )
        for b in range(KSIZE):
            small[g, pl.ds(a * KSIZE + b, 1), :] = jnp.sum(acc[b], axis=0, keepdims=True)
        return carry

    lax.fori_loop(0, KSIZE, weight_row, 0)


HALF = 256


def block_kernel(
    near_ref, count_ref, sample_ref, x_ref, g_ref, win_ref, wout_ref, ocean_ref, wt_ref, cb_ref,
    gain_ref, nbias_ref, bout_ref, bin_ref,
    native_out, total_out, big_out, small_ref, stat_ref,
    xbuf, gbuf, tiles, grad, mask, pool0, pool1, padded, conv, w, lanes, member,
    weight_buf, win_hi, win_lo, wout_hi, wout_lo, update_hi, update_lo, scaled_hi, scaled_lo,
    back, extra, dw, vec, hvec, db, gpad, spread,
    other, slots1, sum1, slots2, sum2, zslots, big, small, tile, sslots, zcslots,
    inner, outer, partial, load_sem, store_sem, send, recv,
):
    pool = (pool0, pool1)
    me = lax.axis_index("tiles")
    core, z, x, y, xy = me % 2, (me // 2) % 4, (me // INNER) % 4, me // 32, me // INNER
    ahead, behind, partner = halo_peers()
    z_peers = [me + (((z + j) % 4) - z) * 2 for j in range(1, 4)]
    x_peers = [me + (((x + j) % 4) - x) * INNER for j in range(1, 4)]
    y_peers = [me + (((y + j) % 4) - y) * 32 for j in range(1, 4)]
    xy_peers = outer_peers()
    zc_peers = inner_peers()
    ready = greet([ahead, behind, partner] + zc_peers + xy_peers)

    used = [0]
    started = []

    def start(source, target, peer):
        i = used[0]
        used[0] += 1
        copy = remote(source, target, send.at[i], recv.at[i], peer)
        copy.start()
        started.append(copy)
        return copy

    def arrived(copies):
        for copy in copies:
            copy.wait_recv()

    def sent():
        for copy in started:
            copy.wait_send()
        started.clear()

    loads = load_native(x_ref, xbuf, load_sem) + load_native(g_ref, gbuf, load_sem, 4)
    loads.append(pltpu.make_async_copy(win_ref, weight_buf.at[0], load_sem.at[8]))
    loads.append(pltpu.make_async_copy(wout_ref, weight_buf.at[1], load_sem.at[9]))
    for copy in loads[:4]:
        copy.start()
    for half in range(2):
        xbuf[half, pl.ds(2000, 48), :] = jnp.zeros((48, LANES), F32)
        gbuf[half, pl.ds(2000, 48), :] = jnp.zeros((48, LANES), F32)

    out_ahead, out_behind, out_partner = [], [], []
    for p, (g, half) in enumerate(PIECES):
        loads[p].wait()
        to_rows(xbuf, tiles, g, half)
        for first, rim, cells in rim_spans(half):
            pool[g][pl.ds(4 * RIM_ROWS + rim * CAP, cells * CAP), :] = tiles[
                g, pl.ds(first * CAP, cells * CAP), :
            ]
        if p == 0:
            ready()
        own = piece(pool, 4, p)
        out_ahead.append(start(own, piece(pool, 1, p), ahead))
        out_behind.append(start(own, piece(pool, 0, p), behind))
        out_partner.append(start(own, piece(pool, 3, p), partner))

    for copy in loads[4:]:
        copy.start()
    taps = wt_ref[...]
    taps = jnp.concatenate([taps, jnp.zeros((KSIZE * KSIZE, 6), F32)], axis=1)
    for g in range(GROUPS):
        for k in range(KSIZE * KSIZE):
            w[g, k] = jnp.broadcast_to(
                taps[k : k + 1, g * LANES : (g + 1) * LANES], (CAP, LANES)
            )
    for g in range(GROUPS):
        pool[g][pl.ds(5 * RIM_ROWS, RIM_ROWS), :] = jnp.zeros((RIM_ROWS, LANES), F32)

        def clear(i, carry):
            padded[g, pl.ds(i * PAD * CAP, PAD * CAP), :] = jnp.zeros((PAD * CAP, LANES), F32)
            return carry

        lax.fori_loop(0, PAD, clear, 0)

        def centre(r, carry):
            padded[g, pl.ds(((r + RIM) * PAD + RIM) * CAP, SIDE * CAP), :] = tiles[
                g, pl.ds(r * SIDE * CAP, SIDE * CAP), :
            ]
            return carry

        lax.fori_loop(0, SIDE, centre, 0)
    for i, ref in enumerate((cb_ref, gain_ref, nbias_ref, bout_ref)):
        line = jnp.concatenate([ref[...], jnp.zeros((1, 6), F32)], axis=1)
        for g in range(GROUPS):
            lanes[g, i : i + 1, :] = line[:, g * LANES : (g + 1) * LANES]
    row = lax.broadcasted_iota(jnp.int32, (CAP, LANES), 0)
    lane = lax.broadcasted_iota(jnp.int32, (CAP, LANES), 1)
    sample = jnp.zeros((CAP, LANES), jnp.int32)
    for t in range(CAP):
        sample = jnp.where(row == t, sample_ref[t], sample)
    member[...] = (sample == lane).astype(F32)
    vec[...] = jnp.zeros_like(vec)
    passed = []

    def pass_on(p):
        out_ahead[p].wait_recv()
        passed.append(start(piece(pool, 1, p), piece(pool, 2, p), partner))

    own_conv(0, padded, conv, w, lanes)
    pass_on(0)
    own_conv(1, padded, conv, w, lanes)
    pass_on(1)
    for p, (g, half) in enumerate(PIECES):
        loads[4 + p].wait()
        to_rows(gbuf, grad, g, half)
    slot = lax.broadcasted_iota(jnp.int32, (CAP, CELLS), 0)
    ocean = jnp.where(slot < count_ref[0], ocean_ref[...].astype(F32), 0.0)
    for half in range(2):
        for t in range(CAP):
            mask[pl.ds(half * 1024 + t, LANES, stride=CAP), :] = jnp.broadcast_to(
                ocean[t : t + 1, half * LANES : (half + 1) * LANES], (LANES, LANES)
            ).T
    for i, (high, low) in enumerate(((win_hi, win_lo), (wout_hi, wout_lo))):
        loads[8 + i].wait()
        value = jnp.concatenate([weight_buf[i], jnp.zeros((1000, 6), F32)], axis=1)
        value = jnp.concatenate([value, jnp.zeros((24, 256), F32)], axis=0)
        high[...], low[...] = split(value)
    win, wout = (win_hi, win_lo), (wout_hi, wout_lo)
    scaled, update = (scaled_hi, scaled_lo), (update_hi, update_lo)
    hidden_gradient(grad, mask, wout, update_hi, update_lo, back, vec)
    ends = jnp.concatenate(
        [flat([lanes[g, 1:3, :] for g in range(GROUPS)]), jnp.zeros((14, 256), F32)], axis=0
    )
    lines = dot3(split(ends), (win_hi[...], win_lo[...]), 1, 1)
    bias_in = jnp.concatenate([bin_ref[...], jnp.zeros((1, 24), F32)], axis=1)
    lines = jnp.concatenate([lines[0:1], lines[1:2] + bias_in], axis=0)
    onehots(near_ref, me, spread)
    sums = []
    for g in range(GROUPS):
        if g == 1:
            pass_on(2)
            pass_on(3)
        for copies in (out_behind, out_partner, passed):
            arrived(copies[2 * g : 2 * g + 2])
        gather(g, near_ref, me, pool, padded)
        halo_conv(g, padded, conv, w)
        sums.append(masked_sum(g, conv, mask))

    def reduce_vector(i, vector, merge, between, later):
        partial[i] = vector
        copies = exchange_start(
            partial.at[i], send, recv, inner.at[i], used[0], me % INNER, zc_peers
        )
        used[0] += INNER - 1
        between()
        for copy in copies:
            copy.wait()
        partial[2 + i] = merge(inner[i])
        copies = exchange_start(
            partial.at[2 + i], send, recv, outer.at[i], used[0], xy, xy_peers
        )
        used[0] += OUTER - 1
        later()
        for copy in copies:
            copy.wait()
        return merge(outer[i])

    tile_mean = tile_average(sums[0][0] + sums[1][0], sums[0][1])
    stats = local_stats(tile_mean, sums[0][1], conv, mask, member[...])
    sent()
    products = [pool[c // 3].at[pl.ds(c % 3 * ROWS, ROWS), :] for c in range(6)]
    products += [extra.at[c] for c in range(2)]
    product = lambda first: centred_product(first, tile_mean, conv, lanes, win, products)
    stat = reduce_vector(0, stats, merge_stats, lambda: product(0), lambda: product(PRODUCT_ROWS))
    stat_ref[...] = stat

    mine = pl.multiple_of(core * HALF, HALF)
    theirs = pl.multiple_of((1 - core) * HALF, HALF)
    orders = [((y, y_peers, 32), (x, x_peers, INNER)), ((x, x_peers, INNER), (y, y_peers, 32))]

    def at(q, i, j, rows):
        (first, _, _), (second, _, _) = orders[q]
        i = first if i is None else i
        first_row = core * HALF + q * 128 + i * 32 + (0 if j is None else j * 8)
        return pl.ds(pl.multiple_of(first_row, 8), rows)

    def weight_sum(h):
        k = h // HIDDEN_PART
        part = pl.ds(h, HIDDEN_PART)
        halves = start(dw.at[pl.ds(theirs, HALF), part], other.at[k], partner)
        yield
        halves.wait_recv()
        dw[pl.ds(mine, HALF), part] = dw[pl.ds(mine, HALF), part] + other[k]
        yield
        copies = []
        for q, ((i, peers, stride), _) in enumerate(orders):
            for peer in peers:
                rows = at(q, (peer // stride) % 4, None, 32)
                copies.append(start(dw.at[rows, part], slots1.at[k, q, i], peer))
            slots1[k, q, i] = dw[at(q, None, None, 32), part]
        yield
        arrived(copies)
        copies = []
        for q, (_, (j, peers, stride)) in enumerate(orders):
            sum1[k, q] = jnp.sum(slots1[k, q], axis=0)
            for peer in peers:
                rows = pl.ds(pl.multiple_of(((peer // stride) % 4) * 8, 8), 8)
                copies.append(start(sum1.at[k, q, rows, :], slots2.at[k, q, j], peer))
            slots2[k, q, j] = sum1[k, q, pl.ds(pl.multiple_of(j * 8, 8), 8), :]
        yield
        arrived(copies)
        for q in range(2):
            sum2[k, q] = jnp.sum(slots2[k, q], axis=0)
        copies = [start(sum2.at[k], zslots.at[k, z], peer) for peer in z_peers]
        zslots[k, z] = sum2[k]
        yield
        arrived(copies)
        copies = []
        for q, (_, (j, peers, _)) in enumerate(orders):
            rows = at(q, None, j, 8)
            big[rows, part] = zslots[k, 0, q] + zslots[k, 1, q] + zslots[k, 2, q] + zslots[k, 3, q]
            copies += [start(big.at[rows, part], big.at[rows, part], peer) for peer in peers]
        yield
        arrived(copies)
        copies = []
        for q, ((_, peers, _), _) in enumerate(orders):
            rows = at(q, None, None, 32)
            copies += [start(big.at[rows, part], big.at[rows, part], peer) for peer in peers]
        yield
        arrived(copies)
        own = big.at[pl.ds(mine, HALF), part]
        crossed = start(own, own, partner)
        yield
        crossed.wait_recv()
        yield

    scaled_operand(stat, member[...], conv, lanes, scaled_hi, scaled_lo)

    def weights(h):
        weight_products(
            h, stat, member[...], tile_mean, lines, scaled, update, products, back, dw, hvec
        )

    def gradient(low, high, sums):
        return scaled_gradient(
            low, high, sums, stat, member[...], win, back, conv, lanes, gbuf, vec
        )

    weights(0)
    weights(WEIGHT_PART)
    early = weight_sum(0)
    next(early)
    weights(2 * WEIGHT_PART)
    next(early)
    next(early)
    weights(3 * WEIGHT_PART)
    late = weight_sum(HIDDEN_PART)
    next(late)
    zero = jnp.zeros((CAP, LANES), F32)
    sums = gradient(0, BLOCKS - 1, (zero, zero))
    next(late)
    next(late)
    next(early)
    sums = gradient(BLOCKS - 1, BLOCKS, sums)
    rows = [
        jnp.sum(member[...] * jnp.sum(value, axis=1, keepdims=True), axis=0, keepdims=True)
        for value in sums
    ]

    def before_outer():
        output_block(0, products, wout, tiles, mask, lanes)
        next(early)
        output_block(1, products, wout, tiles, mask, lanes)
        next(late)

    def after_outer():
        output_block(2, products, wout, tiles, mask, lanes)
        next(early)
        output_block(3, products, wout, tiles, mask, lanes)
        next(late)
        for g in range(GROUPS):

            def clear_rows(i, carry):
                pool[g][pl.ds(i * HALF_RIM, HALF_RIM), :] = jnp.zeros((HALF_RIM, LANES), F32)
                return carry

            lax.fori_loop(0, 2 * BACK_ROLES, clear_rows, 0)
        next(early)

    sums = reduce_vector(1, stack_rows(*rows), merge_sums, before_outer, after_outer)
    conv_gradient(stat, sums, member[...], conv, gbuf, mask, lanes, db)

    payload, direct, near, merged = [], [], [], []

    def pay(p):
        g, part = PIECES[p]
        return back.at[g, pl.ds(part * HALF_RIM, HALF_RIM), :]

    def got(i, p):
        g, part = PIECES[p]
        return back.at[2 + 2 * i + g, pl.ds(part * HALF_RIM, HALF_RIM), :]

    def rims_of(p):
        g, half = PIECES[p]
        input_gradient(g, HALF_ROWS[half], gbuf, w, gpad)
        scatter(g, half, gpad, spread, pool)
        payload.append(start(piece(pool, 2, p), pay(p), partner))
        near.append(start(piece(pool, 3, p), got(2, p), partner))

    def merge(p):
        payload[p].wait_recv()
        g, part = PIECES[p]
        rows = pl.ds(RIM_ROWS + part * HALF_RIM, HALF_RIM)
        pool[g][rows, :] = pool[g][rows, :] + back[g, pl.ds(part * HALF_RIM, HALF_RIM), :]
        merged.append(start(piece(pool, 1, p), got(1, p), behind))

    def off_chip(p):
        direct.append(start(piece(pool, 0, p), got(0, p), ahead))

    rims_of(0)
    next(late)
    off_chip(0)
    rims_of(1)
    merge(0)
    next(late)
    off_chip(1)
    own_gradient(0, gpad, grad, mask)
    merge(1)
    next(early)

    for g in range(GROUPS):
        weight_gradient(g, padded, gbuf, small)
        lines = [jnp.sum(db[g], axis=0, keepdims=True)]
        lines += [jnp.sum(vec[g, i], axis=0, keepdims=True) for i in range(3)]
        lines += [hvec[0:1, pl.ds((g * 4 + i) * LANES, LANES)] for i in range(4)]
        for i, line in enumerate(lines):
            small[g, pl.ds(49 + i, 1), :] = line
        small[g, pl.ds(57, 7), :] = jnp.zeros((7, LANES), F32)
    small_tile = lambda q: small.at[q // 8, pl.ds(pl.multiple_of((q % 8) * CAP, CAP), CAP), :]
    small_scattered = [start(small_tile(peer // INNER), sslots.at[xy], peer) for peer in xy_peers]
    sslots[xy] = small[xy // 8, pl.ds(pl.multiple_of((xy % 8) * CAP, CAP), CAP), :]
    rims_of(2)
    off_chip(2)
    next(late)
    merge(2)
    rims_of(3)
    own_gradient(1, gpad, grad, mask)
    arrived(small_scattered)
    tile[...] = jnp.sum(sslots[...], axis=0)
    zc_gathered = [start(tile, zcslots.at[me % INNER], peer) for peer in zc_peers]
    zcslots[me % INNER] = tile[...]
    off_chip(3)
    merge(3)
    next(early)
    next(late)
    stores = store_native(xbuf, native_out, store_sem)
    for p in range(4):
        from_rows(tiles, xbuf, *PIECES[p])
        stores[p].start()
    stores.append(pltpu.make_async_copy(big, big_out, store_sem.at[4]))
    stores[4].start()
    arrived(zc_gathered)
    small_ref[xy] = jnp.sum(zcslots[...], axis=0)
    small_gathered = [start(small_ref.at[xy], small_ref.at[xy], peer) for peer in xy_peers]
    for p, (g, half) in enumerate(PIECES):
        arrived([near[p], direct[p], merged[p]])
        for first, rim, cells in rim_spans(half):
            rows = pl.ds(first * CAP, cells * CAP)
            span = pl.ds(rim * CAP, cells * CAP)
            mine_at = pl.ds(4 * RIM_ROWS + rim * CAP, cells * CAP)
            grad[g, rows, :] = (grad[g, rows, :] + pool[g][mine_at, :]) + (
                back[6 + g, span, :] + (back[2 + g, span, :] + back[4 + g, span, :])
            )
        rows = pl.ds(half * 1024, 1024)
        stores.append(
            pltpu.make_async_copy(grad.at[g, rows, :], total_out.at[g, rows, :], store_sem.at[5 + p])
        )
        stores[-1].start()
    arrived(small_gathered)
    sent()
    for copy in stores:
        copy.wait()


def block(near, count, sample, x, g, win, wout, ocean, wt, cb, gain, nbias, bout, bin_):
    rows = (GROUPS, ROWS, LANES)
    vector = (CAP, LANES)
    weight = pltpu.VMEM((HIDDEN_PAD, 256), BF16)
    operand = pltpu.VMEM((ROWS, 256), BF16)
    copies = 16 + 2 * (INNER + OUTER - 2) + 2 * 29 + 16 + 15 + 7 + 15
    return pl.pallas_call(
        block_kernel,
        in_specs=[SMEM_SPEC] * 3 + [ANY_SPEC] * 4 + [VMEM_SPEC] * 7,
        out_specs=(ANY_SPEC,) * 3 + (VMEM_SPEC,) * 2,
        out_shape=(
            shape(2000, 256), shape(*rows), shape(512, HIDDEN_PAD), shape(16, *vector),
            shape(*vector),
        ),
        scratch_shapes=[
            buffer(*rows), buffer(*rows), buffer(*rows), buffer(*rows),
            buffer(ROWS, LANES), buffer(ROLES * RIM_ROWS, LANES), buffer(ROLES * RIM_ROWS, LANES),
            buffer(GROUPS, PAD * PAD * CAP, LANES), buffer(*rows),
            buffer(GROUPS, KSIZE * KSIZE, CAP, LANES), buffer(GROUPS, *vector),
            buffer(*vector), buffer(2, 1000, 250), weight, weight, weight, weight,
            operand, operand, operand, operand,
            buffer(HIDDEN_CHUNKS, ROWS, LANES), buffer(2, ROWS, LANES),
            buffer(512, HIDDEN_PAD), buffer(GROUPS, 3, *vector), buffer(1, HIDDEN_PAD),
            buffer(GROUPS, *vector), buffer(PAD * PAD * CAP, LANES),
            pltpu.VMEM((8, BACK_ROLES * LANES, LANES), BF16),
            buffer(2, HALF, HIDDEN_PART), buffer(2, 2, 4, 32, HIDDEN_PART),
            buffer(2, 2, 32, HIDDEN_PART), buffer(2, 2, 4, 8, HIDDEN_PART),
            buffer(2, 2, 8, HIDDEN_PART), buffer(2, 4, 2, 8, HIDDEN_PART),
            buffer(512, HIDDEN_PAD),
            buffer(GROUPS, 64, LANES), buffer(*vector), buffer(OUTER, *vector),
            buffer(INNER, *vector), buffer(2, INNER, *vector), buffer(2, OUTER, *vector),
            buffer(4, *vector), semaphores(10), semaphores(9), semaphores(copies),
            semaphores(copies),
        ],
        compiler_params=params(collective_id=1, has_side_effects=True),
        name="block",
    )(near, count, sample, x, g, win, wout, ocean, wt, cb, gain, nbias, bout, bin_)


def final_kernel(
    total_ref, native_ref, big_ref, small_ref, stat_ref,
    out_ref, tiles_ref, dwin_ref, dwout_ref, dconv_ref, db_ref, dgain_ref, dnbias_ref, dbin_ref,
    dbout_ref, total, buf, through, big, load_sem, store_sem,
):
    loads = [
        pltpu.make_async_copy(
            total_ref.at[g, pl.ds(half * 1024, 1024), :],
            total.at[g, pl.ds(half * 1024, 1024), :],
            load_sem.at[p],
        )
        for p, (g, half) in enumerate(PIECES)
    ]
    loads.append(pltpu.make_async_copy(big_ref, big, load_sem.at[4]))
    loads.append(pltpu.make_async_copy(native_ref, through, load_sem.at[5]))
    for copy in loads:
        copy.start()
    stores = store_native(buf, tiles_ref, store_sem)
    for p, (g, half) in enumerate(PIECES):
        loads[p].wait()
        from_rows(total, buf, g, half)
        stores[p].start()
    loads[5].wait()
    stores.append(pltpu.make_async_copy(through, out_ref, store_sem.at[4]))
    stores[4].start()
    sample = lax.broadcasted_iota(jnp.int32, (1, LANES), 1) < SAMPLES
    cells = jnp.sum(jnp.where(sample, stat_ref[0:1, :], 0.0), axis=1, keepdims=True)
    share = 250.0 / cells
    loads[4].wait()
    dwin_ref[...] = big[0:256, :].T[:1000, :250] * share
    dwout_ref[...] = big[256:512, :].T[:1000, :250] * share
    parts = [
        jnp.concatenate([small_ref[g * 8 + i] for i in range(8)], axis=0) * share
        for g in range(GROUPS)
    ]
    whole = jnp.concatenate(parts, axis=1)
    dconv_ref[...] = whole[0:49, :250]
    for i, ref in enumerate((db_ref, dbout_ref, dgain_ref, dnbias_ref)):
        ref[...] = whole[49 + i : 50 + i, :250]
    line = jnp.concatenate([part[53 + i : 54 + i] for part in parts for i in range(4)], axis=1)
    dbin_ref[...] = line[:, :1000]
    for copy in stores:
        copy.wait()


def final(total, out, big, small, stat):
    return pl.pallas_call(
        final_kernel,
        in_specs=[ANY_SPEC] * 3 + [VMEM_SPEC] * 2,
        out_specs=(ANY_SPEC,) * 2 + (VMEM_SPEC,) * 8,
        out_shape=(
            shape(2000, 256), shape(2000, 256), shape(1000, 250), shape(1000, 250),
            shape(49, 250), shape(1, 250), shape(1, 250), shape(1, 250), shape(1, 1000),
            shape(1, 250),
        ),
        scratch_shapes=[
            buffer(GROUPS, ROWS, LANES), buffer(GROUPS, ROWS, LANES), buffer(2000, 256),
            buffer(512, HIDDEN_PAD), semaphores(6), semaphores(5),
        ],
        compiler_params=params(),
        name="final",
    )(total, out, big, small, stat)


def native(x):
    return jnp.transpose(x, (1, 0, 2)).reshape(2000, CELLS)


def from_native(x):
    return jnp.transpose(x.reshape(250, CAP, CELLS), (1, 0, 2))


def local(
    tiles_in, conv_weight, conv_bias, norm_gain, norm_bias, weight_in, bias_in,
    weight_out, bias_out, grad_out, tile_counts, ocean_mask, neighbours, sample_ids,
):
    out, total, big, small, stat = block(
        neighbours, tile_counts, sample_ids, native(tiles_in), native(grad_out), weight_in.T,
        weight_out, ocean_mask, conv_weight.T, conv_bias[None], norm_gain[None], norm_bias[None],
        bias_out[None], bias_in[None],
    )
    output, grad_tiles, dwin, dwout, dconv, db, dgain, dnbias, dbin, dbout = final(
        total, out, big, small, stat
    )
    return (
        from_native(output), from_native(grad_tiles), dconv.T, db[0], dgain[0], dnbias[0],
        dwin.T, dbin[0], dwout, dbout[0],
    )


def solution(mesh):
    tiles = P("tiles")
    whole = P()
    return jax.shard_map(
        local,
        mesh=mesh,
        in_specs=(tiles,) + (whole,) * 8 + (tiles,) * 5,
        out_specs=(tiles, tiles) + (whole,) * 8,
        check_vma=False,
    )
```

```python
import functools

import jax
import jax.numpy as jnp
from jax import lax
from jax.experimental import pallas as pl
from jax.experimental.pallas import tpu as pltpu
from jax.sharding import PartitionSpec as P

SIDE = 16
KSIZE = 7
RIM = 3
REACH = 2
SAMPLES = 5
CAP = 8
CELLS = SIDE * SIDE
PAD = SIDE + 2 * RIM
LANES = 128
GROUPS = 2
ROWS = CELLS * CAP
RIM_CELLS = 156
RIM_ROWS = RIM_CELLS * CAP
HIDDEN_PAD = 1024
NORM_EPSILON = 1e-05
F32 = jnp.float32
BF16 = jnp.bfloat16
MIB = 1 << 20
MESH = pl.DeviceIdType.MESH
VMEM_SPEC = pl.BlockSpec(memory_space=pltpu.VMEM)
SMEM_SPEC = pl.BlockSpec(memory_space=pltpu.SMEM)
ANY_SPEC = pl.BlockSpec(memory_space=pl.ANY)


def params(mib=62, **more):
    return pltpu.CompilerParams(vmem_limit_bytes=mib * MIB, **more)


HALF_RIM = RIM_ROWS // 2


def rim_spans(half):
    base = half * 78
    outer = 0 if half == 0 else SIDE - RIM
    inner = RIM if half == 0 else SIDE // 2
    spans = [(outer * SIDE, base, 48)]
    for i in range(5):
        spans.append(((inner + i) * SIDE, base + 48 + i * RIM, RIM))
        spans.append(((inner + i) * SIDE + SIDE - RIM, base + 63 + i * RIM, RIM))
    return spans


RIM_OF = {
    first + i: rim + i
    for half in range(2)
    for first, rim, cells in rim_spans(half)
    for i in range(cells)
}


def rim_index(r, c):
    return RIM_OF[r * SIDE + c]


def region_runs():
    spans = {-1: (0, SIDE - RIM, RIM), 0: (RIM, 0, SIDE), 1: (RIM + SIDE, 0, RIM)}
    order = [(-1, -1), (-1, 0), (-1, 1), (0, -1), (0, 1), (1, -1), (1, 0), (1, 1)]
    runs = []
    for dr, dc in order:
        dst_r, src_r, rows = spans[dr]
        dst_c, src_c, cols = spans[dc]
        found = []

        def add(cells):
            start = 0
            while start < len(cells):
                stop = start + 1
                while (
                    stop < len(cells)
                    and stop - start < 8
                    and cells[stop][0] - cells[stop - 1][0] == cells[1][0] - cells[0][0]
                    and cells[stop][1] - cells[stop - 1][1] == cells[1][1] - cells[0][1]
                ):
                    stop += 1
                step = (cells[1][0] - cells[0][0], cells[1][1] - cells[0][1])
                found.append((cells[start][0], step[0], cells[start][1], step[1], stop - start))
                start = stop

        if dr == 0:
            for j in range(cols):
                cells = [
                    ((dst_r + i) * PAD + dst_c + j, rim_index(src_r + i, src_c + j))
                    for i in range(rows)
                ]
                for low, high in ((0, RIM), (RIM, 8), (8, SIDE - RIM), (SIDE - RIM, SIDE)):
                    add(cells[low:high])
        else:
            for i in range(rows):
                add(
                    [
                        ((dst_r + i) * PAD + dst_c + j, rim_index(src_r + i, src_c + j))
                        for j in range(cols)
                    ]
                )
        runs.append(found)
    return runs


RUNS = region_runs()


ROLES = 6
PIECES = [(g, half) for g in range(GROUPS) for half in range(2)]


def piece(ref, role, p):
    g, half = PIECES[p]
    return ref[g].at[pl.ds(role * RIM_ROWS + half * HALF_RIM, HALF_RIM), :]


def halo_peers():
    me = lax.axis_index("tiles")
    total = lax.axis_size("tiles")
    sign = 2 * (me % 2) - 1
    ahead = (me + 2 * sign + total) % total
    behind = (me - 2 * sign + total) % total
    return ahead, behind, me - sign


def remote(src, dst, send, recv, peer):
    return pltpu.make_async_remote_copy(
        src_ref=src, dst_ref=dst, send_sem=send, recv_sem=recv,
        device_id=(peer,), device_id_type=MESH,
    )


def greet(peers):
    barrier = pltpu.get_barrier_semaphore()
    for peer in peers:
        pl.semaphore_signal(barrier, inc=1, device_id=(peer,), device_id_type=MESH)
    return lambda: pl.semaphore_wait(barrier, len(peers))


def load_native(x_ref, buf, sems, first=0):
    copies = []
    for g, half in PIECES:
        rows = 1024 if g == 0 else 976
        copies.append(
            pltpu.make_async_copy(
                x_ref.at[pl.ds(g * 1024, rows), pl.ds(half * LANES, LANES)],
                buf.at[half, pl.ds(g * 1024, rows), :],
                sems.at[first + len(copies)],
            )
        )
    return copies


def to_rows(buf, out, g, half):
    for t in range(CAP):
        block = buf[half, pl.ds(g * 1024 + t, LANES, stride=CAP), :]
        out[g, pl.ds(half * 1024 + t, LANES, stride=CAP), :] = block.T


def store_native(buf, out_ref, sems, first=0):
    copies = []
    for g, half in PIECES:
        rows = 1024 if g == 0 else 976
        copies.append(
            pltpu.make_async_copy(
                buf.at[half, pl.ds(g * 1024, rows), :],
                out_ref.at[pl.ds(g * 1024, rows), pl.ds(half * LANES, LANES)],
                sems.at[first + len(copies)],
            )
        )
    return copies


def from_rows(rows, buf, g, half):
    for t in range(CAP):
        block = rows[g, pl.ds(half * 1024 + t, LANES, stride=CAP), :]
        buf[half, pl.ds(g * 1024 + t, LANES, stride=CAP), :] = block.T


def lane_mask(g):
    lane = lax.broadcasted_iota(jnp.int32, (CAP, LANES), 1)
    return (lane < 250 - g * LANES).astype(F32)


def shape(*dims):
    return jax.ShapeDtypeStruct(dims, F32)


def buffer(*dims):
    return pltpu.VMEM(dims, F32)


def semaphores(count):
    return pltpu.SemaphoreType.DMA((count,))


INNER = 8
OUTER = 16


def inner_peers():
    me = lax.axis_index("tiles")
    group, place = me // INNER, me % INNER
    return [group * INNER + (place + j) % INNER for j in range(1, INNER)]


def outer_peers():
    me = lax.axis_index("tiles")
    group, place = me // INNER, me % INNER
    return [((group + j) % OUTER) * INNER + place for j in range(1, OUTER)]


def exchange_start(x, send, recv, slots, first, mine, peers):
    copies = [
        remote(x, slots.at[mine], send.at[first + j], recv.at[first + j], peer)
        for j, peer in enumerate(peers)
    ]
    for copy in copies:
        copy.start()
    slots[mine] = x[...]
    return copies


def merge_stats(parts):
    n = jnp.sum(parts[:, 0:1], axis=0)
    mean = jnp.sum(parts[:, 0:1] * parts[:, 1:2], axis=0) / jnp.maximum(n, 1.0)
    off = parts[:, 1:2] - mean[None]
    m2 = jnp.sum(parts[:, 2:3] + parts[:, 0:1] * off * off, axis=0)
    return stack_rows(n, mean, m2)


def stack_rows(*rows):
    row_id = lax.broadcasted_iota(jnp.int32, (CAP, LANES), 0)
    value = jnp.zeros((CAP, LANES), F32)
    for i, row in enumerate(rows):
        value = jnp.where(row_id == i, row, value)
    return value


def merge_sums(parts):
    return jnp.sum(parts, axis=0)


def by_tile(x):
    return x.reshape(-1, CAP, LANES)


def own_conv(g, padded, conv, w, lanes_ref):
    bias = jnp.broadcast_to(lanes_ref[g, 0:1, :], (CAP, LANES))[None]

    def row(r, carry):
        acc = jnp.broadcast_to(bias, (SIDE, CAP, LANES))
        for a in range(KSIZE):
            x = by_tile(padded[g, pl.ds((r + a) * PAD * CAP, PAD * CAP), :])
            for b in range(KSIZE):
                acc = acc + w[g, a * KSIZE + b][None] * x[b : b + SIDE]
        conv[g, pl.ds(r * SIDE * CAP, SIDE * CAP), :] = acc.reshape(-1, LANES)
        return carry

    lax.fori_loop(0, SIDE, row, 0, unroll=4)


def place_of(n, me):
    offset = (n // CAP - me) * (2 * (me % 2) - 1)
    role = jnp.where(offset == 2, 0, jnp.where(offset == -2, 1, 4))
    role = jnp.where(offset == 1, 2, jnp.where(offset == -1, 3, role))
    valid = n >= 0
    return jnp.where(valid, role, 5), jnp.where(valid, n % CAP, 0)


def gather(g, near_ref, me, pool, padded):
    def fill(t, carry):
        for k in range(8):
            role, slot = place_of(near_ref[t, k], me)
            q = role * RIM_ROWS + slot
            for dst, dst_step, src, src_step, length in RUNS[k]:
                padded[g, pl.ds(dst * CAP + t, length, stride=dst_step * CAP), :] = pool[g][
                    pl.ds(q + src * CAP, length, stride=src_step * CAP), :
                ]
        return carry

    lax.fori_loop(0, CAP, fill, 0)


def halo_conv(g, padded, conv, w):
    blank = jnp.zeros((RIM, CAP, LANES), F32)
    for r in [0, 1, 2, 13, 14, 15]:
        rows = pl.ds(r * SIDE * CAP, SIDE * CAP)
        acc = by_tile(conv[g, rows, :])
        for a in range(KSIZE):
            if RIM <= r + a < RIM + SIDE:
                continue
            x = by_tile(padded[g, pl.ds(((r + a) * PAD + RIM) * CAP, SIDE * CAP), :])
            x = jnp.concatenate([blank, x, blank], axis=0)
            for b in range(KSIZE):
                acc = acc + w[g, a * KSIZE + b][None] * x[b : b + SIDE]
        conv[g, rows, :] = acc.reshape(-1, LANES)

    def columns(r, carry):
        left = [jnp.zeros((CAP, LANES), F32) for _ in range(RIM)]
        right = [jnp.zeros((CAP, LANES), F32) for _ in range(RIM)]
        for a in range(KSIZE):
            first = (r + a) * PAD * CAP
            xl = by_tile(padded[g, pl.ds(first, RIM * CAP), :])
            xr = by_tile(padded[g, pl.ds(first + (RIM + SIDE) * CAP, RIM * CAP), :])
            for c in range(RIM):
                for b in range(RIM - c):
                    left[c] = left[c] + w[g, a * KSIZE + b] * xl[c + b]
                for b in range(KSIZE - 1 - c, KSIZE):
                    right[c] = right[c] + w[g, a * KSIZE + b] * xr[c + b - KSIZE + 1]
        for c in range(RIM):
            cell = pl.ds((r * SIDE + c) * CAP, CAP)
            conv[g, cell, :] = conv[g, cell, :] + left[c]
            cell = pl.ds((r * SIDE + SIDE - RIM + c) * CAP, CAP)
            conv[g, cell, :] = conv[g, cell, :] + right[c]
        return carry

    lax.fori_loop(0, SIDE, columns, 0)


def masked_sum(g, conv, mask):
    zero = jnp.zeros((CAP, LANES), F32)

    def add(r, carry):
        rows = pl.ds(r * SIDE * CAP, SIDE * CAP)
        m = by_tile(mask[rows, :])
        x = by_tile(conv[g, rows, :])
        return carry[0] + jnp.sum(x * m, axis=0), carry[1] + jnp.sum(m, axis=0)

    return lax.fori_loop(0, SIDE, add, (zero, zero))


def tile_average(sums, cells):
    total = jnp.broadcast_to(jnp.sum(sums, axis=1, keepdims=True), (CAP, LANES))
    return total / jnp.maximum(250.0 * cells, 1.0)


def local_stats(mean, cells, conv, mask, member):
    entries = 250.0 * cells
    zero = jnp.zeros((CAP, LANES), F32)
    squares = zero
    for g in range(GROUPS):

        def square(r, acc):
            rows = pl.ds(r * SIDE * CAP, SIDE * CAP)
            diff = by_tile(conv[g, rows, :]) - mean[None]
            return acc + jnp.sum(diff * diff * by_tile(mask[rows, :]), axis=0)

        squares = squares + lax.fori_loop(0, SIDE, square, zero) * lane_mask(g)
    spread = jnp.broadcast_to(jnp.sum(squares, axis=1, keepdims=True), (CAP, LANES))
    n_tile = member * entries
    n = jnp.sum(n_tile, axis=0, keepdims=True)
    centre = jnp.sum(n_tile * mean, axis=0, keepdims=True) / jnp.maximum(n, 1.0)
    off = mean - centre
    m2 = jnp.sum(member * spread + n_tile * off * off, axis=0, keepdims=True)
    return stack_rows(n, centre, m2)


def split(x):
    high = x.astype(BF16)
    return high, (x - high.astype(F32)).astype(BF16)


def dot3(a, b, lhs_dim, rhs_dim):
    dims = (((lhs_dim,), (rhs_dim,)), ((), ()))
    left = jnp.concatenate([a[0], a[1], a[0]], axis=lhs_dim)
    right = jnp.concatenate([b[0], b[0], b[1]], axis=rhs_dim)
    return lax.dot_general(left, right, dimension_numbers=dims, preferred_element_type=F32)


def gelu_parts(x):
    cdf = 0.5 + 0.5 * lax.erf(x * 0.7071067811865476)
    density = 0.3989422804014327 * jnp.exp2((-0.5 * 1.4426950408889634) * (x * x))
    return x * cdf, cdf + x * density


BLOCK_ROWS = 512
BLOCKS = ROWS // BLOCK_ROWS
HIDDEN_PART = 512
WEIGHT_PART = 256
PRODUCT_ROWS = 1024


def tile_values(stat_row, member):
    return jnp.broadcast_to(
        jnp.sum(member * stat_row, axis=1, keepdims=True), (CAP, LANES)
    )


def norm_values(stat, member):
    n = stat[0:1]
    variance = stat[2:3] / n
    inv = lax.rsqrt(variance + NORM_EPSILON)
    sample = lax.broadcasted_iota(jnp.int32, (1, LANES), 1) < SAMPLES
    inv = jnp.where(sample, inv, 0.0)
    return tile_values(stat[1:2], member), tile_values(inv, member)


HIDDEN_CHUNKS = HIDDEN_PAD // LANES


def wide(x, parts):
    return jnp.concatenate([x] * parts, axis=1)


def flat(parts):
    return jnp.concatenate([p.reshape(-1, LANES) for p in parts], axis=1)


def block_rows(i):
    return pl.ds(pl.multiple_of(i * BLOCK_ROWS, BLOCK_ROWS), BLOCK_ROWS)


def hidden_gradient(grad, mask, wout, update_hi, update_lo, back, vec):
    def block(i, carry):
        rows = block_rows(i)
        m = by_tile(mask[rows, :])
        g_update = [by_tile(grad[g, rows, :]) * m for g in range(GROUPS)]
        for g in range(GROUPS):
            vec[g, 0] += jnp.sum(g_update[g], axis=0)
        operand = split(flat(g_update))
        update_hi[rows, :], update_lo[rows, :] = operand
        for h in range(0, HIDDEN_PAD, HIDDEN_PART):
            part = slice(h, h + HIDDEN_PART)
            value = dot3(operand, (wout[0][part, :], wout[1][part, :]), 1, 1)
            for c in range(HIDDEN_PART // LANES):
                back[h // LANES + c, rows, :] = value[:, c * LANES : (c + 1) * LANES]
        return carry

    lax.fori_loop(0, BLOCKS, block, 0)


def centred_product(first, tile_mean, conv, lanes, win, ahead):
    rows = pl.ds(first, PRODUCT_ROWS)
    operand = split(
        flat(
            [
                (by_tile(conv[g, rows, :]) - tile_mean[None]) * lanes[g, 1:2, :][None]
                for g in range(GROUPS)
            ]
        )
    )
    for h in range(0, HIDDEN_PAD, HIDDEN_PART):
        part = slice(h, h + HIDDEN_PART)
        value = dot3(operand, (win[0][part, :], win[1][part, :]), 1, 1)
        for c in range(HIDDEN_PART // LANES):
            ahead[h // LANES + c][rows, :] = value[:, c * LANES : (c + 1) * LANES]


def scaled_operand(stat, member, conv, lanes, scaled_hi, scaled_lo):
    mean, inv = norm_values(stat, member)

    def block(i, carry):
        rows = block_rows(i)
        scaled_hi[rows, :], scaled_lo[rows, :] = split(
            flat(
                [
                    (by_tile(conv[g, rows, :]) - mean[None]) * inv[None] * lanes[g, 1:2, :][None]
                    + lanes[g, 2:3, :][None]
                    for g in range(GROUPS)
                ]
            )
        )
        return carry

    lax.fori_loop(0, BLOCKS, block, 0)


def weight_products(h, stat, member, tile_mean, lines, scaled, update, ahead, back, dw, hvec):
    mean, inv = norm_values(stat, member)
    part = slice(h, h + WEIGHT_PART)
    chunks = range(h // LANES, (h + WEIGHT_PART) // LANES)
    offset = lines[1:2, part] + wide((tile_mean - mean) * inv, len(chunks)) * lines[0:1, part]
    pre = jnp.concatenate([ahead[c][...] for c in chunks], axis=1)
    pre = pre.reshape(-1, CAP, WEIGHT_PART) * wide(inv, len(chunks))[None] + offset[None]
    hidden, slope = gelu_parts(pre.reshape(-1, WEIGHT_PART))
    g_pre = jnp.concatenate([back[c] for c in chunks], axis=1) * slope
    for i, c in enumerate(chunks):
        span = slice(i * LANES, (i + 1) * LANES)
        ahead[c][...] = hidden[:, span]
        back[c] = g_pre[:, span]
    hvec[:, part] = jnp.sum(g_pre, axis=0, keepdims=True)
    dw[0:256, part] = dot3((scaled[0][...], scaled[1][...]), split(g_pre), 0, 0)
    dw[256:512, part] = dot3((update[0][...], update[1][...]), split(hidden), 0, 0)


def scaled_gradient(low, high, sums, stat, member, win, back, conv, lanes, gscaled, vec):
    mean, inv = norm_values(stat, member)
    win = (win[0][...], win[1][...])

    def block(i, carry):
        rows = block_rows(i)
        g_pre = split(jnp.concatenate([back[c, rows, :] for c in range(HIDDEN_CHUNKS)], axis=1))
        value = dot3(g_pre, win, 1, 0)
        first, second = carry
        for g in range(GROUPS):
            gs = by_tile(value[:, g * LANES : (g + 1) * LANES])
            normed = (by_tile(conv[g, rows, :]) - mean[None]) * inv[None]
            gscaled[g, rows, :] = gs.reshape(-1, LANES)
            gain_sum = jnp.sum(gs * normed, axis=0)
            bias_sum = jnp.sum(gs, axis=0)
            vec[g, 1] += gain_sum
            vec[g, 2] += bias_sum
            first = first + bias_sum * lanes[g, 1:2, :]
            second = second + gain_sum * lanes[g, 1:2, :]
        return first, second

    return lax.fori_loop(low, high, block, sums)


def output_block(i, ahead, wout, tiles, mask, lanes):
    rows = pl.ds(i * BLOCK_ROWS, BLOCK_ROWS)
    hidden = split(jnp.concatenate([chunk[rows, :] for chunk in ahead], axis=1))
    value = dot3(hidden, (wout[0][...], wout[1][...]), 1, 0)
    for g in range(GROUPS):
        part = value[:, g * LANES : (g + 1) * LANES] + lanes[g, 3:4, :]
        tiles[g, rows, :] = mask[rows, :] * (tiles[g, rows, :] + part)


def conv_gradient(g, stat, sums, member, conv, gscaled, mask, lanes, db):
    mean, inv = norm_values(stat, member)
    sample = lax.broadcasted_iota(jnp.int32, (1, LANES), 1) < SAMPLES
    share = jnp.where(sample, 1.0 / stat[0:1], 0.0)
    first = tile_values(sums[0:1] * share, member)
    second = tile_values(sums[1:2] * share, member)
    gain = lanes[g, 1:2, :][None]

    def gradient(r, acc):
        rows = pl.ds(r * SIDE * CAP, SIDE * CAP)
        normed = (by_tile(conv[g, rows, :]) - mean[None]) * inv[None]
        g_normed = by_tile(gscaled[g, rows, :]) * gain
        value = (by_tile(mask[rows, :]) * inv[None]) * (
            g_normed - first[None] - normed * second[None]
        )
        gscaled[g, rows, :] = value.reshape(-1, LANES)
        return acc + jnp.sum(value, axis=0)

    db[g] = lax.fori_loop(0, SIDE, gradient, jnp.zeros((CAP, LANES), F32)) * lane_mask(g)


def input_gradient(g, ranges, gconv, w, gpad):
    def tap(r, a, acc):
        x = by_tile(gconv[g, pl.ds((r - a) * SIDE * CAP, SIDE * CAP), :])
        for b in range(KSIZE):
            part = w[g, a * KSIZE + b][None] * x
            acc = acc[:b] + tuple(acc[b + i] + part[i] for i in range(SIDE)) + acc[b + SIDE :]
        return acc

    def store(r, acc):
        for i in range(PAD):
            gpad[pl.ds((r * PAD + i) * CAP, CAP), :] = acc[i]

    def blank():
        return tuple(jnp.zeros((CAP, LANES), F32) for _ in range(PAD))

    def full_row(r, carry):
        acc = blank()
        for a in range(KSIZE):
            acc = tap(r, a, acc)
        store(r, acc)
        return carry

    for low, high in ranges:
        for r in range(low, min(high, KSIZE - 1)):
            acc = blank()
            for a in range(r + 1):
                acc = tap(r, a, acc)
            store(r, acc)
        if min(high, SIDE) > max(low, KSIZE - 1):
            lax.fori_loop(max(low, KSIZE - 1), min(high, SIDE), full_row, 0)
        for r in range(max(low, SIDE), high):
            acc = blank()
            for a in range(r - SIDE + 1, KSIZE):
                acc = tap(r, a, acc)
            store(r, acc)


HALF_ROWS = [((RIM, RIM + 8), (RIM + SIDE, PAD)), ((0, RIM), (RIM + 8, RIM + SIDE))]


def own_gradient(g, gpad, grad, mask):
    def add(r, carry):
        rows = pl.ds(r * SIDE * CAP, SIDE * CAP)
        centre = gpad[pl.ds(((r + RIM) * PAD + RIM) * CAP, SIDE * CAP), :]
        grad[g, rows, :] = grad[g, rows, :] * mask[rows, :] + centre
        return carry

    lax.fori_loop(0, SIDE, add, 0)


def scatter_chunks():
    spans = {-1: (0, SIDE - RIM), 0: (RIM, 0), 1: (RIM + SIDE, 0)}
    order = [(-1, -1), (-1, 0), (-1, 1), (0, -1), (0, 1), (1, -1), (1, 0), (1, 1)]
    chunks = [[], []]
    for dr, dc in order:
        dst_r, src_r = spans[dr]
        dst_c, src_c = spans[dc]
        cols = RIM if dc else SIDE
        groups = [[], []]
        if dr == 0:
            groups = [[range(0, 3), range(3, 8)], [range(8, 13), range(13, 16)]]
        elif dc == 0:
            groups[dr < 0] = [[0], [1], [2]]
        else:
            groups[dr < 0] = [range(3)]
        for half in range(2):
            chunks[half].append(
                [
                    [
                        ((dst_r + i) * PAD + dst_c, rim_index(src_r + i, src_c), cols)
                        for i in group
                    ]
                    for group in groups[half]
                ]
            )
    return chunks


CHUNKS = scatter_chunks()
CHUNK = 16
BACK_ROLES = 5


def onehots(near_ref, me, spread):
    size = (BACK_ROLES, CHUNK, CAP, LANES)
    role = lax.broadcasted_iota(jnp.int32, size, 0)
    cell = lax.broadcasted_iota(jnp.int32, size, 1)
    slot = lax.broadcasted_iota(jnp.int32, size, 2)
    lane = lax.broadcasted_iota(jnp.int32, size, 3)
    code = jnp.where(lane // CAP == cell, role * CAP + slot, -1)
    code = code.reshape(BACK_ROLES * LANES, LANES)
    lane = lax.broadcasted_iota(jnp.int32, (1, LANES), 1) % CAP
    for k in range(8):
        wanted = jnp.full((1, LANES), -2, jnp.int32)
        for t in range(CAP):
            n = near_ref[t, k]
            role, slot = place_of(n, me)
            wanted = jnp.where(lane == t, jnp.where(n >= 0, role * CAP + slot, -2), wanted)
        spread[k] = jnp.where(code == wanted, 1.0, 0.0).astype(BF16)


def scatter(g, half, gpad, spread, pool):
    outer = 1 if half else 6
    for k in [outer] + [k for k in range(8) if k != outer and CHUNKS[half][k]]:
        hot = spread[k]
        hot = jnp.concatenate([hot, hot], axis=1)
        for chunk in CHUNKS[half][k]:
            fresh = k == outer or len(chunk) == 5
            parts = [gpad[pl.ds(dst * CAP, cells * CAP), :] for dst, _, cells in chunk]
            used = sum(cells for _, _, cells in chunk)
            if used < CHUNK:
                parts.append(jnp.zeros(((CHUNK - used) * CAP, LANES), F32))
            value = parts[0] if len(parts) == 1 else jnp.concatenate(parts, axis=0)
            value = jnp.concatenate(split(value), axis=0)
            moved = jnp.dot(hot, value, preferred_element_type=F32)
            for role in range(BACK_ROLES):
                first = role * LANES
                for _, rim, cells in chunk:
                    rows = pl.ds(role * RIM_ROWS + rim * CAP, cells * CAP)
                    value = moved[first : first + cells * CAP]
                    pool[g][rows, :] = value if fresh else pool[g][rows, :] + value
                    first += cells * CAP


def weight_gradient(g, padded, gconv, small):
    def weight_row(a, carry):
        def one(r, acc):
            x = by_tile(padded[g, pl.ds((r + a) * PAD * CAP, PAD * CAP), :])
            y = by_tile(gconv[g, pl.ds(r * SIDE * CAP, SIDE * CAP), :])
            acc = list(acc)
            for c in range(SIDE):
                for b in range(KSIZE):
                    acc[b] = acc[b] + x[c + b] * y[c]
            return tuple(acc)

        acc = lax.fori_loop(
            0, SIDE, one, tuple(jnp.zeros((CAP, LANES), F32) for _ in range(KSIZE)), unroll=2
        )
        for b in range(KSIZE):
            small[g, pl.ds(a * KSIZE + b, 1), :] = jnp.sum(acc[b], axis=0, keepdims=True)
        return carry

    lax.fori_loop(0, KSIZE, weight_row, 0)


HALF = 256


def block_kernel(
    near_in, count_in, sample_in, x_ref, g_ref, win_ref, wout_ref, ocean_in, wt_in, cb_in,
    gain_in, nbias_in, bout_in, bin_in,
    native_out, total_out, big_out, small_ref, stat_ref,
    near_ref, count_ref, sample_ref, ocean_ref, wt_ref, cb_ref, gain_ref, nbias_ref, bout_ref,
    bin_ref, xbuf, gbuf, tiles, grad, mask, pool0, pool1, padded, conv, w, lanes, member,
    weight_buf, win_hi, win_lo, wout_hi, wout_lo, update_hi, update_lo, scaled_hi, scaled_lo,
    back, extra, dw, vec, hvec, db, gpad, spread,
    other, slots1, sum1, slots2, sum2, zslots, big, small, tile, sslots, zcslots,
    inner, outer, partial, load_sem, store_sem, send, recv,
):
    pool = (pool0, pool1)
    me = lax.axis_index("tiles")
    core, z, x, y, xy = me % 2, (me // 2) % 4, (me // INNER) % 4, me // 32, me // INNER
    ahead, behind, partner = halo_peers()
    z_peers = [me + (((z + j) % 4) - z) * 2 for j in range(1, 4)]
    x_peers = [me + (((x + j) % 4) - x) * INNER for j in range(1, 4)]
    y_peers = [me + (((y + j) % 4) - y) * 32 for j in range(1, 4)]
    xy_peers = outer_peers()
    zc_peers = inner_peers()
    ready = greet([ahead, behind, partner] + zc_peers + xy_peers)

    used = [0]
    started = []

    def start(source, target, peer):
        i = used[0]
        used[0] += 1
        copy = remote(source, target, send.at[i], recv.at[i], peer)
        copy.start()
        started.append(copy)
        return copy

    def arrived(copies):
        for copy in copies:
            copy.wait_recv()

    def sent():
        for copy in started:
            copy.wait_send()
        started.clear()

    loads = load_native(x_ref, xbuf, load_sem) + load_native(g_ref, gbuf, load_sem, 4)
    loads.append(pltpu.make_async_copy(win_ref, weight_buf.at[0], load_sem.at[8]))
    loads.append(pltpu.make_async_copy(wout_ref, weight_buf.at[1], load_sem.at[9]))
    for copy in loads[:4]:
        copy.start()
    operands = [
        (wt_in, wt_ref), (cb_in, cb_ref), (gain_in, gain_ref), (nbias_in, nbias_ref),
        (bout_in, bout_ref), (sample_in, sample_ref), (count_in, count_ref),
        (ocean_in, ocean_ref), (bin_in, bin_ref), (near_in, near_ref),
    ]
    fetched = [
        pltpu.make_async_copy(source, target, load_sem.at[10 + i])
        for i, (source, target) in enumerate(operands)
    ]
    for copy in fetched:
        copy.start()
    for half in range(2):
        xbuf[half, pl.ds(2000, 48), :] = jnp.zeros((48, LANES), F32)
        gbuf[half, pl.ds(2000, 48), :] = jnp.zeros((48, LANES), F32)

    out_ahead, out_behind, out_partner = [], [], []
    for p, (g, half) in enumerate(PIECES):
        loads[p].wait()
        to_rows(xbuf, tiles, g, half)
        for first, rim, cells in rim_spans(half):
            pool[g][pl.ds(4 * RIM_ROWS + rim * CAP, cells * CAP), :] = tiles[
                g, pl.ds(first * CAP, cells * CAP), :
            ]
        if p == 0:
            ready()
        own = piece(pool, 4, p)
        out_ahead.append(start(own, piece(pool, 1, p), ahead))
        out_behind.append(start(own, piece(pool, 0, p), behind))
        out_partner.append(start(own, piece(pool, 3, p), partner))

    for copy in loads[4:]:
        copy.start()
    for copy in fetched:
        copy.wait()
    taps = wt_ref[...]
    taps = jnp.concatenate([taps, jnp.zeros((KSIZE * KSIZE, 6), F32)], axis=1)
    for g in range(GROUPS):
        for k in range(KSIZE * KSIZE):
            w[g, k] = jnp.broadcast_to(
                taps[k : k + 1, g * LANES : (g + 1) * LANES], (CAP, LANES)
            )
    for g in range(GROUPS):
        pool[g][pl.ds(5 * RIM_ROWS, RIM_ROWS), :] = jnp.zeros((RIM_ROWS, LANES), F32)

        def clear(i, carry):
            padded[g, pl.ds(i * PAD * CAP, PAD * CAP), :] = jnp.zeros((PAD * CAP, LANES), F32)
            return carry

        lax.fori_loop(0, PAD, clear, 0)

        def centre(r, carry):
            padded[g, pl.ds(((r + RIM) * PAD + RIM) * CAP, SIDE * CAP), :] = tiles[
                g, pl.ds(r * SIDE * CAP, SIDE * CAP), :
            ]
            return carry

        lax.fori_loop(0, SIDE, centre, 0)
    for i, ref in enumerate((cb_ref, gain_ref, nbias_ref, bout_ref)):
        line = jnp.concatenate([ref[...], jnp.zeros((1, 6), F32)], axis=1)
        for g in range(GROUPS):
            lanes[g, i : i + 1, :] = line[:, g * LANES : (g + 1) * LANES]
    row = lax.broadcasted_iota(jnp.int32, (CAP, LANES), 0)
    lane = lax.broadcasted_iota(jnp.int32, (CAP, LANES), 1)
    sample = jnp.zeros((CAP, LANES), jnp.int32)
    for t in range(CAP):
        sample = jnp.where(row == t, sample_ref[t], sample)
    member[...] = (sample == lane).astype(F32)
    vec[...] = jnp.zeros_like(vec)
    passed = []

    def pass_on(p):
        out_ahead[p].wait_recv()
        passed.append(start(piece(pool, 1, p), piece(pool, 2, p), partner))

    own_conv(0, padded, conv, w, lanes)
    pass_on(0)
    own_conv(1, padded, conv, w, lanes)
    pass_on(1)
    for p, (g, half) in enumerate(PIECES):
        loads[4 + p].wait()
        to_rows(gbuf, grad, g, half)
    slot = lax.broadcasted_iota(jnp.int32, (CAP, CELLS), 0)
    ocean = jnp.where(slot < count_ref[0], ocean_ref[...].astype(F32), 0.0)
    for half in range(2):
        for t in range(CAP):
            mask[pl.ds(half * 1024 + t, LANES, stride=CAP), :] = jnp.broadcast_to(
                ocean[t : t + 1, half * LANES : (half + 1) * LANES], (LANES, LANES)
            ).T
    for i, (high, low) in enumerate(((win_hi, win_lo), (wout_hi, wout_lo))):
        loads[8 + i].wait()
        value = jnp.concatenate([weight_buf[i], jnp.zeros((1000, 6), F32)], axis=1)
        value = jnp.concatenate([value, jnp.zeros((24, 256), F32)], axis=0)
        high[...], low[...] = split(value)
    win, wout = (win_hi, win_lo), (wout_hi, wout_lo)
    scaled, update = (scaled_hi, scaled_lo), (update_hi, update_lo)
    hidden_gradient(grad, mask, wout, update_hi, update_lo, back, vec)
    ends = jnp.concatenate(
        [flat([lanes[g, 1:3, :] for g in range(GROUPS)]), jnp.zeros((14, 256), F32)], axis=0
    )
    lines = dot3(split(ends), (win_hi[...], win_lo[...]), 1, 1)
    bias_in = jnp.concatenate([bin_ref[...], jnp.zeros((1, 24), F32)], axis=1)
    lines = jnp.concatenate([lines[0:1], lines[1:2] + bias_in], axis=0)
    onehots(near_ref, me, spread)
    sums = []
    for g in range(GROUPS):
        if g == 1:
            pass_on(2)
            pass_on(3)
        for copies in (out_behind, out_partner, passed):
            arrived(copies[2 * g : 2 * g + 2])
        gather(g, near_ref, me, pool, padded)
        halo_conv(g, padded, conv, w)
        sums.append(masked_sum(g, conv, mask))

    def reduce_vector(i, vector, merge, between, later):
        partial[i] = vector
        copies = exchange_start(
            partial.at[i], send, recv, inner.at[i], used[0], me % INNER, zc_peers
        )
        used[0] += INNER - 1
        between()
        for copy in copies:
            copy.wait()
        partial[2 + i] = merge(inner[i])
        copies = exchange_start(
            partial.at[2 + i], send, recv, outer.at[i], used[0], xy, xy_peers
        )
        used[0] += OUTER - 1
        later()
        for copy in copies:
            copy.wait()
        return merge(outer[i])

    tile_mean = tile_average(sums[0][0] + sums[1][0], sums[0][1])
    stats = local_stats(tile_mean, sums[0][1], conv, mask, member[...])
    sent()
    products = [pool[c // 3].at[pl.ds(c % 3 * ROWS, ROWS), :] for c in range(6)]
    products += [extra.at[c] for c in range(2)]
    product = lambda first: centred_product(first, tile_mean, conv, lanes, win, products)
    stat = reduce_vector(0, stats, merge_stats, lambda: product(0), lambda: product(PRODUCT_ROWS))
    stat_ref[...] = stat

    mine = pl.multiple_of(core * HALF, HALF)
    theirs = pl.multiple_of((1 - core) * HALF, HALF)
    orders = [((y, y_peers, 32), (x, x_peers, INNER)), ((x, x_peers, INNER), (y, y_peers, 32))]

    def at(q, i, j, rows):
        (first, _, _), (second, _, _) = orders[q]
        i = first if i is None else i
        first_row = core * HALF + q * 128 + i * 32 + (0 if j is None else j * 8)
        return pl.ds(pl.multiple_of(first_row, 8), rows)

    def weight_sum(h):
        k = h // HIDDEN_PART
        part = pl.ds(h, HIDDEN_PART)
        halves = start(dw.at[pl.ds(theirs, HALF), part], other.at[k], partner)
        yield
        halves.wait_recv()
        dw[pl.ds(mine, HALF), part] = dw[pl.ds(mine, HALF), part] + other[k]
        yield
        copies = []
        for q, ((i, peers, stride), _) in enumerate(orders):
            for peer in peers:
                rows = at(q, (peer // stride) % 4, None, 32)
                copies.append(start(dw.at[rows, part], slots1.at[k, q, i], peer))
            slots1[k, q, i] = dw[at(q, None, None, 32), part]
        yield
        arrived(copies)
        copies = []
        for q, (_, (j, peers, stride)) in enumerate(orders):
            sum1[k, q] = jnp.sum(slots1[k, q], axis=0)
            for peer in peers:
                rows = pl.ds(pl.multiple_of(((peer // stride) % 4) * 8, 8), 8)
                copies.append(start(sum1.at[k, q, rows, :], slots2.at[k, q, j], peer))
            slots2[k, q, j] = sum1[k, q, pl.ds(pl.multiple_of(j * 8, 8), 8), :]
        yield
        arrived(copies)
        for q in range(2):
            sum2[k, q] = jnp.sum(slots2[k, q], axis=0)
        copies = [start(sum2.at[k], zslots.at[k, z], peer) for peer in z_peers]
        zslots[k, z] = sum2[k]
        yield
        arrived(copies)
        copies = []
        for q, (_, (j, peers, _)) in enumerate(orders):
            rows = at(q, None, j, 8)
            big[rows, part] = zslots[k, 0, q] + zslots[k, 1, q] + zslots[k, 2, q] + zslots[k, 3, q]
            copies += [start(big.at[rows, part], big.at[rows, part], peer) for peer in peers]
        yield
        arrived(copies)
        copies = []
        for q, ((_, peers, _), _) in enumerate(orders):
            rows = at(q, None, None, 32)
            copies += [start(big.at[rows, part], big.at[rows, part], peer) for peer in peers]
        yield
        arrived(copies)
        own = big.at[pl.ds(mine, HALF), part]
        crossed = start(own, own, partner)
        yield
        crossed.wait_recv()
        yield

    scaled_operand(stat, member[...], conv, lanes, scaled_hi, scaled_lo)

    def weights(h):
        weight_products(
            h, stat, member[...], tile_mean, lines, scaled, update, products, back, dw, hvec
        )

    def gradient(low, high, sums):
        return scaled_gradient(
            low, high, sums, stat, member[...], win, back, conv, lanes, gbuf, vec
        )

    weights(0)
    weights(WEIGHT_PART)
    early = weight_sum(0)
    next(early)
    weights(2 * WEIGHT_PART)
    next(early)
    next(early)
    weights(3 * WEIGHT_PART)
    late = weight_sum(HIDDEN_PART)
    next(late)
    zero = jnp.zeros((CAP, LANES), F32)
    sums = gradient(0, BLOCKS - 1, (zero, zero))
    next(late)
    next(late)
    next(early)
    sums = gradient(BLOCKS - 1, BLOCKS, sums)
    rows = [
        jnp.sum(member[...] * jnp.sum(value, axis=1, keepdims=True), axis=0, keepdims=True)
        for value in sums
    ]

    def before_outer():
        output_block(0, products, wout, tiles, mask, lanes)
        next(early)
        output_block(1, products, wout, tiles, mask, lanes)

    def after_outer():
        next(late)
        output_block(2, products, wout, tiles, mask, lanes)
        next(early)
        output_block(3, products, wout, tiles, mask, lanes)
        next(late)
        next(early)

    sums = reduce_vector(1, stack_rows(*rows), merge_sums, before_outer, after_outer)
    back_of = lambda g: conv_gradient(g, stat, sums, member[...], conv, gbuf, mask, lanes, db)
    back_of(0)

    payload, direct, near, merged = [], [], [], []

    def pay(p):
        g, part = PIECES[p]
        return back.at[g, pl.ds(part * HALF_RIM, HALF_RIM), :]

    def got(i, p):
        g, part = PIECES[p]
        return back.at[2 + 2 * i + g, pl.ds(part * HALF_RIM, HALF_RIM), :]

    def rims_of(p):
        g, half = PIECES[p]
        input_gradient(g, HALF_ROWS[half], gbuf, w, gpad)
        scatter(g, half, gpad, spread, pool)
        payload.append(start(piece(pool, 2, p), pay(p), partner))
        near.append(start(piece(pool, 3, p), got(2, p), partner))

    def rows_of(p, part, role=0):
        count = HALF_RIM // 2 if p == 3 else HALF_RIM
        return pl.ds(role * RIM_ROWS + PIECES[p][1] * HALF_RIM + part * count, count)

    def off_chip(p, part=0):
        g = PIECES[p][0]
        target = back.at[2 + g, rows_of(p, part), :]
        direct.append(start(pool[g].at[rows_of(p, part), :], target, ahead))

    def merge(p, part=0):
        g = PIECES[p][0]
        if part == 0:
            payload[p].wait_recv()
        rows = rows_of(p, part, 1)
        pool[g][rows, :] = pool[g][rows, :] + back[g, rows_of(p, part), :]
        merged.append(start(pool[g].at[rows, :], back.at[4 + g, rows_of(p, part), :], behind))

    rims_of(0)
    next(late)
    off_chip(0)
    rims_of(1)
    merge(0)
    next(late)
    off_chip(1)
    merge(1)
    next(early)
    own_gradient(0, gpad, grad, mask)
    back_of(1)
    rims_of(2)
    off_chip(2)
    merge(2)

    for g in range(GROUPS):
        weight_gradient(g, padded, gbuf, small)
        if g == 0:
            next(late)
        lines = [jnp.sum(db[g], axis=0, keepdims=True)]
        lines += [jnp.sum(vec[g, i], axis=0, keepdims=True) for i in range(3)]
        lines += [hvec[0:1, pl.ds((g * 4 + i) * LANES, LANES)] for i in range(4)]
        for i, line in enumerate(lines):
            small[g, pl.ds(49 + i, 1), :] = line
        small[g, pl.ds(57, 7), :] = jnp.zeros((7, LANES), F32)
    small_tile = lambda q: small.at[q // 8, pl.ds(pl.multiple_of((q % 8) * CAP, CAP), CAP), :]
    small_scattered = [start(small_tile(peer // INNER), sslots.at[xy], peer) for peer in xy_peers]
    sslots[xy] = small[xy // 8, pl.ds(pl.multiple_of((xy % 8) * CAP, CAP), CAP), :]
    rims_of(3)
    off_chip(3)
    merge(3)
    own_gradient(1, gpad, grad, mask)
    arrived(small_scattered)
    tile[...] = jnp.sum(sslots[...], axis=0)
    zc_gathered = [start(tile, zcslots.at[me % INNER], peer) for peer in zc_peers]
    zcslots[me % INNER] = tile[...]
    off_chip(3, 1)
    merge(3, 1)
    next(early)
    next(late)

    stores = store_native(xbuf, native_out, store_sem)
    for p in range(4):
        from_rows(tiles, xbuf, *PIECES[p])
        stores[p].start()
    stores.append(pltpu.make_async_copy(big, big_out, store_sem.at[4]))
    stores[4].start()
    arrived(zc_gathered)
    small_ref[xy] = jnp.sum(zcslots[...], axis=0)
    small_gathered = [start(small_ref.at[xy], small_ref.at[xy], peer) for peer in xy_peers]
    for p, (g, half) in enumerate(PIECES):
        arrived([near[p], direct[p], merged[p]])
        if p == 3:
            arrived([direct[4], merged[4]])
        for first, rim, cells in rim_spans(half):
            rows = pl.ds(first * CAP, cells * CAP)
            span = pl.ds(rim * CAP, cells * CAP)
            mine_at = pl.ds(4 * RIM_ROWS + rim * CAP, cells * CAP)
            grad[g, rows, :] = (grad[g, rows, :] + pool[g][mine_at, :]) + (
                back[6 + g, span, :] + (back[2 + g, span, :] + back[4 + g, span, :])
            )
        rows = pl.ds(half * 1024, 1024)
        stores.append(
            pltpu.make_async_copy(grad.at[g, rows, :], total_out.at[g, rows, :], store_sem.at[5 + p])
        )
        stores[-1].start()
    arrived(small_gathered)
    sent()
    for copy in stores:
        copy.wait()


def block(near, count, sample, x, g, win, wout, ocean, wt, cb, gain, nbias, bout, bin_):
    rows = (GROUPS, ROWS, LANES)
    vector = (CAP, LANES)
    weight = pltpu.VMEM((HIDDEN_PAD, 256), BF16)
    operand = pltpu.VMEM((ROWS, 256), BF16)
    copies = 16 + 2 * (INNER + OUTER - 2) + 2 * 29 + 18 + 15 + 7 + 15
    return pl.pallas_call(
        block_kernel,
        in_specs=[ANY_SPEC] * 14,
        out_specs=(ANY_SPEC,) * 3 + (VMEM_SPEC,) * 2,
        out_shape=(
            shape(2000, 256), shape(*rows), shape(512, HIDDEN_PAD), shape(16, *vector),
            shape(*vector),
        ),
        scratch_shapes=[
            pltpu.SMEM((CAP, 8), jnp.int32), pltpu.SMEM((1,), jnp.int32),
            pltpu.SMEM((CAP,), jnp.int32), pltpu.VMEM((CAP, CELLS), jnp.int32),
            buffer(KSIZE * KSIZE, 250), buffer(1, 250), buffer(1, 250), buffer(1, 250),
            buffer(1, 250), buffer(1, 1000),
            buffer(*rows), buffer(*rows), buffer(*rows), buffer(*rows),
            buffer(ROWS, LANES), buffer(ROLES * RIM_ROWS, LANES), buffer(ROLES * RIM_ROWS, LANES),
            buffer(GROUPS, PAD * PAD * CAP, LANES), buffer(*rows),
            buffer(GROUPS, KSIZE * KSIZE, CAP, LANES), buffer(GROUPS, *vector),
            buffer(*vector), buffer(2, 1000, 250), weight, weight, weight, weight,
            operand, operand, operand, operand,
            buffer(HIDDEN_CHUNKS, ROWS, LANES), buffer(2, ROWS, LANES),
            buffer(512, HIDDEN_PAD), buffer(GROUPS, 3, *vector), buffer(1, HIDDEN_PAD),
            buffer(GROUPS, *vector), buffer(PAD * PAD * CAP, LANES),
            pltpu.VMEM((8, BACK_ROLES * LANES, LANES), BF16),
            buffer(2, HALF, HIDDEN_PART), buffer(2, 2, 4, 32, HIDDEN_PART),
            buffer(2, 2, 32, HIDDEN_PART), buffer(2, 2, 4, 8, HIDDEN_PART),
            buffer(2, 2, 8, HIDDEN_PART), buffer(2, 4, 2, 8, HIDDEN_PART),
            buffer(512, HIDDEN_PAD),
            buffer(GROUPS, 64, LANES), buffer(*vector), buffer(OUTER, *vector),
            buffer(INNER, *vector), buffer(2, INNER, *vector), buffer(2, OUTER, *vector),
            buffer(4, *vector), semaphores(20), semaphores(10), semaphores(copies),
            semaphores(copies),
        ],
        compiler_params=params(collective_id=1, has_side_effects=True),
        name="block",
    )(near, count, sample, x, g, win, wout, ocean, wt, cb, gain, nbias, bout, bin_)


def final_kernel(
    total_ref, native_ref, big_ref, small_ref, stat_ref,
    out_ref, tiles_ref, dwin_ref, dwout_ref, dconv_ref, db_ref, dgain_ref, dnbias_ref, dbin_ref,
    dbout_ref, total, buf, through, big, load_sem, store_sem,
):
    loads = [
        pltpu.make_async_copy(
            total_ref.at[g, pl.ds(half * 1024, 1024), :],
            total.at[g, pl.ds(half * 1024, 1024), :],
            load_sem.at[p],
        )
        for p, (g, half) in enumerate(PIECES)
    ]
    loads.append(pltpu.make_async_copy(big_ref, big, load_sem.at[4]))
    loads.append(pltpu.make_async_copy(native_ref, through, load_sem.at[5]))
    for copy in loads:
        copy.start()
    stores = store_native(buf, tiles_ref, store_sem)
    for p, (g, half) in enumerate(PIECES):
        loads[p].wait()
        from_rows(total, buf, g, half)
        stores[p].start()
    loads[5].wait()
    stores.append(pltpu.make_async_copy(through, out_ref, store_sem.at[4]))
    stores[4].start()
    sample = lax.broadcasted_iota(jnp.int32, (1, LANES), 1) < SAMPLES
    cells = jnp.sum(jnp.where(sample, stat_ref[0:1, :], 0.0), axis=1, keepdims=True)
    share = 250.0 / cells
    loads[4].wait()
    dwin_ref[...] = big[0:256, :].T[:1000, :250] * share
    dwout_ref[...] = big[256:512, :].T[:1000, :250] * share
    parts = [
        jnp.concatenate([small_ref[g * 8 + i] for i in range(8)], axis=0) * share
        for g in range(GROUPS)
    ]
    whole = jnp.concatenate(parts, axis=1)
    dconv_ref[...] = whole[0:49, :250]
    for i, ref in enumerate((db_ref, dbout_ref, dgain_ref, dnbias_ref)):
        ref[...] = whole[49 + i : 50 + i, :250]
    line = jnp.concatenate([part[53 + i : 54 + i] for part in parts for i in range(4)], axis=1)
    dbin_ref[...] = line[:, :1000]
    for copy in stores:
        copy.wait()


def final(total, out, big, small, stat):
    return pl.pallas_call(
        final_kernel,
        in_specs=[ANY_SPEC] * 3 + [VMEM_SPEC] * 2,
        out_specs=(ANY_SPEC,) * 2 + (VMEM_SPEC,) * 8,
        out_shape=(
            shape(2000, 256), shape(2000, 256), shape(1000, 250), shape(1000, 250),
            shape(49, 250), shape(1, 250), shape(1, 250), shape(1, 250), shape(1, 1000),
            shape(1, 250),
        ),
        scratch_shapes=[
            buffer(GROUPS, ROWS, LANES), buffer(GROUPS, ROWS, LANES), buffer(2000, 256),
            buffer(512, HIDDEN_PAD), semaphores(6), semaphores(5),
        ],
        compiler_params=params(),
        name="final",
    )(total, out, big, small, stat)


def native(x):
    return jnp.transpose(x, (1, 0, 2)).reshape(2000, CELLS)


def from_native(x):
    return jnp.transpose(x.reshape(250, CAP, CELLS), (1, 0, 2))


def local(
    tiles_in, conv_weight, conv_bias, norm_gain, norm_bias, weight_in, bias_in,
    weight_out, bias_out, grad_out, tile_counts, ocean_mask, neighbours, sample_ids,
):
    out, total, big, small, stat = block(
        neighbours, tile_counts, sample_ids, native(tiles_in), native(grad_out), weight_in.T,
        weight_out, ocean_mask, conv_weight.T, conv_bias[None], norm_gain[None], norm_bias[None],
        bias_out[None], bias_in[None],
    )
    output, grad_tiles, dwin, dwout, dconv, db, dgain, dnbias, dbin, dbout = final(
        total, out, big, small, stat
    )
    return (
        from_native(output), from_native(grad_tiles), dconv.T, db[0], dgain[0], dnbias[0],
        dwin.T, dbin[0], dwout, dbout[0],
    )


def solution(mesh):
    tiles = P("tiles")
    whole = P()
    return jax.shard_map(
        local,
        mesh=mesh,
        in_specs=(tiles,) + (whole,) * 8 + (tiles,) * 5,
        out_specs=(tiles, tiles) + (whole,) * 8,
        check_vma=False,
    )
```
